256 devices in a mesh: tile: 64 (over y, z, core), head: 4 (over x).
Axes of the slice: x: 4, y: 4, z: 8, core: 2. Of those that a mesh axis runs over, the one named last changes fastest.
Arguments:
- obs_feat: bfloat16 [524288, 512], P('tile', 'head'), may hold values from -70 to 70, as said below
- row_valid: int32 [524288], P('tile'), may hold values 0 or 1
- block_owner: int32 [4096, 1], P('tile'), may hold values from 0 to 63; in each aligned block of 64 rows (0 to 63, 64 to 127, ...) at most 2 rows name the same one
- block_pattern: int32 [4096, 16], P('tile'), may hold values 0 or 1
- latent: bfloat16 [32768, 512], P('tile'), may hold values from -35 to 35, as said below
- w_query: bfloat16 [512, 512], P(None, 'head'), may hold values from -0.25 to 0.25
- w_key: bfloat16 [512, 512], P(None, 'head'), may hold values from -0.25 to 0.25
- w_value: bfloat16 [512, 512], P(None, 'head'), may hold values from -0.25 to 0.25
- self_bias: float32 [8], P('head'), may hold values from 2.5 to 4.5
- w_out: bfloat16 [512, 512], P('head'), may hold values from -0.25 to 0.25
- norm_gain: float32 [512], replicated, may hold values from 0.25 to 1.75
- w_inc: bfloat16 [512, 128], replicated, may hold values from -0.25 to 0.25
- target: bfloat16 [32768, 128], P('tile'), may hold values from -6 to 6
Outputs:
- increment: float32 [32768, 128], P('tile')
- head_gradient: float32 [512, 128], P('head')
The draws below stay inside these ranges and needn't reach their ends.
Inputs may be any that keep to these rules, and one draw needn't show every extreme that they name: `obs_feat`: embedded features; rows may differ widely in scale. `latent`: latent state; rows may differ widely in scale. `block_owner`: among the 64 blocks of one shard, no tile is named by more than 2 blocks, a bound that some block reaches.
All inputs are finite; a program needn't handle non-finite values. No bound on the sum of `row_valid` or of `block_pattern` on one device may be relied on, other than what follows from the above.
Results may differ from the reference program's by a relative error of at most 0.0093.
Values may be sent and summed in bfloat16 or wider, within the bound.
No kernel may reach another device: no remote copies, remote signals or barrier semaphores. Data moves between devices by JAX's collectives and lax.ppermute only.
A program may use at most 128 MiB of HBM per device.

```python
import math
import jax
import jax.numpy as jnp
import numpy as np
from jax import lax

D = 512
HEADS = 8
OUT = 128
BLK = 128
LSUB = 16
NB_DEV = 64
LAT_DEV = 512
HD = 64
CAP = 2
MEASURED_COUNT = 524288
NBLK = 4096
HIDDEN_SITE_COUNT = 32768
SUB_LAT = 32
N_TILE = 64


def draw_obs_feat(key, part):
    key = jax.random.fold_in(key, 11)
    first = jax.random.fold_in(key, 0)
    payload_entries = jax.random.truncated_normal(first, -4.0, 4.0, (MEASURED_COUNT, D), jnp.float32)
    return payload_entries.astype(jnp.bfloat16)


def draw_latent(key, part):
    key = jax.random.fold_in(key, 23)
    first = jax.random.fold_in(key, 0)
    payload_entries = 0.5 * jax.random.truncated_normal(first, -4.0, 4.0, (HIDDEN_SITE_COUNT, D), jnp.float32)
    return payload_entries.astype(jnp.bfloat16)


def with_ends(values, stream_key, least, high):
    longest = values.shape.index(max(values.shape))
    spots = []
    for shift in (0, 1):
        where = [jax.random.randint(jax.random.fold_in(stream_key, axis), (), 0, length) for axis, length in enumerate(values.shape)]
        where[longest] = (where[longest] + shift) % values.shape[longest]
        spots.append(tuple(where))
    return values.at[spots[0]].set(least).at[spots[1]].set(high)


def block_scale(rng, shape, cuts, least, high):
    loudness, own = 1.0, jax.random.fold_in(rng, 6)
    for position, shards_of in cuts:
        steps = jnp.exp(jax.random.uniform(jax.random.fold_in(own, position), (shards_of,), jnp.float32, least / len(cuts), high / len(cuts)))
        loudness = loudness * jnp.repeat(steps, shape[position] // shards_of).reshape([-1 if axis == position else 1 for axis in range(len(shape))])
    return loudness


def deal_out(stream_key, own, number, rows, count, top, reach, slope):
    ranking = jax.random.permutation(stream_key, count)
    crowded, common = load_shares(count, rows * top, reach, slope, True), load_shares(count, rows * top, reach, slope, False)
    places = jnp.arange(count)

    def named(tallies, turn):
        used = int((tallies > 0).sum())
        fixed = max(1, used // 4)
        shifted = fixed + (places - fixed + turn * (used - fixed)) % max(1, count - fixed)
        return jnp.zeros((count,), jnp.int32).at[ranking[jnp.where(places < fixed, places, shifted)]].set(jnp.asarray(tallies, jnp.int32))

    tallies = jnp.where(number % 4 == 0, named(crowded, number // 4), named(common, number - number // 4 - 1))
    mixed = jax.random.permutation(jax.random.fold_in(own, 3), count)
    giver, taker = mixed[0:count // 2 * 2:2], mixed[1:count // 2 * 2:2]
    margin = jnp.minimum(tallies[giver] - 1, reach - tallies[taker]) // 2
    margin = jnp.where((giver == ranking[0]) | (taker == ranking[0]) | (tallies[taker] == 0), 0, jnp.maximum(margin, 0))
    shifted = jax.random.randint(jax.random.fold_in(own, 4), (count // 2,), 0, 1 << 20) % (margin + 1)
    tallies = tallies.at[giver].add(-shifted).at[taker].add(shifted)
    labels = jnp.searchsorted(jnp.cumsum(tallies), jnp.arange(rows * top), side="right").astype(jnp.int32)
    listing = labels.reshape(top, rows).T
    listing = listing[jax.random.permutation(jax.random.fold_in(own, 1), rows)]
    turn = jax.random.randint(jax.random.fold_in(own, 2), (rows, 1), 0, top)
    return jnp.take_along_axis(listing, (jnp.arange(top)[None, :] + turn) % top, axis=1)


def load_shares(amount, total, reach, skew, full):
    portions = [(1 << 20) // math.isqrt(rank ** skew) + 1 for rank in range(1, amount + 1)]
    largest = reach if full else min(reach, max(-(-total // amount), total * portions[0] // sum(portions)))
    least = 1 if total - largest >= amount - 1 else 0
    holding, rest = [largest] + [least] * (amount - 1), total - largest - least * (amount - 1)
    while rest > 0:
        candidates = [i for i in range(1, amount) if holding[i] < largest] or [i for i in range(1, amount) if holding[i] < reach]
        mass, remaining = sum([portions[i] for i in candidates]), rest
        for i in candidates:
            extra = min(reach - holding[i], max(1, remaining * portions[i] // mass), rest)
            holding[i] = holding[i] + extra
            rest = rest - extra
    return np.array(holding)


def normal_values(key, dims, deviation, most, cuts=(), kind=jnp.bfloat16):
    loudness = block_scale(key, dims, cuts, -0.22, 0.18) if cuts else 1.0
    result = jax.random.normal(key, dims, jnp.float32) * deviation * loudness
    return jnp.minimum(jnp.maximum(result, -most), most).astype(kind)


def setup_inputs(seed: int = 0) -> dict:
    keys = jax.random.split(jax.random.key(seed), 14)
    obs_feat = draw_obs_feat(jax.random.fold_in(keys[13], 71), 0)
    row_valid = with_ends((jax.random.randint(keys[1], (MEASURED_COUNT,), 0, 8) < 7).astype(jnp.int32), jax.random.fold_in(keys[1], 1), 0, 1)
    block_owner_keys = jax.random.split(jax.random.fold_in(keys[2], 1), NBLK // NB_DEV)
    block_owner_turns = jax.random.permutation(jax.random.fold_in(keys[2], 3), NBLK // NB_DEV)
    block_owner = jax.vmap(lambda own, number: deal_out(jax.random.fold_in(keys[2], 2), own, number, NB_DEV, N_TILE, 1, CAP, 2))(block_owner_keys, block_owner_turns).reshape((NBLK, 1))
    block_pattern = with_ends((jax.random.randint(keys[3], (NBLK, LSUB), 0, 32) < 1).astype(jnp.int32), jax.random.fold_in(keys[3], 1), 0, 1)
    latent = draw_latent(jax.random.fold_in(keys[13], 71), 0)
    w_query = normal_values(keys[5], (D, D), D ** -0.5, 0.25, ((1, 4),))
    w_key = normal_values(keys[6], (D, D), D ** -0.5, 0.25, ((1, 4),))
    w_value = normal_values(keys[7], (D, D), D ** -0.5, 0.25, ((1, 4),))
    self_bias = jnp.clip(2.5 + 2.0 * jax.random.uniform(keys[8], (HEADS,), jnp.float32) ** block_scale(keys[8], (HEADS,), ((0, 4),), -0.2, 0.2), 2.5, 4.5)
    w_out = normal_values(keys[9], (D, D), D ** -0.5, 0.25, ((0, 4),))
    norm_gain = jnp.clip(1.0 + 0.15 * jax.random.normal(keys[10], (D,), jnp.float32), 0.25, 1.75)
    w_inc = normal_values(keys[11], (D, OUT), D ** -0.5, 0.25)
    target = normal_values(keys[12], (HIDDEN_SITE_COUNT, OUT), 1.0, 6.0, ((0, 64),))
    return {"obs_feat": obs_feat, "row_valid": row_valid, "block_owner": block_owner, "block_pattern": block_pattern, "latent": latent, "w_query": w_query, "w_key": w_key, "w_value": w_value, "self_bias": self_bias, "w_out": w_out, "norm_gain": norm_gain, "w_inc": w_inc, "target": target}


def rounded(payload_entries):
    return lax.optimization_barrier(payload_entries.astype(jnp.bfloat16)).astype(jnp.float32)

def reference(obs_feat, row_valid, block_owner, block_pattern, latent, w_query, w_key, w_value, self_bias, w_out, norm_gain, w_inc, target):
    score_scale = 1.0 / math.sqrt(HD)
    all_keys = jnp.dot(obs_feat, w_key, preferred_element_type=jnp.float32).astype(jnp.bfloat16).reshape(NBLK, BLK, HEADS, HD)
    all_values = jnp.dot(obs_feat, w_value, preferred_element_type=jnp.float32).astype(jnp.bfloat16).reshape(NBLK, BLK, HEADS, HD)
    destinations = block_owner[:, 0].reshape(N_TILE, NB_DEV)
    onehot = (destinations[:, :, None] == jnp.arange(N_TILE, dtype=jnp.int32)[None, None, :]).astype(jnp.int32)
    slot_rank = lax.optimization_barrier(jnp.sum((jnp.cumsum(onehot, axis=1) - onehot) * onehot, axis=2))
    row_mask = (row_valid.reshape(NBLK, BLK, 1) * block_pattern.reshape(NBLK, 1, LSUB)).astype(jnp.float32)
    member = (jnp.arange(LAT_DEV, dtype=jnp.int32)[:, None] // SUB_LAT == jnp.arange(LSUB, dtype=jnp.int32)[None, :]).astype(jnp.float32)

    def owner_step(tile_pos):
        matches = (destinations[:, :, None] == tile_pos) & (slot_rank[:, :, None] == jnp.arange(CAP, dtype=jnp.int32)[None, None, :])
        local_block = lax.optimization_barrier(jnp.sum(jnp.where(matches, jnp.arange(NB_DEV, dtype=jnp.int32)[None, :, None], 0), axis=1))
        filled = jnp.any(matches, axis=1).astype(jnp.float32).reshape(-1)
        block_ids = (jnp.arange(N_TILE, dtype=jnp.int32)[:, None] * NB_DEV + local_block).reshape(-1).astype(jnp.int32)
        gathered_keys = all_keys[block_ids].reshape(-1, HEADS, HD).astype(jnp.float32)
        gathered_values = all_values[block_ids].reshape(-1, HEADS, HD).astype(jnp.float32)
        slot_mask = (row_mask[block_ids] * filled[:, None, None]).reshape(-1, LSUB)
        allowed = jnp.dot(member, slot_mask.T, precision=lax.Precision.HIGHEST) > 0.5
        latent_rows = lax.dynamic_slice_in_dim(latent, (tile_pos * LAT_DEV).astype(jnp.int32), LAT_DEV, 0)
        queries = rounded(jnp.dot(latent_rows, w_query, preferred_element_type=jnp.float32)).reshape(LAT_DEV, HEADS, HD)
        own_key = rounded(jnp.dot(latent_rows, w_key, preferred_element_type=jnp.float32)).reshape(LAT_DEV, HEADS, HD)
        own_value = rounded(jnp.dot(latent_rows, w_value, preferred_element_type=jnp.float32)).reshape(LAT_DEV, HEADS, HD)
        own_score = lax.optimization_barrier(jnp.sum(queries * own_key, axis=-1)).T * score_scale + self_bias[:, None]
        scores = jnp.einsum('lhd,khd->hlk', queries, gathered_keys) * score_scale
        scores = jnp.where(allowed[None], scores, jnp.float32(-1e+30))
        row_max = jnp.maximum(own_score, lax.optimization_barrier(jnp.max(scores, axis=-1)))
        weights = jnp.exp(scores - row_max[..., None])
        own_weight = jnp.exp(own_score - row_max)
        denominator = own_weight + lax.optimization_barrier(jnp.sum(weights, axis=-1))
        numerator = jnp.einsum('hlk,khd->hld', rounded(weights), gathered_values)
        numerator = numerator + rounded(own_weight)[..., None] * own_value.transpose(1, 0, 2)
        mixed = numerator / denominator[..., None]
        return mixed.transpose(1, 0, 2).reshape(LAT_DEV, D).astype(jnp.bfloat16)
    attended = lax.map(owner_step, jnp.arange(N_TILE, dtype=jnp.int32)).reshape(HIDDEN_SITE_COUNT, D)
    updated = latent.astype(jnp.float32) + jnp.dot(attended, w_out, preferred_element_type=jnp.float32)
    normed = (updated * lax.rsqrt(lax.optimization_barrier(jnp.mean(updated * updated, axis=-1, keepdims=True)) + 1e-06) * norm_gain).astype(jnp.bfloat16)
    predicted = jnp.dot(normed, w_inc, preferred_element_type=jnp.float32)
    residual = predicted - target.astype(jnp.float32)
    gradient_result = jnp.dot(normed.astype(jnp.float32).T, residual, precision=lax.Precision.HIGHEST) / math.sqrt(HIDDEN_SITE_COUNT)
    return (predicted, gradient_result)
```

```python
import math

import jax
import jax.numpy as jnp
from jax import lax
from jax.experimental import pallas as pl
from jax.experimental.pallas import tpu as pltpu
from jax.sharding import PartitionSpec as P

BF = jnp.bfloat16
F32 = jnp.float32
NEG = -1e30
SLOTS = 2
CHUNK = 4


def route_kernel(owner, obs, info, payload, marks, counts, sem):
    tiles = payload.shape[0]
    blocks = obs.shape[0]
    marks[...] = jnp.zeros_like(marks)

    def clear(t, carry):
        counts[t] = 0
        return carry

    lax.fori_loop(0, tiles, clear, 0)

    def send(b, carry):
        t = owner[b]
        k = jnp.minimum(counts[t], SLOTS - 1)
        counts[t] = k + 1
        pltpu.make_async_copy(obs.at[b], payload.at[t, :, k], sem).start()
        marks[t * SLOTS + k] = info[b]
        return carry

    lax.fori_loop(0, blocks, send, 0)
    pltpu.make_async_copy(obs, obs, sem).wait()


def split3(v):
    hi = v.astype(BF).astype(F32)
    mid = (v - hi).astype(BF).astype(F32)
    return hi, mid, v - hi - mid


def attend_kernel(counts, lists, first, x, bias, qw, own, lat, wv, out, xbuf, acc, top, den):
    g = pl.program_id(0)
    heads, sub, width = qw.shape
    rows = heads * sub
    quarter = x.shape[3]
    parts = x.shape[1]
    cols = x.shape[4]
    n = counts[g]
    keep = first[0].astype(F32)
    queries = qw[...].reshape(rows, width)
    top[...] = own[...].reshape(rows, 128)
    den[...] = jnp.full((rows, 128), keep, F32)
    latent = lat[...].astype(F32) * keep
    acc[...] = jnp.broadcast_to(latent[None], (heads, sub, width)).reshape(rows, width)
    lane_slot = lax.broadcasted_iota(jnp.int32, (1, CHUNK * quarter), 1) // quarter

    def step(c, carry):
        shade = jnp.full((1, CHUNK * quarter), NEG, F32)
        for u in range(CHUNK):
            place = c * CHUNK + u
            slot = lists[g, jnp.minimum(place, n - 1)]
            s, k = slot // SLOTS, slot % SLOTS
            for i in range(parts):
                xbuf[u * quarter:(u + 1) * quarter, i * cols:(i + 1) * cols] = x[s, i, k]
            live = (lane_slot == u) & (place < n)
            shade = jnp.where(live, bias[pl.ds(slot, 1), :], shade)
        rows_x = xbuf[...]
        scores = lax.dot_general(
            queries, rows_x, (((1,), (1,)), ((), ())), preferred_element_type=F32
        ) + shade
        old = top[...]
        new = jnp.maximum(old, jnp.max(scores, axis=1, keepdims=True))
        weights = jnp.exp(scores - new)
        shrink = jnp.exp(old - new)
        top[...] = new
        den[...] = den[...] * shrink + jnp.sum(weights, axis=1, keepdims=True)
        more = jnp.dot(weights.astype(BF), rows_x, preferred_element_type=F32)
        acc[...] = acc[...] * jnp.concatenate([shrink] * (width // 128), axis=1) + more
        return carry

    lax.fori_loop(0, (n + CHUNK - 1) // CHUNK, step, 0)
    mixed = jnp.dot(acc[...].astype(BF), wv[...], preferred_element_type=F32)
    mixed = mixed.reshape(heads, sub, width)
    head_of = lax.broadcasted_iota(jnp.int32, (sub, width), 1) // (width // heads)
    lane = lax.broadcasted_iota(jnp.int32, (sub, 128), 1)
    top3 = split3(top[...].reshape(heads, sub, 128))
    den3 = split3(den[...].reshape(heads, sub, 128))
    numer = jnp.zeros((sub, width), F32)
    stats = jnp.zeros((sub, 128), F32)
    for h in range(heads):
        numer = jnp.where(head_of == h, mixed[h], numer)
        for q, part in enumerate(top3 + den3):
            stats = jnp.where(lane == q * heads + h, part[h], stats)
    out[:, :width] = numer.astype(BF)
    out[:, width:] = stats.astype(BF)


def finish_kernel(place, r0, r1, r2, r3, lat, w_out, gain, w_inc, target, out):
    width = lat.shape[1]
    heads = 8
    tops, dens, nums = [], [], []
    line = lax.broadcasted_iota(jnp.int32, (128, 2 * width), 0)
    col = lax.broadcasted_iota(jnp.int32, (128, 2 * width), 1)
    kind = line // heads
    match = (line % heads == (col % width) // (width // heads)) & (
        kind // 3 == col // width
    ) & (kind < 6)
    spread = match.astype(F32).astype(BF)
    for r in (r0, r1, r2, r3):
        wide = jnp.dot(r[:, width:], spread, preferred_element_type=F32)
        tops.append(wide[:, :width])
        dens.append(wide[:, width:])
        nums.append(r[:, :width].astype(F32))
    best = jnp.maximum(jnp.maximum(tops[0], tops[1]), jnp.maximum(tops[2], tops[3]))
    scale = [jnp.exp(v - best) for v in tops]
    numer = sum(a * b for a, b in zip(scale, nums))
    denom = sum(a * b for a, b in zip(scale, dens))
    attended = (numer / denom).astype(BF)
    updated = lat[...].astype(F32) + jnp.dot(attended, w_out[...], preferred_element_type=F32)
    power = jnp.mean(updated * updated, axis=1, keepdims=True)
    normed = (updated * lax.rsqrt(power + 1e-6) * gain[...]).astype(BF)
    predicted = jnp.dot(normed, w_inc[...], preferred_element_type=F32)
    residual = predicted - target[...].astype(F32)
    high = residual.astype(BF)
    low = (residual - high.astype(F32)).astype(BF)
    dims = (((0,), (0,)), ((), ()))
    grad = lax.dot_general(normed, high, dims, preferred_element_type=F32)
    grad = grad + lax.dot_general(normed, low, dims, preferred_element_type=F32)
    rows = predicted.shape[0]
    for d in range(4):
        out[d, :128, :] = grad[d * 128:(d + 1) * 128]
        out[d, 128:128 + rows, :] = predicted


def body(
    obs_feat,
    row_valid,
    block_owner,
    block_pattern,
    latent,
    w_query,
    w_key,
    w_value,
    self_bias,
    w_out,
    norm_gain,
    w_inc,
    target,
):
    tiles = lax.axis_size("tile")
    groups = lax.axis_size("head")
    me = lax.axis_index("head")
    blocks = block_owner.shape[0]
    block_rows = obs_feat.shape[0] // blocks
    quarter = block_rows // groups
    cols = obs_feat.shape[1]
    lat_rows, width = latent.shape
    subs = block_pattern.shape[1]
    sub = lat_rows // subs
    local_heads = self_bias.shape[0]
    heads = local_heads * groups
    head_size = width // heads
    slots = tiles * SLOTS
    share = lat_rows // groups

    def swap(v, axis, mask, size):
        return lax.ppermute(v, axis, [(d, d ^ mask) for d in range(size)])

    def pick(v, which):
        return lax.dynamic_index_in_dim(v, which, 0, keepdims=False)

    valid = lax.dynamic_index_in_dim(
        row_valid.reshape(blocks, groups, quarter), me, 1, keepdims=False
    )
    info = jnp.stack(
        [
            jnp.tile(valid, (1, 128 // quarter)),
            jnp.pad(block_pattern, ((0, 0), (0, 128 - subs))),
        ],
        axis=1,
    ).astype(F32)
    payload, marks = pl.pallas_call(
        route_kernel,
        grid_spec=pltpu.PrefetchScalarGridSpec(
            num_scalar_prefetch=1,
            grid=(1,),
            in_specs=[
                pl.BlockSpec(memory_space=pl.ANY),
                pl.BlockSpec((blocks, 2, 128), lambda i, o: (0, 0, 0)),
            ],
            out_specs=[
                pl.BlockSpec(memory_space=pl.ANY),
                pl.BlockSpec((slots, 2, 128), lambda i, o: (0, 0, 0)),
            ],
            scratch_shapes=[pltpu.SMEM((tiles,), jnp.int32), pltpu.SemaphoreType.DMA],
        ),
        out_shape=[
            jax.ShapeDtypeStruct((tiles, groups, SLOTS, quarter, cols), BF),
            jax.ShapeDtypeStruct((slots, 2, 128), F32),
        ],
        name="route",
    )(block_owner[:, 0], obs_feat.reshape(blocks, groups, quarter, cols), info)

    marks = lax.all_to_all(marks, "tile", split_axis=0, concat_axis=0, tiled=True)
    arrived = lax.all_to_all(
        payload.reshape(tiles * groups, SLOTS, quarter, cols),
        ("tile", "head"),
        split_axis=0,
        concat_axis=0,
        tiled=True,
    ).reshape(tiles, groups, SLOTS, quarter, cols)

    bias = (marks[:, 0, :] - 1.0) * (-NEG)
    live = (marks[:, 1, :subs] > 0.5).T
    before = jnp.triu(jnp.ones((slots, slots), BF), 1)
    place = jnp.dot(live.astype(BF), before, preferred_element_type=F32).astype(jnp.int32)
    counts = jnp.sum(live.astype(jnp.int32), axis=1)
    order = jnp.arange(slots, dtype=jnp.int32)
    hit = live[:, None, :] & (place[:, None, :] == order[None, :, None])
    lists = jnp.sum(jnp.where(hit, order[None, None, :], 0), axis=2)

    stacked = lax.all_gather(
        jnp.concatenate([w_query, w_key, w_value, w_out.T], axis=1), "head", axis=0
    )
    wq, wk, wv, wo = [
        stacked[:, :, a * 128:(a + 1) * 128].transpose(1, 0, 2).reshape(width, width)
        for a in range(4)
    ]
    wo = wo.T
    by_distance = jnp.stack(
        [self_bias] + [swap(self_bias, "head", d, groups) for d in range(1, groups)]
    )
    turn = jnp.arange(groups, dtype=jnp.int32) ^ me
    bias_all = jnp.take(by_distance, turn, axis=0).reshape(heads)
    queries = jnp.dot(latent, wq, preferred_element_type=F32).astype(BF)
    own_key = jnp.dot(latent, wk, preferred_element_type=F32).astype(BF)
    q3 = queries.reshape(lat_rows, heads, head_size)
    k3 = wk.reshape(width, heads, head_size)
    scale = 1.0 / math.sqrt(head_size)
    qw = (
        jnp.einsum("lhd,khd->hlk", q3, k3, preferred_element_type=F32) * scale
    ).astype(BF)
    own = (
        jnp.sum(
            q3.astype(F32) * own_key.reshape(lat_rows, heads, head_size).astype(F32), axis=-1
        ).T
        * scale
        + bias_all[:, None]
    )
    own = jnp.broadcast_to(own[:, :, None], (heads, lat_rows, 128))

    whole = lambda *shape: pl.BlockSpec(shape, lambda g, *_: (0,) * len(shape))
    partial = pl.pallas_call(
        attend_kernel,
        grid_spec=pltpu.PrefetchScalarGridSpec(
            num_scalar_prefetch=3,
            grid=(subs,),
            in_specs=[
                whole(tiles, groups, SLOTS, quarter, cols),
                whole(slots, 128),
                pl.BlockSpec((heads, sub, width), lambda g, *_: (0, g, 0)),
                pl.BlockSpec((heads, sub, 128), lambda g, *_: (0, g, 0)),
                pl.BlockSpec((sub, width), lambda g, *_: (g, 0)),
                whole(width, width),
            ],
            out_specs=pl.BlockSpec((sub, width + 128), lambda g, *_: (g, 0)),
            scratch_shapes=[
                pltpu.VMEM((CHUNK * quarter, width), BF),
                pltpu.VMEM((heads * sub, width), F32),
                pltpu.VMEM((heads * sub, 128), F32),
                pltpu.VMEM((heads * sub, 128), F32),
            ],
        ),
        out_shape=jax.ShapeDtypeStruct((lat_rows, width + 128), BF),
        compiler_params=pltpu.CompilerParams(vmem_limit_bytes=40 * 1024 * 1024),
        name="attend",
    )(counts, lists, (me == 0).astype(jnp.int32)[None], arrived, bias, qw, own, latent, wv)

    partial = partial.reshape(groups, share, width + 128)
    received = [pick(partial, me)] + [
        swap(pick(partial, me ^ d), "head", d, groups) for d in range(1, groups)
    ]
    row = lambda *shape: pl.BlockSpec(shape, lambda i, m: (m[0], 0))
    full = lambda *shape: pl.BlockSpec(shape, lambda i, m: (0,) * len(shape))
    packed = pl.pallas_call(
        finish_kernel,
        grid_spec=pltpu.PrefetchScalarGridSpec(
            num_scalar_prefetch=1,
            grid=(1,),
            in_specs=[full(share, width + 128)] * 4
            + [
                row(share, width),
                full(width, width),
                full(1, width),
                full(width, 128),
                row(share, 128),
            ],
            out_specs=full(groups, 128 + share, 128),
        ),
        out_shape=jax.ShapeDtypeStruct((groups, 128 + share, 128), F32),
        compiler_params=pltpu.CompilerParams(vmem_limit_bytes=32 * 1024 * 1024),
        name="finish",
    )(
        me[None].astype(jnp.int32),
        *received,
        latent,
        wo,
        norm_gain[None, :],
        w_inc,
        target,
    )
    pieces = [pick(packed, me)] + [
        swap(pick(packed, me ^ d), "head", d, groups) for d in range(1, groups)
    ]
    grads = [p[:128] for p in pieces]
    grad = (grads[0] + grads[1]) + (grads[2] + grads[3])
    stacked_pred = jnp.stack([p[128:] for p in pieces])
    predicted = jnp.take(
        stacked_pred, jnp.arange(groups, dtype=jnp.int32) ^ me, axis=0
    ).reshape(lat_rows, 128)
    for mask in (1, 2, 4, 8, 16, 32):
        grad = grad + swap(grad, "tile", mask, tiles)
    return predicted, grad * (1.0 / math.sqrt(lat_rows * tiles))


def solution(mesh):
    in_specs = (
        P("tile", "head"),
        P("tile"),
        P("tile", None),
        P("tile", None),
        P("tile", None),
        P(None, "head"),
        P(None, "head"),
        P(None, "head"),
        P("head"),
        P("head", None),
        P(),
        P(),
        P("tile", None),
    )
    out_specs = (P("tile", None), P("head", None))
    return jax.shard_map(body, mesh=mesh, in_specs=in_specs, out_specs=out_specs, check_vma=False)
```

```python
import math

import jax
import jax.numpy as jnp
from jax import lax
from jax.experimental import pallas as pl
from jax.experimental.pallas import tpu as pltpu
from jax.sharding import PartitionSpec as P

BF = jnp.bfloat16
F32 = jnp.float32
NEG = -1e30
SLOTS = 2
CHUNK = 4


def route_kernel(owner, obs, payload, counts):
    tiles = payload.shape[0]
    blocks = obs.shape[0]

    def clear(t, carry):
        counts[t] = 0
        return carry

    lax.fori_loop(0, tiles, clear, 0)

    def send(b, carry):
        t = owner[b]
        k = jnp.minimum(counts[t], SLOTS - 1)
        counts[t] = k + 1
        payload[t, :, k] = obs[b]
        return carry

    lax.fori_loop(0, blocks, send, 0)


def split3(v):
    hi = v.astype(BF).astype(F32)
    mid = (v - hi).astype(BF).astype(F32)
    return hi, mid, v - hi - mid


def attend_kernel(counts, lists, first, x, bias, qw, own, lat, wv, out, xbuf, acc, top, den):
    g = pl.program_id(0)
    heads, sub, width = qw.shape
    rows = heads * sub
    quarter = x.shape[3]
    parts = x.shape[1]
    cols = x.shape[4]
    n = counts[g]
    keep = first[0].astype(F32)
    queries = qw[...].reshape(rows, width)
    top[...] = own[...].reshape(rows, 128)
    den[...] = jnp.full((rows, 128), keep, F32)
    latent = lat[...].astype(F32) * keep
    acc[...] = jnp.broadcast_to(latent[None], (heads, sub, width)).reshape(rows, width)
    lane_slot = lax.broadcasted_iota(jnp.int32, (1, CHUNK * quarter), 1) // quarter

    def step(c, carry):
        shade = jnp.full((1, CHUNK * quarter), NEG, F32)
        for u in range(CHUNK):
            place = c * CHUNK + u
            item = lists[g, jnp.minimum(place, n - 1)]
            slot, mark = item // (SLOTS * x.shape[0]), item % (SLOTS * x.shape[0])
            s, k = slot // SLOTS, slot % SLOTS
            for i in range(parts):
                xbuf[u * quarter:(u + 1) * quarter, i * cols:(i + 1) * cols] = x[s, i, k]
            live = (lane_slot == u) & (place < n)
            shade = jnp.where(live, bias[pl.ds(mark, 1), :], shade)
        rows_x = xbuf[...]
        scores = lax.dot_general(
            queries, rows_x, (((1,), (1,)), ((), ())), preferred_element_type=F32
        ) + shade
        old = top[...]
        new = jnp.maximum(old, jnp.max(scores, axis=1, keepdims=True))
        weights = jnp.exp(scores - new)
        shrink = jnp.exp(old - new)
        top[...] = new
        den[...] = den[...] * shrink + jnp.sum(weights, axis=1, keepdims=True)
        more = jnp.dot(weights.astype(BF), rows_x, preferred_element_type=F32)
        acc[...] = acc[...] * jnp.concatenate([shrink] * (width // 128), axis=1) + more
        return carry

    lax.fori_loop(0, (n + CHUNK - 1) // CHUNK, step, 0)
    mixed = jnp.dot(acc[...].astype(BF), wv[...], preferred_element_type=F32)
    mixed = mixed.reshape(heads, sub, width)
    head_of = lax.broadcasted_iota(jnp.int32, (sub, width), 1) // (width // heads)
    lane = lax.broadcasted_iota(jnp.int32, (sub, 128), 1)
    top3 = split3(top[...].reshape(heads, sub, 128))
    den3 = split3(den[...].reshape(heads, sub, 128))
    numer = jnp.zeros((sub, width), F32)
    stats = jnp.zeros((sub, 128), F32)
    for h in range(heads):
        numer = jnp.where(head_of == h, mixed[h], numer)
        for q, part in enumerate(top3 + den3):
            stats = jnp.where(lane == q * heads + h, part[h], stats)
    out[:, :width] = numer.astype(BF)
    out[:, width:] = stats.astype(BF)


def finish_kernel(place, r0, r1, r2, r3, lat, w_out, gain, w_inc, target, out):
    width = lat.shape[1]
    heads = 8
    tops, dens, nums = [], [], []
    line = lax.broadcasted_iota(jnp.int32, (128, 2 * width), 0)
    col = lax.broadcasted_iota(jnp.int32, (128, 2 * width), 1)
    kind = line // heads
    match = (line % heads == (col % width) // (width // heads)) & (
        kind // 3 == col // width
    ) & (kind < 6)
    spread = match.astype(F32).astype(BF)
    for r in (r0, r1, r2, r3):
        wide = jnp.dot(r[:, width:], spread, preferred_element_type=F32)
        tops.append(wide[:, :width])
        dens.append(wide[:, width:])
        nums.append(r[:, :width].astype(F32))
    best = jnp.maximum(jnp.maximum(tops[0], tops[1]), jnp.maximum(tops[2], tops[3]))
    scale = [jnp.exp(v - best) for v in tops]
    numer = sum(a * b for a, b in zip(scale, nums))
    denom = sum(a * b for a, b in zip(scale, dens))
    attended = (numer / denom).astype(BF)
    updated = lat[...].astype(F32) + jnp.dot(attended, w_out[...], preferred_element_type=F32)
    power = jnp.mean(updated * updated, axis=1, keepdims=True)
    normed = (updated * lax.rsqrt(power + 1e-6) * gain[...]).astype(BF)
    predicted = jnp.dot(normed, w_inc[...], preferred_element_type=F32)
    residual = predicted - target[...].astype(F32)
    high = residual.astype(BF)
    low = (residual - high.astype(F32)).astype(BF)
    dims = (((0,), (0,)), ((), ()))
    grad = lax.dot_general(normed, high, dims, preferred_element_type=F32)
    grad = grad + lax.dot_general(normed, low, dims, preferred_element_type=F32)
    rows = predicted.shape[0]
    for d in range(4):
        out[d, :128, :] = grad[d * 128:(d + 1) * 128]
        out[d, 128:128 + rows, :] = predicted


def body(
    obs_feat,
    row_valid,
    block_owner,
    block_pattern,
    latent,
    w_query,
    w_key,
    w_value,
    self_bias,
    w_out,
    norm_gain,
    w_inc,
    target,
):
    tiles = lax.axis_size("tile")
    groups = lax.axis_size("head")
    me = lax.axis_index("head")
    blocks = block_owner.shape[0]
    block_rows = obs_feat.shape[0] // blocks
    quarter = block_rows // groups
    cols = obs_feat.shape[1]
    lat_rows, width = latent.shape
    subs = block_pattern.shape[1]
    sub = lat_rows // subs
    local_heads = self_bias.shape[0]
    heads = local_heads * groups
    head_size = width // heads
    slots = tiles * SLOTS
    share = lat_rows // groups

    def swap(v, axis, mask, size):
        return lax.ppermute(v, axis, [(d, d ^ mask) for d in range(size)])

    def pick(v, which):
        return lax.dynamic_index_in_dim(v, which, 0, keepdims=False)

    tile = lax.axis_index("tile")
    whole = lambda *shape: pl.BlockSpec(shape, lambda g, *_: (0,) * len(shape))
    payload = pl.pallas_call(
        route_kernel,
        grid_spec=pltpu.PrefetchScalarGridSpec(
            num_scalar_prefetch=1,
            grid=(1,),
            in_specs=[whole(blocks, groups, quarter, cols)],
            out_specs=whole(tiles, groups, SLOTS, quarter, cols),
            scratch_shapes=[pltpu.SMEM((tiles,), jnp.int32)],
        ),
        out_shape=jax.ShapeDtypeStruct((tiles, groups, SLOTS, quarter, cols), BF),
        compiler_params=pltpu.CompilerParams(vmem_limit_bytes=32 * 1024 * 1024),
        name="route",
    )(block_owner[:, 0], obs_feat.reshape(blocks, groups, quarter, cols))
    arrived = lax.all_to_all(
        payload.reshape(tiles * groups, SLOTS, quarter, cols),
        ("tile", "head"),
        split_axis=0,
        concat_axis=0,
        tiled=True,
    ).reshape(tiles, groups, SLOTS, quarter, cols)

    valid = pick(row_valid.reshape(blocks, groups, quarter).transpose(1, 0, 2), me)
    marks = jnp.concatenate([valid, block_pattern, block_owner], axis=1).astype(BF)
    marks = jnp.pad(marks, ((0, 0), (0, 64 - marks.shape[1])))[None]
    source = jnp.zeros((1,), jnp.int32) + tile
    for mask in (8, 4, 2, 32, 16, 1):
        marks = jnp.concatenate([marks, swap(marks, "tile", mask, tiles)], axis=0)
        source = jnp.concatenate([source, source ^ mask])
    mine = marks[:, :, quarter + subs] == tile.astype(BF)
    earlier = jnp.triu(jnp.ones((blocks, blocks), BF), 1)
    rank = jnp.einsum("eb,bc->ec", mine.astype(BF), earlier, preferred_element_type=F32)
    chosen = mine[:, None, :] & (
        rank[:, None, :] == jnp.arange(SLOTS, dtype=F32)[None, :, None]
    )
    marks = jnp.einsum(
        "ekb,ebc->ekc", chosen.astype(BF), marks, preferred_element_type=F32
    ).reshape(slots, 64)

    bias = jnp.tile((marks[:, :quarter] - 1.0) * (-NEG), (1, 128 // quarter))
    live = (marks[:, quarter:quarter + subs] > 0.5).T
    before = jnp.triu(jnp.ones((slots, slots), BF), 1)
    place = jnp.dot(live.astype(BF), before, preferred_element_type=F32).astype(jnp.int32)
    counts = jnp.sum(live.astype(jnp.int32), axis=1)
    order = jnp.arange(slots, dtype=jnp.int32)
    entry = (source[:, None] * SLOTS + jnp.arange(SLOTS, dtype=jnp.int32)).reshape(slots)
    hit = live[:, None, :] & (place[:, None, :] == order[None, :, None])
    lists = jnp.sum(
        jnp.where(hit, (entry * slots + order)[None, None, :], 0), axis=2
    )

    stacked = lax.all_gather(
        jnp.concatenate([w_query, w_key, w_value, w_out.T], axis=1), "head", axis=0
    )
    wq, wk, wv, wo = [
        stacked[:, :, a * 128:(a + 1) * 128].transpose(1, 0, 2).reshape(width, width)
        for a in range(4)
    ]
    wo = wo.T
    by_distance = jnp.stack(
        [self_bias] + [swap(self_bias, "head", d, groups) for d in range(1, groups)]
    )
    turn = jnp.arange(groups, dtype=jnp.int32) ^ me
    bias_all = jnp.take(by_distance, turn, axis=0).reshape(heads)
    queries = jnp.dot(latent, wq, preferred_element_type=F32).astype(BF)
    own_key = jnp.dot(latent, wk, preferred_element_type=F32).astype(BF)
    q3 = queries.reshape(lat_rows, heads, head_size)
    k3 = wk.reshape(width, heads, head_size)
    scale = 1.0 / math.sqrt(head_size)
    qw = (
        jnp.einsum("lhd,khd->hlk", q3, k3, preferred_element_type=F32) * scale
    ).astype(BF)
    own = (
        jnp.sum(
            q3.astype(F32) * own_key.reshape(lat_rows, heads, head_size).astype(F32), axis=-1
        ).T
        * scale
        + bias_all[:, None]
    )
    own = jnp.broadcast_to(own[:, :, None], (heads, lat_rows, 128))

    partial = pl.pallas_call(
        attend_kernel,
        grid_spec=pltpu.PrefetchScalarGridSpec(
            num_scalar_prefetch=3,
            grid=(subs,),
            in_specs=[
                whole(tiles, groups, SLOTS, quarter, cols),
                whole(slots, 128),
                pl.BlockSpec((heads, sub, width), lambda g, *_: (0, g, 0)),
                pl.BlockSpec((heads, sub, 128), lambda g, *_: (0, g, 0)),
                pl.BlockSpec((sub, width), lambda g, *_: (g, 0)),
                whole(width, width),
            ],
            out_specs=pl.BlockSpec((sub, width + 128), lambda g, *_: (g, 0)),
            scratch_shapes=[
                pltpu.VMEM((CHUNK * quarter, width), BF),
                pltpu.VMEM((heads * sub, width), F32),
                pltpu.VMEM((heads * sub, 128), F32),
                pltpu.VMEM((heads * sub, 128), F32),
            ],
        ),
        out_shape=jax.ShapeDtypeStruct((lat_rows, width + 128), BF),
        compiler_params=pltpu.CompilerParams(vmem_limit_bytes=40 * 1024 * 1024),
        name="attend",
    )(counts, lists, (me == 0).astype(jnp.int32)[None], arrived, bias, qw, own, latent, wv)

    partial = partial.reshape(groups, share, width + 128)
    received = [pick(partial, me)] + [
        swap(pick(partial, me ^ d), "head", d, groups) for d in range(1, groups)
    ]
    row = lambda *shape: pl.BlockSpec(shape, lambda i, m: (m[0], 0))
    full = lambda *shape: pl.BlockSpec(shape, lambda i, m: (0,) * len(shape))
    packed = pl.pallas_call(
        finish_kernel,
        grid_spec=pltpu.PrefetchScalarGridSpec(
            num_scalar_prefetch=1,
            grid=(1,),
            in_specs=[full(share, width + 128)] * 4
            + [
                row(share, width),
                full(width, width),
                full(1, width),
                full(width, 128),
                row(share, 128),
            ],
            out_specs=full(groups, 128 + share, 128),
        ),
        out_shape=jax.ShapeDtypeStruct((groups, 128 + share, 128), F32),
        compiler_params=pltpu.CompilerParams(vmem_limit_bytes=32 * 1024 * 1024),
        name="finish",
    )(
        me[None].astype(jnp.int32),
        *received,
        latent,
        wo,
        norm_gain[None, :],
        w_inc,
        target,
    )
    grads = [pick(packed, me)[:128]] + [
        swap(pick(packed, me ^ d)[:128], "head", d, groups) for d in range(1, groups)
    ]
    grad = (grads[0] + grads[1]) + (grads[2] + grads[3])
    for low, high in ((1, 2), (4, 8), (16, 32)):
        a, b, c = (swap(grad, "tile", m, tiles) for m in (low, high, low + high))
        grad = (grad + a) + (b + c)
    mine = packed[0, 128:]
    preds = jnp.stack([mine] + [swap(mine, "head", d, groups) for d in range(1, groups)])
    predicted = jnp.take(preds, turn, axis=0).reshape(lat_rows, 128)
    return predicted, grad * (1.0 / math.sqrt(lat_rows * tiles))


def solution(mesh):
    in_specs = (
        P("tile", "head"),
        P("tile"),
        P("tile", None),
        P("tile", None),
        P("tile", None),
        P(None, "head"),
        P(None, "head"),
        P(None, "head"),
        P("head"),
        P("head", None),
        P(),
        P(),
        P("tile", None),
    )
    out_specs = (P("tile", None), P("head", None))
    return jax.shard_map(body, mesh=mesh, in_specs=in_specs, out_specs=out_specs, check_vma=False)
```

```python
import functools
import math

import jax
import jax.numpy as jnp
from jax import lax
from jax.experimental import pallas as pl
from jax.experimental.pallas import tpu as pltpu
from jax.sharding import PartitionSpec as P

BF = jnp.bfloat16
F32 = jnp.float32
NEG = -1e30
SLOTS = 2
CHUNK = 4


def route_kernel(owner, alive, obs, row_marks, pattern, first, second, marks, slots, info):
    tiles = first.shape[0]
    blocks, parts, quarter = obs.shape[:3]
    lane = lax.broadcasted_iota(jnp.int32, (blocks, 128), 1)
    rows = row_marks[...].astype(F32)
    spot = lax.broadcasted_iota(jnp.int32, (pattern.shape[1], 128), 1)
    line = lax.broadcasted_iota(jnp.int32, (pattern.shape[1], 128), 0)
    shift = (spot == line + quarter).astype(F32).astype(BF)
    groups = jnp.dot(pattern[...].astype(F32).astype(BF), shift, preferred_element_type=F32)
    for j in range(parts):
        turned = rows if j == 0 else pltpu.roll(rows, 128 - j * quarter, 1)
        info[j, :blocks] = jnp.where(lane < quarter, turned, groups)
        info[j, blocks:] = jnp.zeros((8, 128), F32)

    def clear(t, carry):
        marks[t] = 0
        slots[t] = blocks
        slots[tiles + t] = blocks
        return carry

    lax.fori_loop(0, tiles, clear, 0)

    def place(b, carry):
        t = owner[b]

        @pl.when(alive[b] > 0)
        def _():
            k = jnp.minimum(marks[t], SLOTS - 1)
            marks[t] = k + 1
            slots[k * tiles + t] = b

        return carry

    lax.fori_loop(0, blocks, place, 0)
    line8 = lax.broadcasted_iota(jnp.int32, (8, 128), 0)

    def fill(t, carry):
        b0 = slots[t]
        b1 = slots[tiles + t]
        for j in range(parts):
            one = info[j, pl.ds(b0, 1), :]
            two = info[j, pl.ds(b1, 1), :]
            pair = jnp.where(line8 == 0, one, jnp.where(line8 == 1, two, 0.0))
            first[t, j, quarter:quarter + 8, :] = pair.astype(BF)

        @pl.when(b0 < blocks)
        def _():
            first[t, :, :quarter, :] = obs[b0]

        @pl.when(b1 < blocks)
        def _():
            second[t] = obs[b1]

        return carry

    lax.fori_loop(0, tiles, fill, 0)


def lists_kernel(arrived, lists, bias):
    tiles = arrived.shape[0]
    quarter = arrived.shape[2] - 8
    subs = lists.shape[1]
    found = arrived[:, 0, quarter:quarter + 8, :].astype(F32)
    ahead = (
        lax.broadcasted_iota(jnp.int32, (tiles, tiles), 0)
        < lax.broadcasted_iota(jnp.int32, (tiles, tiles), 1)
    ).astype(F32).astype(BF)
    pick_group = (
        lax.broadcasted_iota(jnp.int32, (subs, 128), 1)
        == lax.broadcasted_iota(jnp.int32, (subs, 128), 0) + quarter
    ).astype(F32).astype(BF)
    up = lax.broadcasted_iota(jnp.int32, (128, 128), 0)
    along = lax.broadcasted_iota(jnp.int32, (128, 128), 1)
    widen = ((up < quarter) & (up == along % quarter)).astype(F32).astype(BF)
    turn = lax.broadcasted_iota(jnp.int32, (subs, 128, tiles), 1).astype(F32)
    name = lax.broadcasted_iota(jnp.int32, (subs, 128, tiles), 2).astype(F32)
    last = lax.broadcasted_iota(jnp.int32, (subs, 128), 1) == 127
    for k in range(SLOTS):
        mine = found[:, k, :].astype(BF)
        live = lax.dot_general(
            pick_group, mine, (((1,), (1,)), ((), ())), preferred_element_type=F32
        )
        place = jnp.dot(live.astype(BF), ahead, preferred_element_type=F32)
        hit = (place[:, None, :] == turn) & (live[:, None, :] > 0.5)
        order = jnp.sum(jnp.where(hit, name, 0.0), axis=2)
        count = jnp.sum(live, axis=1, keepdims=True)
        lists[k] = jnp.where(last, count, order).astype(jnp.int32)
        rows = jnp.dot(mine, widen, preferred_element_type=F32)
        bias[k] = (rows - 1.0) * (-NEG)


def split3(v):
    hi = v.astype(BF).astype(F32)
    mid = (v - hi).astype(BF).astype(F32)
    return hi, mid, v - hi - mid


def attend_kernel(final, lists, x, bias, qw, begun, given, wv, *rest):
    if final:
        out, xbuf, acc, top, den = rest
    else:
        out, states, xbuf, acc, top, den = rest
    g = pl.program_id(0)
    heads, sub, width = qw.shape
    rows = heads * sub
    quarter = 32
    parts = x.shape[1]
    cols = x.shape[3]
    n = lists[g, 127]
    lane = lax.broadcasted_iota(jnp.int32, (sub, 128), 1)
    start = begun[...]
    tops = [jnp.broadcast_to(start[:, h:h + 1], (sub, 128)) for h in range(heads)]
    dens = [
        jnp.broadcast_to(start[:, heads + h:heads + h + 1], (sub, 128)) for h in range(heads)
    ]

    def store(numer, tops, dens):
        stats = jnp.zeros((sub, 128), F32)
        if final:
            for h in range(heads):
                for q, part in enumerate(split3(tops[h]) + split3(dens[h])):
                    stats = jnp.where(lane == q * heads + h, part, stats)
            out[:, :width] = numer.astype(BF)
            out[:, width:] = stats.astype(BF)
        else:
            for h in range(heads):
                stats = jnp.where(lane == h, tops[h], stats)
                stats = jnp.where(lane == heads + h, dens[h], stats)
            out[...] = numer
            states[...] = stats

    @pl.when(n == 0)
    def _():
        store(given[...], tops, dens)

    @pl.when(n > 0)
    def _():
        queries = qw[...].reshape(rows, width)
        for h in range(heads):
            top[h * sub:(h + 1) * sub, :] = tops[h]
            den[h * sub:(h + 1) * sub, :] = dens[h]
        acc[...] = jnp.zeros_like(acc)
        lane_slot = lax.broadcasted_iota(jnp.int32, (1, CHUNK * quarter), 1) // quarter

        def step(c, carry):
            shade = jnp.full((1, CHUNK * quarter), NEG, F32)
            for u in range(CHUNK):
                place = c * CHUNK + u
                s = lists[g, jnp.minimum(place, n - 1)]
                for i in range(parts):
                    xbuf[u * quarter:(u + 1) * quarter, i * cols:(i + 1) * cols] = x[
                        s, i, :quarter, :
                    ]
                live = (lane_slot == u) & (place < n)
                shade = jnp.where(live, bias[pl.ds(s, 1), :], shade)
            rows_x = xbuf[...]
            scores = lax.dot_general(
                queries, rows_x, (((1,), (1,)), ((), ())), preferred_element_type=F32
            ) + shade
            old = top[...]
            new = jnp.maximum(old, jnp.max(scores, axis=1, keepdims=True))
            weights = jnp.exp(scores - new)
            shrink = jnp.exp(old - new)
            top[...] = new
            den[...] = den[...] * shrink + jnp.sum(weights, axis=1, keepdims=True)
            more = jnp.dot(weights.astype(BF), rows_x, preferred_element_type=F32)
            acc[...] = acc[...] * jnp.concatenate([shrink] * (width // 128), axis=1) + more
            return carry

        lax.fori_loop(0, (n + CHUNK - 1) // CHUNK, step, 0)
        mixed = jnp.dot(acc[...].astype(BF), wv[...], preferred_element_type=F32)
        mixed = mixed.reshape(heads, sub, width)
        head_of = lax.broadcasted_iota(jnp.int32, (sub, width), 1) // (width // heads)
        before = given[...]
        numer = jnp.zeros((sub, width), F32)
        ends = [top[h * sub:(h + 1) * sub, :] for h in range(heads)]
        sums = [den[h * sub:(h + 1) * sub, :] for h in range(heads)]
        for h in range(heads):
            shrink = jnp.concatenate([jnp.exp(tops[h] - ends[h])] * (width // 128), axis=1)
            numer = jnp.where(head_of == h, before * shrink + mixed[h], numer)
        store(numer, ends, sums)


def finish_kernel(place, r0, r1, r2, r3, lat, w_out, gain, w_inc, target, out):
    width = lat.shape[1]
    heads = 8
    tops, dens, nums = [], [], []
    line = lax.broadcasted_iota(jnp.int32, (128, 2 * width), 0)
    col = lax.broadcasted_iota(jnp.int32, (128, 2 * width), 1)
    kind = line // heads
    match = (line % heads == (col % width) // (width // heads)) & (
        kind // 3 == col // width
    ) & (kind < 6)
    spread = match.astype(F32).astype(BF)
    for r in (r0, r1, r2, r3):
        wide = jnp.dot(r[:, width:], spread, preferred_element_type=F32)
        tops.append(wide[:, :width])
        dens.append(wide[:, width:])
        nums.append(r[:, :width].astype(F32))
    best = jnp.maximum(jnp.maximum(tops[0], tops[1]), jnp.maximum(tops[2], tops[3]))
    scale = [jnp.exp(v - best) for v in tops]
    numer = sum(a * b for a, b in zip(scale, nums))
    denom = sum(a * b for a, b in zip(scale, dens))
    attended = (numer / denom).astype(BF)
    updated = lat[...].astype(F32) + jnp.dot(attended, w_out[...], preferred_element_type=F32)
    power = jnp.mean(updated * updated, axis=1, keepdims=True)
    normed = (updated * lax.rsqrt(power + 1e-6) * gain[...]).astype(BF)
    predicted = jnp.dot(normed, w_inc[...], preferred_element_type=F32)
    residual = predicted - target[...].astype(F32)
    high = residual.astype(BF)
    low = (residual - high.astype(F32)).astype(BF)
    dims = (((0,), (0,)), ((), ()))
    grad = lax.dot_general(normed, high, dims, preferred_element_type=F32)
    grad = grad + lax.dot_general(normed, low, dims, preferred_element_type=F32)
    rows = predicted.shape[0]
    for d in range(4):
        out[d, :128, :] = grad[d * 128:(d + 1) * 128]
        out[d, 128:128 + rows, :] = predicted


def body(
    obs_feat,
    row_valid,
    block_owner,
    block_pattern,
    latent,
    w_query,
    w_key,
    w_value,
    self_bias,
    w_out,
    norm_gain,
    w_inc,
    target,
):
    tiles = lax.axis_size("tile")
    groups = lax.axis_size("head")
    me = lax.axis_index("head")
    blocks = block_owner.shape[0]
    block_rows = obs_feat.shape[0] // blocks
    quarter = block_rows // groups
    cols = obs_feat.shape[1]
    lat_rows, width = latent.shape
    subs = block_pattern.shape[1]
    sub = lat_rows // subs
    local_heads = self_bias.shape[0]
    heads = local_heads * groups
    head_size = width // heads
    share = lat_rows // groups

    def swap(v, axis, mask, size):
        return lax.ppermute(v, axis, [(d, d ^ mask) for d in range(size)])

    def pick(v, which):
        return lax.dynamic_index_in_dim(v, which, 0, keepdims=False)

    tile = lax.axis_index("tile")
    whole = lambda *shape: pl.BlockSpec(shape, lambda g, *_: (0,) * len(shape))
    depth = quarter + 8
    first, second = pl.pallas_call(
        route_kernel,
        grid_spec=pltpu.PrefetchScalarGridSpec(
            num_scalar_prefetch=2,
            grid=(1,),
            in_specs=[
                whole(blocks, groups, quarter, cols),
                whole(blocks, block_rows),
                whole(blocks, subs),
            ],
            out_specs=[
                whole(tiles, groups, depth, cols),
                whole(tiles, groups, quarter, cols),
            ],
            scratch_shapes=[
                pltpu.SMEM((tiles,), jnp.int32),
                pltpu.SMEM((SLOTS * tiles,), jnp.int32),
                pltpu.VMEM((groups, blocks + 8, 128), F32),
            ],
        ),
        out_shape=[
            jax.ShapeDtypeStruct((tiles, groups, depth, cols), BF),
            jax.ShapeDtypeStruct((tiles, groups, quarter, cols), BF),
        ],
        compiler_params=pltpu.CompilerParams(vmem_limit_bytes=32 * 1024 * 1024),
        name="route",
    )(
        block_owner[:, 0],
        jnp.max(block_pattern, axis=1),
        obs_feat.reshape(blocks, groups, quarter, cols),
        row_valid.reshape(blocks, block_rows),
        block_pattern,
    )

    def exchange(v):
        flat = v.reshape((tiles * groups,) + v.shape[2:])
        flat = lax.all_to_all(flat, ("tile", "head"), split_axis=0, concat_axis=0, tiled=True)
        return flat.reshape(v.shape)

    first = exchange(first)
    second = exchange(second)

    lists, bias = pl.pallas_call(
        lists_kernel,
        grid=(1,),
        in_specs=[pl.BlockSpec((tiles, 1, depth, cols), lambda g: (0, 0, 0, 0))],
        out_specs=[whole(SLOTS, subs, 128), whole(SLOTS, tiles, 128)],
        out_shape=[
            jax.ShapeDtypeStruct((SLOTS, subs, 128), jnp.int32),
            jax.ShapeDtypeStruct((SLOTS, tiles, 128), F32),
        ],
        name="lists",
    )(first)

    stacked = lax.all_gather(
        jnp.concatenate([w_query, w_key, w_value, w_out.T], axis=1), "head", axis=0
    )
    wq, wk, wv, wo = [
        stacked[:, :, a * 128:(a + 1) * 128].transpose(1, 0, 2).reshape(width, width)
        for a in range(4)
    ]
    wo = wo.T
    by_distance = jnp.stack(
        [self_bias] + [swap(self_bias, "head", d, groups) for d in range(1, groups)]
    )
    turn = jnp.arange(groups, dtype=jnp.int32) ^ me
    bias_all = jnp.take(by_distance, turn, axis=0).reshape(heads)
    queries = jnp.dot(latent, wq, preferred_element_type=F32).astype(BF)
    own_key = jnp.dot(latent, wk, preferred_element_type=F32).astype(BF)
    q3 = queries.reshape(lat_rows, heads, head_size)
    k3 = wk.reshape(width, heads, head_size)
    scale = 1.0 / math.sqrt(head_size)
    qw = (
        jnp.einsum("lhd,khd->hlk", q3, k3, preferred_element_type=F32) * scale
    ).astype(BF)
    own = (
        jnp.sum(
            q3.astype(F32) * own_key.reshape(lat_rows, heads, head_size).astype(F32), axis=-1
        )
        * scale
        + bias_all[None, :]
    )
    keep = (me == 0).astype(F32)
    states = jnp.pad(
        jnp.concatenate([own, jnp.full((lat_rows, heads), keep)], axis=1),
        ((0, 0), (0, 128 - 2 * heads)),
    )
    numer = jnp.dot(latent, wv, preferred_element_type=F32) * keep

    def attend(k, x, numer, states, final):
        if final:
            out_specs = pl.BlockSpec((sub, width + 128), lambda g, *_: (g, 0))
            out_shape = jax.ShapeDtypeStruct((lat_rows, width + 128), BF)
        else:
            out_specs = [
                pl.BlockSpec((sub, width), lambda g, *_: (g, 0)),
                pl.BlockSpec((sub, 128), lambda g, *_: (g, 0)),
            ]
            out_shape = [
                jax.ShapeDtypeStruct((lat_rows, width), F32),
                jax.ShapeDtypeStruct((lat_rows, 128), F32),
            ]
        return pl.pallas_call(
            functools.partial(attend_kernel, final),
            grid_spec=pltpu.PrefetchScalarGridSpec(
                num_scalar_prefetch=1,
                grid=(subs,),
                in_specs=[
                    whole(*x.shape),
                    whole(tiles, 128),
                    pl.BlockSpec((heads, sub, width), lambda g, *_: (0, g, 0)),
                    pl.BlockSpec((sub, 128), lambda g, *_: (g, 0)),
                    pl.BlockSpec((sub, width), lambda g, *_: (g, 0)),
                    whole(width, width),
                ],
                out_specs=out_specs,
                scratch_shapes=[
                    pltpu.VMEM((CHUNK * quarter, width), BF),
                    pltpu.VMEM((heads * sub, width), F32),
                    pltpu.VMEM((heads * sub, 128), F32),
                    pltpu.VMEM((heads * sub, 128), F32),
                ],
            ),
            out_shape=out_shape,
            compiler_params=pltpu.CompilerParams(vmem_limit_bytes=40 * 1024 * 1024),
            name="attend",
        )(lists[k], x, bias[k], qw, states, numer, wv)

    numer, states = attend(0, first, numer, states, False)
    partial = attend(1, second, numer, states, True)

    partial = partial.reshape(groups, share, width + 128)
    received = [pick(partial, me)] + [
        swap(pick(partial, me ^ d), "head", d, groups) for d in range(1, groups)
    ]
    row = lambda *shape: pl.BlockSpec(shape, lambda i, m: (m[0], 0))
    full = lambda *shape: pl.BlockSpec(shape, lambda i, m: (0,) * len(shape))
    packed = pl.pallas_call(
        finish_kernel,
        grid_spec=pltpu.PrefetchScalarGridSpec(
            num_scalar_prefetch=1,
            grid=(1,),
            in_specs=[full(share, width + 128)] * 4
            + [
                row(share, width),
                full(width, width),
                full(1, width),
                full(width, 128),
                row(share, 128),
            ],
            out_specs=full(groups, 128 + share, 128),
        ),
        out_shape=jax.ShapeDtypeStruct((groups, 128 + share, 128), F32),
        compiler_params=pltpu.CompilerParams(vmem_limit_bytes=32 * 1024 * 1024),
        name="finish",
    )(
        me[None].astype(jnp.int32),
        *received,
        latent,
        wo,
        norm_gain[None, :],
        w_inc,
        target,
    )
    grads = [pick(packed, me)[:128]] + [
        swap(pick(packed, me ^ d)[:128], "head", d, groups) for d in range(1, groups)
    ]
    grad = (grads[0] + grads[1]) + (grads[2] + grads[3])
    for low, high in ((1, 2), (4, 8), (16, 32)):
        a, b, c = (swap(grad, "tile", m, tiles) for m in (low, high, low + high))
        grad = (grad + a) + (b + c)
    mine = packed[0, 128:]
    preds = jnp.stack([mine] + [swap(mine, "head", d, groups) for d in range(1, groups)])
    predicted = jnp.take(preds, turn, axis=0).reshape(lat_rows, 128)
    return predicted, grad * (1.0 / math.sqrt(lat_rows * tiles))


def solution(mesh):
    in_specs = (
        P("tile", "head"),
        P("tile"),
        P("tile", None),
        P("tile", None),
        P("tile", None),
        P(None, "head"),
        P(None, "head"),
        P(None, "head"),
        P("head"),
        P("head", None),
        P(),
        P(),
        P("tile", None),
    )
    out_specs = (P("tile", None), P("head", None))
    return jax.shard_map(body, mesh=mesh, in_specs=in_specs, out_specs=out_specs, check_vma=False)
```

```python
import functools
import math

import jax
import jax.numpy as jnp
from jax import lax
from jax.experimental import pallas as pl
from jax.experimental.pallas import tpu as pltpu
from jax.sharding import PartitionSpec as P

BF = jnp.bfloat16
F32 = jnp.float32
NEG = -1e30
SLOTS = 2
CHUNK = 4
MARK_ROWS = 2


def marks_kernel(owner, alive, row_marks, pattern, marks, slots, info, taken):
    tiles = marks.shape[0]
    blocks = row_marks.shape[0]
    quarter = 32
    j = owner[blocks]
    turned = pltpu.roll(row_marks[...].astype(F32), (128 - j * quarter) % 128, 1)
    lane = lax.broadcasted_iota(jnp.int32, (blocks, 128), 1)
    spot = lax.broadcasted_iota(jnp.int32, (pattern.shape[1], 128), 1)
    line = lax.broadcasted_iota(jnp.int32, (pattern.shape[1], 128), 0)
    shift = (spot == line + quarter).astype(F32).astype(BF)
    groups = jnp.dot(pattern[...].astype(F32).astype(BF), shift, preferred_element_type=F32)
    info[...] = jnp.where(lane < quarter, turned, groups)
    marks[...] = jnp.zeros_like(marks)

    def clear(t, carry):
        taken[t] = 0
        slots[t] = blocks
        slots[tiles + t] = blocks
        return carry

    lax.fori_loop(0, tiles, clear, 0)

    def place(b, carry):
        t = owner[b]

        @pl.when(alive[b] > 0)
        def _():
            k = jnp.minimum(taken[t], SLOTS - 1)
            taken[t] = k + 1
            slots[k * tiles + t] = b
            marks[t, pl.ds(k, 1), :] = info[pl.ds(b, 1), :]

        return carry

    lax.fori_loop(0, blocks, place, 0)


def pack_kernel(slots, obs, payload):
    tiles = payload.shape[0]
    blocks = obs.shape[0]

    def fill(t, carry):
        for k in range(SLOTS):
            b = slots[k * tiles + t]

            @pl.when(b < blocks)
            def _():
                payload[t, :, k] = obs[b]

        return carry

    lax.fori_loop(0, tiles, fill, 0)


def lists_kernel(found, lists, bias):
    tiles = found.shape[0]
    slots = SLOTS * tiles
    quarter = 32
    subs = lists.shape[0]
    mine = jnp.concatenate([found[:, k, :] for k in range(SLOTS)], axis=0).astype(BF)
    ahead = (
        lax.broadcasted_iota(jnp.int32, (slots, slots), 0)
        < lax.broadcasted_iota(jnp.int32, (slots, slots), 1)
    ).astype(F32).astype(BF)
    pick_group = (
        lax.broadcasted_iota(jnp.int32, (subs, 128), 1)
        == lax.broadcasted_iota(jnp.int32, (subs, 128), 0) + quarter
    ).astype(F32).astype(BF)
    up = lax.broadcasted_iota(jnp.int32, (128, 128), 0)
    along = lax.broadcasted_iota(jnp.int32, (128, 128), 1)
    widen = ((up < quarter) & (up == along % quarter)).astype(F32).astype(BF)
    live = lax.dot_general(
        pick_group, mine, (((1,), (1,)), ((), ())), preferred_element_type=F32
    )
    place = jnp.dot(live.astype(BF), ahead, preferred_element_type=F32)
    turn = lax.broadcasted_iota(jnp.int32, (subs, slots, slots), 1).astype(F32)
    name = lax.broadcasted_iota(jnp.int32, (subs, slots, slots), 2).astype(F32)
    hit = (place[:, None, :] == turn) & (live[:, None, :] > 0.5)
    order = jnp.sum(jnp.where(hit, name, 0.0), axis=2)
    count = jnp.sum(live, axis=1, keepdims=True)
    lists[:, :128] = order.astype(jnp.int32)
    lists[:, 128:] = jnp.broadcast_to(count, (subs, 128)).astype(jnp.int32)
    rows = jnp.dot(mine, widen, preferred_element_type=F32)
    bias[...] = (rows - 1.0) * (-NEG)


def split3(v):
    hi = v.astype(BF).astype(F32)
    mid = (v - hi).astype(BF).astype(F32)
    return hi, mid, v - hi - mid


def attend_kernel(final, lists, x, bias, qw, begun, given, wv, *rest):
    if final:
        out, xbuf, acc, top, den = rest
    else:
        out, states, xbuf, acc, top, den = rest
    g = pl.program_id(0)
    heads, sub, width = qw.shape
    rows = heads * sub
    quarter = 32
    parts = x.shape[1]
    cols = x.shape[4]
    n = lists[g, 128]
    tiles = x.shape[0]
    lane = lax.broadcasted_iota(jnp.int32, (sub, 128), 1)
    start = begun[...]
    tops = [jnp.broadcast_to(start[:, h:h + 1], (sub, 128)) for h in range(heads)]
    dens = [
        jnp.broadcast_to(start[:, heads + h:heads + h + 1], (sub, 128)) for h in range(heads)
    ]

    def store(numer, tops, dens):
        stats = jnp.zeros((sub, 128), F32)
        if final:
            for h in range(heads):
                for q, part in enumerate(split3(tops[h]) + split3(dens[h])):
                    stats = jnp.where(lane == q * heads + h, part, stats)
            out[:, :width] = numer.astype(BF)
            out[:, width:] = stats.astype(BF)
        else:
            for h in range(heads):
                stats = jnp.where(lane == h, tops[h], stats)
                stats = jnp.where(lane == heads + h, dens[h], stats)
            out[...] = numer
            states[...] = stats

    @pl.when(n == 0)
    def _():
        store(given[...], tops, dens)

    @pl.when(n > 0)
    def _():
        queries = qw[...].reshape(rows, width)
        for h in range(heads):
            top[h * sub:(h + 1) * sub, :] = tops[h]
            den[h * sub:(h + 1) * sub, :] = dens[h]
        acc[...] = jnp.zeros_like(acc)
        lane_slot = lax.broadcasted_iota(jnp.int32, (1, CHUNK * quarter), 1) // quarter

        def step(c, carry):
            shade = jnp.full((1, CHUNK * quarter), NEG, F32)
            for u in range(CHUNK):
                place = c * CHUNK + u
                s = lists[g, jnp.minimum(place, n - 1)]
                for i in range(parts):
                    xbuf[u * quarter:(u + 1) * quarter, i * cols:(i + 1) * cols] = x[
                        s % tiles, i, s // tiles
                    ]
                live = (lane_slot == u) & (place < n)
                shade = jnp.where(live, bias[pl.ds(s, 1), :], shade)
            rows_x = xbuf[...]
            scores = lax.dot_general(
                queries, rows_x, (((1,), (1,)), ((), ())), preferred_element_type=F32
            ) + shade
            old = top[...]
            new = jnp.maximum(old, jnp.max(scores, axis=1, keepdims=True))
            weights = jnp.exp(scores - new)
            shrink = jnp.exp(old - new)
            top[...] = new
            den[...] = den[...] * shrink + jnp.sum(weights, axis=1, keepdims=True)
            more = jnp.dot(weights.astype(BF), rows_x, preferred_element_type=F32)
            acc[...] = acc[...] * jnp.concatenate([shrink] * (width // 128), axis=1) + more
            return carry

        lax.fori_loop(0, (n + CHUNK - 1) // CHUNK, step, 0)
        mixed = jnp.dot(acc[...].astype(BF), wv[...], preferred_element_type=F32)
        mixed = mixed.reshape(heads, sub, width)
        head_of = lax.broadcasted_iota(jnp.int32, (sub, width), 1) // (width // heads)
        before = given[...]
        numer = jnp.zeros((sub, width), F32)
        ends = [top[h * sub:(h + 1) * sub, :] for h in range(heads)]
        sums = [den[h * sub:(h + 1) * sub, :] for h in range(heads)]
        for h in range(heads):
            shrink = jnp.concatenate([jnp.exp(tops[h] - ends[h])] * (width // 128), axis=1)
            numer = jnp.where(head_of == h, before * shrink + mixed[h], numer)
        store(numer, ends, sums)


def finish_kernel(place, r0, r1, r2, r3, lat, w_out, gain, w_inc, target, out):
    width = lat.shape[1]
    heads = 8
    tops, dens, nums = [], [], []
    line = lax.broadcasted_iota(jnp.int32, (128, 2 * width), 0)
    col = lax.broadcasted_iota(jnp.int32, (128, 2 * width), 1)
    kind = line // heads
    match = (line % heads == (col % width) // (width // heads)) & (
        kind // 3 == col // width
    ) & (kind < 6)
    spread = match.astype(F32).astype(BF)
    for r in (r0, r1, r2, r3):
        wide = jnp.dot(r[:, width:], spread, preferred_element_type=F32)
        tops.append(wide[:, :width])
        dens.append(wide[:, width:])
        nums.append(r[:, :width].astype(F32))
    best = jnp.maximum(jnp.maximum(tops[0], tops[1]), jnp.maximum(tops[2], tops[3]))
    scale = [jnp.exp(v - best) for v in tops]
    numer = sum(a * b for a, b in zip(scale, nums))
    denom = sum(a * b for a, b in zip(scale, dens))
    attended = (numer / denom).astype(BF)
    updated = lat[...].astype(F32) + jnp.dot(attended, w_out[...], preferred_element_type=F32)
    power = jnp.mean(updated * updated, axis=1, keepdims=True)
    normed = (updated * lax.rsqrt(power + 1e-6) * gain[...]).astype(BF)
    predicted = jnp.dot(normed, w_inc[...], preferred_element_type=F32)
    residual = predicted - target[...].astype(F32)
    high = residual.astype(BF)
    low = (residual - high.astype(F32)).astype(BF)
    dims = (((0,), (0,)), ((), ()))
    grad = lax.dot_general(normed, high, dims, preferred_element_type=F32)
    grad = grad + lax.dot_general(normed, low, dims, preferred_element_type=F32)
    rows = predicted.shape[0]
    for d in range(4):
        out[d, :128, :] = grad[d * 128:(d + 1) * 128]
        out[d, 128:128 + rows, :] = predicted


def body(
    obs_feat,
    row_valid,
    block_owner,
    block_pattern,
    latent,
    w_query,
    w_key,
    w_value,
    self_bias,
    w_out,
    norm_gain,
    w_inc,
    target,
):
    tiles = lax.axis_size("tile")
    groups = lax.axis_size("head")
    me = lax.axis_index("head")
    blocks = block_owner.shape[0]
    block_rows = obs_feat.shape[0] // blocks
    quarter = block_rows // groups
    cols = obs_feat.shape[1]
    lat_rows, width = latent.shape
    subs = block_pattern.shape[1]
    sub = lat_rows // subs
    local_heads = self_bias.shape[0]
    heads = local_heads * groups
    head_size = width // heads
    share = lat_rows // groups

    def swap(v, axis, mask, size):
        return lax.ppermute(v, axis, [(d, d ^ mask) for d in range(size)])

    def pick(v, which):
        return lax.dynamic_index_in_dim(v, which, 0, keepdims=False)

    tile = lax.axis_index("tile")
    whole = lambda *shape: pl.BlockSpec(shape, lambda g, *_: (0,) * len(shape))
    owners = jnp.concatenate([block_owner[:, 0], me[None].astype(jnp.int32)])
    alive = jnp.max(block_pattern, axis=1)
    marks, taken = pl.pallas_call(
        marks_kernel,
        grid_spec=pltpu.PrefetchScalarGridSpec(
            num_scalar_prefetch=2,
            grid=(1,),
            in_specs=[whole(blocks, block_rows), whole(blocks, subs)],
            out_specs=[
                whole(tiles, MARK_ROWS, 128),
                pl.BlockSpec(memory_space=pltpu.SMEM),
            ],
            scratch_shapes=[
                pltpu.VMEM((blocks, 128), F32),
                pltpu.SMEM((tiles,), jnp.int32),
            ],
        ),
        out_shape=[
            jax.ShapeDtypeStruct((tiles, MARK_ROWS, 128), F32),
            jax.ShapeDtypeStruct((SLOTS * tiles,), jnp.int32),
        ],
        name="marks",
    )(owners, alive, row_valid.reshape(blocks, block_rows), block_pattern)
    marks = lax.all_to_all(marks, "tile", split_axis=0, concat_axis=0, tiled=True)
    payload = pl.pallas_call(
        pack_kernel,
        grid_spec=pltpu.PrefetchScalarGridSpec(
            num_scalar_prefetch=1,
            grid=(1,),
            in_specs=[whole(blocks, groups, quarter, cols)],
            out_specs=whole(tiles, groups, SLOTS, quarter, cols),
        ),
        out_shape=jax.ShapeDtypeStruct((tiles, groups, SLOTS, quarter, cols), BF),
        compiler_params=pltpu.CompilerParams(vmem_limit_bytes=32 * 1024 * 1024),
        name="pack",
    )(taken, obs_feat.reshape(blocks, groups, quarter, cols))
    arrived = lax.all_to_all(
        payload.reshape(tiles * groups, SLOTS, quarter, cols),
        ("tile", "head"),
        split_axis=0,
        concat_axis=0,
        tiled=True,
    ).reshape(tiles, groups, SLOTS, quarter, cols)

    lists, bias = pl.pallas_call(
        lists_kernel,
        grid=(1,),
        in_specs=[whole(tiles, MARK_ROWS, 128)],
        out_specs=[whole(subs, 256), whole(SLOTS * tiles, 128)],
        out_shape=[
            jax.ShapeDtypeStruct((subs, 256), jnp.int32),
            jax.ShapeDtypeStruct((SLOTS * tiles, 128), F32),
        ],
        name="lists",
    )(marks)

    stacked = lax.all_gather(
        jnp.concatenate([w_query, w_key, w_value, w_out.T], axis=1), "head", axis=0
    )
    wq, wk, wv, wo = [
        stacked[:, :, a * 128:(a + 1) * 128].transpose(1, 0, 2).reshape(width, width)
        for a in range(4)
    ]
    wo = wo.T
    by_distance = jnp.stack(
        [self_bias] + [swap(self_bias, "head", d, groups) for d in range(1, groups)]
    )
    turn = jnp.arange(groups, dtype=jnp.int32) ^ me
    bias_all = jnp.take(by_distance, turn, axis=0).reshape(heads)
    queries = jnp.dot(latent, wq, preferred_element_type=F32).astype(BF)
    own_key = jnp.dot(latent, wk, preferred_element_type=F32).astype(BF)
    q3 = queries.reshape(lat_rows, heads, head_size)
    k3 = wk.reshape(width, heads, head_size)
    scale = 1.0 / math.sqrt(head_size)
    qw = (
        jnp.einsum("lhd,khd->hlk", q3, k3, preferred_element_type=F32) * scale
    ).astype(BF)
    own = (
        jnp.sum(
            q3.astype(F32) * own_key.reshape(lat_rows, heads, head_size).astype(F32), axis=-1
        )
        * scale
        + bias_all[None, :]
    )
    keep = (me == 0).astype(F32)
    states = jnp.pad(
        jnp.concatenate([own, jnp.full((lat_rows, heads), keep)], axis=1),
        ((0, 0), (0, 128 - 2 * heads)),
    )
    numer = jnp.dot(latent, wv, preferred_element_type=F32) * keep

    def attend(x, numer, states, final):
        if final:
            out_specs = pl.BlockSpec((sub, width + 128), lambda g, *_: (g, 0))
            out_shape = jax.ShapeDtypeStruct((lat_rows, width + 128), BF)
        else:
            out_specs = [
                pl.BlockSpec((sub, width), lambda g, *_: (g, 0)),
                pl.BlockSpec((sub, 128), lambda g, *_: (g, 0)),
            ]
            out_shape = [
                jax.ShapeDtypeStruct((lat_rows, width), F32),
                jax.ShapeDtypeStruct((lat_rows, 128), F32),
            ]
        return pl.pallas_call(
            functools.partial(attend_kernel, final),
            grid_spec=pltpu.PrefetchScalarGridSpec(
                num_scalar_prefetch=1,
                grid=(subs,),
                in_specs=[
                    whole(*x.shape),
                    whole(SLOTS * tiles, 128),
                    pl.BlockSpec((heads, sub, width), lambda g, *_: (0, g, 0)),
                    pl.BlockSpec((sub, 128), lambda g, *_: (g, 0)),
                    pl.BlockSpec((sub, width), lambda g, *_: (g, 0)),
                    whole(width, width),
                ],
                out_specs=out_specs,
                scratch_shapes=[
                    pltpu.VMEM((CHUNK * quarter, width), BF),
                    pltpu.VMEM((heads * sub, width), F32),
                    pltpu.VMEM((heads * sub, 128), F32),
                    pltpu.VMEM((heads * sub, 128), F32),
                ],
            ),
            out_shape=out_shape,
            compiler_params=pltpu.CompilerParams(vmem_limit_bytes=40 * 1024 * 1024),
            name="attend",
        )(lists, x, bias, qw, states, numer, wv)

    partial = attend(arrived, numer, states, True)

    partial = partial.reshape(groups, share, width + 128)
    received = [pick(partial, me)] + [
        swap(pick(partial, me ^ d), "head", d, groups) for d in range(1, groups)
    ]
    row = lambda *shape: pl.BlockSpec(shape, lambda i, m: (m[0], 0))
    full = lambda *shape: pl.BlockSpec(shape, lambda i, m: (0,) * len(shape))
    packed = pl.pallas_call(
        finish_kernel,
        grid_spec=pltpu.PrefetchScalarGridSpec(
            num_scalar_prefetch=1,
            grid=(1,),
            in_specs=[full(share, width + 128)] * 4
            + [
                row(share, width),
                full(width, width),
                full(1, width),
                full(width, 128),
                row(share, 128),
            ],
            out_specs=full(groups, 128 + share, 128),
        ),
        out_shape=jax.ShapeDtypeStruct((groups, 128 + share, 128), F32),
        compiler_params=pltpu.CompilerParams(vmem_limit_bytes=32 * 1024 * 1024),
        name="finish",
    )(
        me[None].astype(jnp.int32),
        *received,
        latent,
        wo,
        norm_gain[None, :],
        w_inc,
        target,
    )
    grads = [pick(packed, me)[:128]] + [
        swap(pick(packed, me ^ d)[:128], "head", d, groups) for d in range(1, groups)
    ]
    grad = (grads[0] + grads[1]) + (grads[2] + grads[3])
    for low, high in ((1, 2), (4, 8), (16, 32)):
        a, b, c = (swap(grad, "tile", m, tiles) for m in (low, high, low + high))
        grad = (grad + a) + (b + c)
    mine = packed[0, 128:]
    preds = jnp.stack([mine] + [swap(mine, "head", d, groups) for d in range(1, groups)])
    predicted = jnp.take(preds, turn, axis=0).reshape(lat_rows, 128)
    return predicted, grad * (1.0 / math.sqrt(lat_rows * tiles))


def solution(mesh):
    in_specs = (
        P("tile", "head"),
        P("tile"),
        P("tile", None),
        P("tile", None),
        P("tile", None),
        P(None, "head"),
        P(None, "head"),
        P(None, "head"),
        P("head"),
        P("head", None),
        P(),
        P(),
        P("tile", None),
    )
    out_specs = (P("tile", None), P("head", None))
    return jax.shard_map(body, mesh=mesh, in_specs=in_specs, out_specs=out_specs, check_vma=False)
```

```python
import math

import jax
import jax.numpy as jnp
from jax import lax
from jax.experimental import pallas as pl
from jax.experimental.pallas import tpu as pltpu
from jax.sharding import PartitionSpec as P

BF = jnp.bfloat16
F32 = jnp.float32
NEG = -1e30
SLOTS = 2
CHUNK = 8
PAIR = 2
MARK_ROWS = 2


def marks_kernel(owner, row_marks, pattern, marks, slots, info, taken):
    tiles = marks.shape[0]
    blocks = row_marks.shape[0]
    subs = pattern.shape[0]
    quarter = 32
    j = lax.axis_index("head")
    turned = pltpu.roll(row_marks[...].astype(F32), (128 - j * quarter) % 128, 1)
    lane = lax.broadcasted_iota(jnp.int32, (blocks, 128), 1)
    spot = lax.broadcasted_iota(jnp.int32, (subs, 128), 1)
    line = lax.broadcasted_iota(jnp.int32, (subs, 128), 0)
    shift = (spot == line + quarter).astype(F32).astype(BF)
    groups = lax.dot_general(
        pattern[...].astype(F32).astype(BF),
        shift,
        (((0,), (0,)), ((), ())),
        preferred_element_type=F32,
    )
    info[...] = jnp.where(lane < quarter, turned, groups)
    marks[...] = jnp.zeros_like(marks)

    def clear(t, carry):
        taken[t] = 0
        slots[t] = blocks
        slots[tiles + t] = blocks
        return carry

    lax.fori_loop(0, tiles, clear, 0, unroll=8)

    def place(b, carry):
        t = owner[b]
        k = jnp.minimum(taken[t], SLOTS - 1)
        taken[t] = k + 1
        slots[k * tiles + t] = b
        marks[t, pl.ds(k, 1), :] = info[pl.ds(b, 1), :]
        return carry

    lax.fori_loop(0, blocks, place, 0, unroll=4)


def pack_kernel(slots, obs, payload):
    tiles = payload.shape[0]
    blocks = obs.shape[0]

    def fill(t, carry):
        for k in range(SLOTS):
            b = slots[k * tiles + t]

            @pl.when(b < blocks)
            def _():
                payload[t, :, k] = obs[b]

            @pl.when(b >= blocks)
            def _():
                payload[t, :, k] = jnp.zeros(obs.shape[1:], BF)

        return carry

    lax.fori_loop(0, tiles, fill, 0)


def lists_kernel(found, lists, bias):
    tiles = found.shape[0]
    slots = SLOTS * tiles
    quarter = 32
    subs = lists.shape[0]
    mine = jnp.concatenate([found[:, k, :] for k in range(SLOTS)], axis=0).astype(BF)
    ahead = (
        lax.broadcasted_iota(jnp.int32, (slots, slots), 0)
        < lax.broadcasted_iota(jnp.int32, (slots, slots), 1)
    ).astype(F32).astype(BF)
    pick_group = (
        lax.broadcasted_iota(jnp.int32, (subs, 128), 1)
        == lax.broadcasted_iota(jnp.int32, (subs, 128), 0) + quarter
    ).astype(F32).astype(BF)
    up = lax.broadcasted_iota(jnp.int32, (128, 128), 0)
    along = lax.broadcasted_iota(jnp.int32, (128, 128), 1)
    widen = ((up < quarter) & (up == along % quarter)).astype(F32).astype(BF)
    live = lax.dot_general(
        pick_group, mine, (((1,), (1,)), ((), ())), preferred_element_type=F32
    )
    place = jnp.dot(live.astype(BF), ahead, preferred_element_type=F32)
    turn = lax.broadcasted_iota(jnp.int32, (subs, slots, slots), 1).astype(F32)
    name = lax.broadcasted_iota(jnp.int32, (subs, slots, slots), 2).astype(F32)
    hit = (place[:, None, :] == turn) & (live[:, None, :] > 0.5)
    order = jnp.sum(jnp.where(hit, name, 0.0), axis=2)
    count = jnp.sum(live, axis=1, keepdims=True)
    lists[:, :128] = order.astype(jnp.int32)
    lists[:, 128:] = jnp.broadcast_to(count, (subs, 128)).astype(jnp.int32)
    rows = jnp.dot(mine, widen, preferred_element_type=F32)
    bias[...] = (rows - 1.0) * (-NEG)


def split3(v):
    hi = v.astype(BF).astype(F32)
    mid = (v - hi).astype(BF).astype(F32)
    return hi, mid, v - hi - mid


def attend_kernel(lists, x, bias, qw, begun, given, wv, out, *scratch):
    step_id = pl.program_id(0)
    heads, both, width = qw.shape
    sub = both // PAIR
    rows = heads * sub
    tiles, parts, _, quarter, cols = x.shape
    size = CHUNK * quarter
    per = 128 // quarter
    lane_slot = lax.broadcasted_iota(jnp.int32, (1, 128), 1) // quarter
    lane = lax.broadcasted_iota(jnp.int32, (sub, 128), 1)
    xbufs, accs, tops, dens = (scratch[q * PAIR:(q + 1) * PAIR] for q in range(4))

    def gather(g, n, c, xbuf):
        shades = []
        for part in range(CHUNK // per):
            shade = jnp.full((1, 128), NEG, F32)
            for v in range(per):
                u = part * per + v
                place = c * CHUNK + u
                s = lists[g, jnp.maximum(jnp.minimum(place, n - 1), 0)]
                for i in range(parts):
                    xbuf[u * quarter:(u + 1) * quarter, i * cols:(i + 1) * cols] = x[
                        s % tiles, i, s // tiles
                    ]
                live = (lane_slot == v) & (place < n)
                shade = jnp.where(live, bias[pl.ds(s, 1), :], shade)
            shades.append(shade)
        return xbuf[...], jnp.concatenate(shades, axis=1)

    def chunk(queries, rows_x, shade, old):
        scores = lax.dot_general(
            queries, rows_x, (((1,), (1,)), ((), ())), preferred_element_type=F32
        ) + shade
        new = jnp.maximum(old, jnp.max(scores, axis=1, keepdims=True))
        weights = jnp.exp(scores - jnp.concatenate([new] * (size // 128), axis=1))
        total = jnp.sum(weights, axis=1, keepdims=True)
        more = jnp.dot(weights.astype(BF), rows_x, preferred_element_type=F32)
        return new, jnp.exp(old - new), total, more

    counts, begins = [], []
    for p in range(PAIR):
        g = step_id * PAIR + p
        n = lists[g, 128]
        counts.append(n)
        start = begun[p * sub:(p + 1) * sub, :]
        old = jnp.concatenate(
            [jnp.broadcast_to(start[:, h:h + 1], (sub, 128)) for h in range(heads)], axis=0
        )
        den = jnp.concatenate(
            [
                jnp.broadcast_to(start[:, heads + h:heads + h + 1], (sub, 128))
                for h in range(heads)
            ],
            axis=0,
        )
        begins.append(old)
        rows_x, shade = gather(g, n, 0, xbufs[p])
        queries = qw[:, p * sub:(p + 1) * sub, :].reshape(rows, width)
        new, shrink, total, more = chunk(queries, rows_x, shade, old)
        accs[p][...] = more
        tops[p][...] = new
        dens[p][...] = den * shrink + total

    for p in range(PAIR):
        g = step_id * PAIR + p

        @pl.when(counts[p] > CHUNK)
        def _(p=p, g=g):
            def again(c, carry):
                rows_x, shade = gather(g, counts[p], c, xbufs[p])
                queries = qw[:, p * sub:(p + 1) * sub, :].reshape(rows, width)
                new, shrink, total, more = chunk(queries, rows_x, shade, tops[p][...])
                tops[p][...] = new
                dens[p][...] = dens[p][...] * shrink + total
                wide = jnp.concatenate([shrink] * (width // 128), axis=1)
                accs[p][...] = accs[p][...] * wide + more
                return carry

            lax.fori_loop(1, (counts[p] + CHUNK - 1) // CHUNK, again, 0)

    half = width // 2
    for p in range(PAIR):
        place = slice(p * sub, (p + 1) * sub)
        top = tops[p][...]
        shrink = jnp.exp(begins[p] - top)
        state = jnp.zeros((sub, 128), F32)
        for h in range(heads):
            line = slice(h * sub, (h + 1) * sub)
            state = jnp.where(lane == h, top[line], state)
            state = jnp.where(lane == heads + h, dens[p][line, :], state)
        hi, mid, lo = split3(state)
        packed = hi + pltpu.roll(mid, 2 * heads, 1) + pltpu.roll(lo, 4 * heads, 1)
        out[place, width:] = packed.astype(BF)
        for side in range(2):
            here = slice(side * rows // 2, (side + 1) * rows // 2)
            mixed = jnp.dot(
                accs[p][here, :].astype(BF),
                wv[:, side * half:(side + 1) * half],
                preferred_element_type=F32,
            )
            for c in range(half // 128):
                col = side * half + c * 128
                two = []
                for h in (2 * c, 2 * c + 1):
                    line = slice(h * sub, (h + 1) * sub)
                    far = side * rows // 2
                    two.append(
                        given[place, col:col + 128] * shrink[far + h * sub:far + (h + 1) * sub]
                        + mixed[line, c * 128:(c + 1) * 128]
                    )
                out[place, col:col + 128] = jnp.where(
                    lane < width // heads, two[0], two[1]
                ).astype(BF)


def combine_kernel(r0, r1, r2, r3, out):
    width = out.shape[1]
    heads = 8
    line = lax.broadcasted_iota(jnp.int32, (128, 2 * width), 0)
    col = lax.broadcasted_iota(jnp.int32, (128, 2 * width), 1)
    match = (
        (line % heads == (col % width) // (width // heads))
        & ((line // heads) % 2 == col // width)
        & (line < 6 * heads)
    )
    spread = match.astype(F32).astype(BF)
    tops, dens, nums = [], [], []
    for r in (r0, r1, r2, r3):
        wide = jnp.dot(r[:, width:], spread, preferred_element_type=F32)
        tops.append(wide[:, :width])
        dens.append(wide[:, width:])
        nums.append(r[:, :width].astype(F32))
    best = jnp.maximum(jnp.maximum(tops[0], tops[1]), jnp.maximum(tops[2], tops[3]))
    scale = [jnp.exp(v - best) for v in tops]
    numer = sum(a * b for a, b in zip(scale, nums))
    denom = sum(a * b for a, b in zip(scale, dens))
    out[...] = (numer / denom).astype(BF)


def finish_kernel(place, a0, a1, a2, a3, lat, w_out, gain, w_inc, target, predicted, grad, cut):
    me = place[0]
    share, width = a0.shape
    dims = (((0,), (0,)), ((), ()))
    total = jnp.zeros(grad.shape, F32)
    for d, a in enumerate((a0, a1, a2, a3)):
        here = pl.ds(pl.multiple_of((me ^ d) * share, share), share)
        updated = lat[here, :].astype(F32) + jnp.dot(
            a[...], w_out[...], preferred_element_type=F32
        )
        power = jnp.mean(updated * updated, axis=1, keepdims=True)
        normed = (updated * lax.rsqrt(power + 1e-6) * gain[...]).astype(BF)
        answer = jnp.dot(normed, w_inc[...], preferred_element_type=F32)
        predicted[here, :] = answer
        residual = answer - target[here, :].astype(F32)
        high = residual.astype(BF)
        low = (residual - high.astype(F32)).astype(BF)
        for c in range(width // 128):
            cut[d, c] = normed[:, c * 128:(c + 1) * 128]
        mine = cut[d, me]
        total = total + lax.dot_general(mine, high, dims, preferred_element_type=F32)
        total = total + lax.dot_general(mine, low, dims, preferred_element_type=F32)
    grad[...] = total


def body(
    obs_feat,
    row_valid,
    block_owner,
    block_pattern,
    latent,
    w_query,
    w_key,
    w_value,
    self_bias,
    w_out,
    norm_gain,
    w_inc,
    target,
):
    tiles = lax.axis_size("tile")
    groups = lax.axis_size("head")
    me = lax.axis_index("head")
    blocks = block_owner.shape[0]
    block_rows = obs_feat.shape[0] // blocks
    quarter = block_rows // groups
    cols = obs_feat.shape[1]
    lat_rows, width = latent.shape
    subs = block_pattern.shape[1]
    sub = lat_rows // subs
    local_heads = self_bias.shape[0]
    heads = local_heads * groups
    head_size = width // heads
    share = lat_rows // groups

    def swap(v, axis, mask, size):
        return lax.ppermute(v, axis, [(d, d ^ mask) for d in range(size)])

    def pick(v, which):
        return lax.dynamic_index_in_dim(v, which, 0, keepdims=False)

    tile = lax.axis_index("tile")
    whole = lambda *shape: pl.BlockSpec(shape, lambda g, *_: (0,) * len(shape))
    marks, taken = pl.pallas_call(
        marks_kernel,
        grid_spec=pltpu.PrefetchScalarGridSpec(
            num_scalar_prefetch=1,
            grid=(1,),
            in_specs=[whole(blocks, block_rows), whole(subs, blocks)],
            out_specs=[
                whole(tiles, MARK_ROWS, 128),
                pl.BlockSpec(memory_space=pltpu.SMEM),
            ],
            scratch_shapes=[
                pltpu.VMEM((blocks, 128), F32),
                pltpu.SMEM((tiles,), jnp.int32),
            ],
        ),
        out_shape=[
            jax.ShapeDtypeStruct((tiles, MARK_ROWS, 128), F32),
            jax.ShapeDtypeStruct((SLOTS * tiles,), jnp.int32),
        ],
        name="marks",
    )(block_owner[:, 0], row_valid.reshape(blocks, block_rows), block_pattern.T)
    marks = lax.all_to_all(marks, "tile", split_axis=0, concat_axis=0, tiled=True)
    payload = pl.pallas_call(
        pack_kernel,
        grid_spec=pltpu.PrefetchScalarGridSpec(
            num_scalar_prefetch=1,
            grid=(1,),
            in_specs=[whole(blocks, groups, quarter, cols)],
            out_specs=whole(tiles, groups, SLOTS, quarter, cols),
        ),
        out_shape=jax.ShapeDtypeStruct((tiles, groups, SLOTS, quarter, cols), BF),
        compiler_params=pltpu.CompilerParams(vmem_limit_bytes=32 * 1024 * 1024),
        name="pack",
    )(taken, obs_feat.reshape(blocks, groups, quarter, cols))
    arrived = lax.all_to_all(
        payload.reshape(tiles * groups, SLOTS, quarter, cols),
        ("tile", "head"),
        split_axis=0,
        concat_axis=0,
        tiled=True,
    ).reshape(tiles, groups, SLOTS, quarter, cols)

    lists, bias = pl.pallas_call(
        lists_kernel,
        grid=(1,),
        in_specs=[whole(tiles, MARK_ROWS, 128)],
        out_specs=[whole(subs, 256), whole(SLOTS * tiles, 128)],
        out_shape=[
            jax.ShapeDtypeStruct((subs, 256), jnp.int32),
            jax.ShapeDtypeStruct((SLOTS * tiles, 128), F32),
        ],
        name="lists",
    )(marks)

    stacked = lax.all_gather(
        jnp.concatenate([w_query, w_key, w_value, w_out.T], axis=1), "head", axis=0
    )
    wq, wk, wv, wo = [
        stacked[:, :, a * 128:(a + 1) * 128].transpose(1, 0, 2).reshape(width, width)
        for a in range(4)
    ]
    wo = wo.T
    by_distance = jnp.stack(
        [self_bias] + [swap(self_bias, "head", d, groups) for d in range(1, groups)]
    )
    turn = jnp.arange(groups, dtype=jnp.int32) ^ me
    bias_all = jnp.take(by_distance, turn, axis=0).reshape(heads)
    queries = jnp.dot(latent, wq, preferred_element_type=F32).astype(BF)
    own_key = jnp.dot(latent, wk, preferred_element_type=F32).astype(BF)
    q3 = queries.reshape(lat_rows, heads, head_size)
    k3 = wk.reshape(width, heads, head_size)
    scale = 1.0 / math.sqrt(head_size)
    qw = (
        jnp.einsum("lhd,khd->hlk", q3, k3, preferred_element_type=F32) * scale
    ).astype(BF)
    own = (
        jnp.sum(
            q3.astype(F32) * own_key.reshape(lat_rows, heads, head_size).astype(F32), axis=-1
        )
        * scale
        + bias_all[None, :]
    )
    keep = (me == 0).astype(F32)
    states = jnp.pad(
        jnp.concatenate([own, jnp.full((lat_rows, heads), keep)], axis=1),
        ((0, 0), (0, 128 - 2 * heads)),
    )
    numer = jnp.dot(latent, wv, preferred_element_type=F32) * keep

    block = PAIR * sub
    scratch = [
        shape
        for shape in (
            pltpu.VMEM((CHUNK * quarter, width), BF),
            pltpu.VMEM((heads * sub, width), F32),
            pltpu.VMEM((heads * sub, 128), F32),
            pltpu.VMEM((heads * sub, 128), F32),
        )
        for _ in range(PAIR)
    ]
    partial = pl.pallas_call(
        attend_kernel,
        grid_spec=pltpu.PrefetchScalarGridSpec(
            num_scalar_prefetch=1,
            grid=(subs // PAIR,),
            in_specs=[
                whole(*arrived.shape),
                whole(SLOTS * tiles, 128),
                pl.BlockSpec((heads, block, width), lambda g, *_: (0, g, 0)),
                pl.BlockSpec((block, 128), lambda g, *_: (g, 0)),
                pl.BlockSpec((block, width), lambda g, *_: (g, 0)),
                whole(width, width),
            ],
            out_specs=pl.BlockSpec((block, width + 128), lambda g, *_: (g, 0)),
            scratch_shapes=scratch,
        ),
        out_shape=jax.ShapeDtypeStruct((lat_rows, width + 128), BF),
        compiler_params=pltpu.CompilerParams(vmem_limit_bytes=40 * 1024 * 1024),
        name="attend",
    )(lists, arrived, bias, qw, states, numer, wv)

    partial = partial.reshape(groups, share, width + 128)
    received = [pick(partial, me)] + [
        swap(pick(partial, me ^ d), "head", d, groups) for d in range(1, groups)
    ]
    attended = pl.pallas_call(
        combine_kernel,
        grid=(1,),
        in_specs=[whole(share, width + 128)] * groups,
        out_specs=whole(share, width),
        out_shape=jax.ShapeDtypeStruct((share, width), BF),
        name="combine",
    )(*received)
    gathered = [attended] + [swap(attended, "head", d, groups) for d in range(1, groups)]
    predicted, grad = pl.pallas_call(
        finish_kernel,
        grid_spec=pltpu.PrefetchScalarGridSpec(
            num_scalar_prefetch=1,
            grid=(1,),
            in_specs=[whole(share, width)] * groups
            + [
                whole(lat_rows, width),
                whole(width, width),
                whole(1, width),
                whole(width, 128),
                whole(lat_rows, 128),
            ],
            out_specs=[whole(lat_rows, 128), whole(cols, 128)],
            scratch_shapes=[pltpu.VMEM((groups, width // 128, share, 128), BF)],
        ),
        out_shape=[
            jax.ShapeDtypeStruct((lat_rows, 128), F32),
            jax.ShapeDtypeStruct((cols, 128), F32),
        ],
        compiler_params=pltpu.CompilerParams(vmem_limit_bytes=32 * 1024 * 1024),
        name="finish",
    )(
        me[None].astype(jnp.int32),
        *gathered,
        latent,
        wo,
        norm_gain[None, :],
        w_inc,
        target,
    )
    for low, high in ((1, 2), (4, 8), (16, 32)):
        a, b, c = (swap(grad, "tile", m, tiles) for m in (low, high, low + high))
        grad = (grad + a) + (b + c)
    return predicted, grad * (1.0 / math.sqrt(lat_rows * tiles))


def solution(mesh):
    in_specs = (
        P("tile", "head"),
        P("tile"),
        P("tile", None),
        P("tile", None),
        P("tile", None),
        P(None, "head"),
        P(None, "head"),
        P(None, "head"),
        P("head"),
        P("head", None),
        P(),
        P(),
        P("tile", None),
    )
    out_specs = (P("tile", None), P("head", None))
    return jax.shard_map(body, mesh=mesh, in_specs=in_specs, out_specs=out_specs, check_vma=False)
```

```python
import math

import jax
import jax.numpy as jnp
from jax import lax
from jax.experimental import pallas as pl
from jax.experimental.pallas import tpu as pltpu
from jax.sharding import PartitionSpec as P

BF = jnp.bfloat16
F32 = jnp.float32
NEG = -1e30
SLOTS = 2
CHUNK = 8
PAIR = 4
MARK_ROWS = 2


def marks_kernel(owner, row_marks, pattern, marks, slots, info, taken):
    tiles = marks.shape[0]
    blocks = row_marks.shape[0]
    subs = pattern.shape[0]
    quarter = 32
    j = lax.axis_index("head")
    turned = pltpu.roll(row_marks[...].astype(F32), (128 - j * quarter) % 128, 1)
    lane = lax.broadcasted_iota(jnp.int32, (blocks, 128), 1)
    spot = lax.broadcasted_iota(jnp.int32, (subs, 128), 1)
    line = lax.broadcasted_iota(jnp.int32, (subs, 128), 0)
    shift = (spot == line + quarter).astype(F32).astype(BF)
    groups = lax.dot_general(
        pattern[...].astype(F32).astype(BF),
        shift,
        (((0,), (0,)), ((), ())),
        preferred_element_type=F32,
    )
    info[...] = jnp.where(lane < quarter, turned, groups)
    marks[...] = jnp.zeros_like(marks)

    def clear(t, carry):
        taken[t] = 0
        slots[t] = blocks
        slots[tiles + t] = blocks
        return carry

    lax.fori_loop(0, tiles, clear, 0, unroll=8)

    def place(b, carry):
        t = owner[b]
        k = jnp.minimum(taken[t], SLOTS - 1)
        taken[t] = k + 1
        slots[k * tiles + t] = b
        marks[t, pl.ds(k, 1), :] = info[pl.ds(b, 1), :]
        return carry

    lax.fori_loop(0, blocks, place, 0, unroll=4)


def pack_kernel(slots, obs, payload):
    tiles = payload.shape[0]
    blocks = obs.shape[0]

    def fill(t, carry):
        for k in range(SLOTS):
            b = slots[k * tiles + t]

            @pl.when(b < blocks)
            def _():
                payload[t, :, k] = obs[b]

            @pl.when(b >= blocks)
            def _():
                payload[t, :, k] = jnp.zeros(obs.shape[1:], BF)

        return carry

    lax.fori_loop(0, tiles, fill, 0)


def lists_kernel(found, lists, bias):
    tiles = found.shape[0]
    slots = SLOTS * tiles
    quarter = 32
    subs = lists.shape[0]
    mine = jnp.concatenate([found[:, k, :] for k in range(SLOTS)], axis=0).astype(BF)
    ahead = (
        lax.broadcasted_iota(jnp.int32, (slots, slots), 0)
        < lax.broadcasted_iota(jnp.int32, (slots, slots), 1)
    ).astype(F32).astype(BF)
    pick_group = (
        lax.broadcasted_iota(jnp.int32, (subs, 128), 1)
        == lax.broadcasted_iota(jnp.int32, (subs, 128), 0) + quarter
    ).astype(F32).astype(BF)
    up = lax.broadcasted_iota(jnp.int32, (128, 128), 0)
    along = lax.broadcasted_iota(jnp.int32, (128, 128), 1)
    widen = ((up < quarter) & (up == along % quarter)).astype(F32).astype(BF)
    live = lax.dot_general(
        pick_group, mine, (((1,), (1,)), ((), ())), preferred_element_type=F32
    )
    place = jnp.dot(live.astype(BF), ahead, preferred_element_type=F32)
    turn = lax.broadcasted_iota(jnp.int32, (subs, slots, slots), 1).astype(F32)
    name = lax.broadcasted_iota(jnp.int32, (subs, slots, slots), 2).astype(F32)
    hit = (place[:, None, :] == turn) & (live[:, None, :] > 0.5)
    order = jnp.sum(jnp.where(hit, name, 0.0), axis=2)
    count = jnp.sum(live, axis=1, keepdims=True)
    lists[:, :128] = order.astype(jnp.int32)
    lists[:, 128:] = jnp.broadcast_to(count, (subs, 128)).astype(jnp.int32)
    rows = jnp.dot(mine, widen, preferred_element_type=F32)
    bias[...] = (rows - 1.0) * (-NEG)


def split3(v):
    hi = v.astype(BF).astype(F32)
    mid = (v - hi).astype(BF).astype(F32)
    return hi, mid, v - hi - mid


def attend_kernel(lists, x, bias, qw, begun, given, wv, out, *scratch):
    step_id = pl.program_id(0)
    heads, both, width = qw.shape
    sub = both // PAIR
    rows = heads * sub
    tiles, parts, _, quarter, cols = x.shape
    size = CHUNK * quarter
    per = 128 // quarter
    lane_slot = lax.broadcasted_iota(jnp.int32, (1, 128), 1) // quarter
    lane = lax.broadcasted_iota(jnp.int32, (sub, 128), 1)
    xbufs, accs, tops, dens = (scratch[q * PAIR:(q + 1) * PAIR] for q in range(4))

    def gather(g, n, c, xbuf):
        shades = []
        for part in range(CHUNK // per):
            shade = jnp.full((1, 128), NEG, F32)
            for v in range(per):
                u = part * per + v
                place = c * CHUNK + u
                s = lists[g, jnp.maximum(jnp.minimum(place, n - 1), 0)]
                for i in range(parts):
                    xbuf[u * quarter:(u + 1) * quarter, i * cols:(i + 1) * cols] = x[
                        s % tiles, i, s // tiles
                    ]
                live = (lane_slot == v) & (place < n)
                shade = jnp.where(live, bias[pl.ds(s, 1), :], shade)
            shades.append(shade)
        return xbuf[...], jnp.concatenate(shades, axis=1)

    def chunk(queries, rows_x, shade, old):
        scores = lax.dot_general(
            queries, rows_x, (((1,), (1,)), ((), ())), preferred_element_type=F32
        ) + shade
        new = jnp.maximum(old, jnp.max(scores, axis=1, keepdims=True))
        weights = jnp.exp(scores - jnp.concatenate([new] * (size // 128), axis=1))
        total = jnp.sum(weights, axis=1, keepdims=True)
        more = jnp.dot(weights.astype(BF), rows_x, preferred_element_type=F32)
        return new, jnp.exp(old - new), total, more

    counts, begins = [], []
    for p in range(PAIR):
        g = step_id * PAIR + p
        n = lists[g, 128]
        counts.append(n)
        start = begun[p * sub:(p + 1) * sub, :]
        old = jnp.concatenate(
            [jnp.broadcast_to(start[:, h:h + 1], (sub, 128)) for h in range(heads)], axis=0
        )
        den = jnp.concatenate(
            [
                jnp.broadcast_to(start[:, heads + h:heads + h + 1], (sub, 128))
                for h in range(heads)
            ],
            axis=0,
        )
        begins.append(old)
        rows_x, shade = gather(g, n, 0, xbufs[p])
        queries = qw[:, p * sub:(p + 1) * sub, :].reshape(rows, width)
        new, shrink, total, more = chunk(queries, rows_x, shade, old)
        accs[p][...] = more
        tops[p][...] = new
        dens[p][...] = den * shrink + total

    for p in range(PAIR):
        g = step_id * PAIR + p

        @pl.when(counts[p] > CHUNK)
        def _(p=p, g=g):
            def again(c, carry):
                rows_x, shade = gather(g, counts[p], c, xbufs[p])
                queries = qw[:, p * sub:(p + 1) * sub, :].reshape(rows, width)
                new, shrink, total, more = chunk(queries, rows_x, shade, tops[p][...])
                tops[p][...] = new
                dens[p][...] = dens[p][...] * shrink + total
                wide = jnp.concatenate([shrink] * (width // 128), axis=1)
                accs[p][...] = accs[p][...] * wide + more
                return carry

            lax.fori_loop(1, (counts[p] + CHUNK - 1) // CHUNK, again, 0)

    half = width // 2
    for p in range(PAIR):
        place = slice(p * sub, (p + 1) * sub)
        top = tops[p][...]
        shrink = jnp.exp(begins[p] - top)
        state = jnp.zeros((sub, 128), F32)
        for h in range(heads):
            line = slice(h * sub, (h + 1) * sub)
            state = jnp.where(lane == h, top[line], state)
            state = jnp.where(lane == heads + h, dens[p][line, :], state)
        hi, mid, lo = split3(state)
        packed = hi + pltpu.roll(mid, 2 * heads, 1) + pltpu.roll(lo, 4 * heads, 1)
        out[place, width:] = packed.astype(BF)
        for side in range(2):
            here = slice(side * rows // 2, (side + 1) * rows // 2)
            mixed = jnp.dot(
                accs[p][here, :].astype(BF),
                wv[:, side * half:(side + 1) * half],
                preferred_element_type=F32,
            )
            for c in range(half // 128):
                col = side * half + c * 128
                two = []
                for h in (2 * c, 2 * c + 1):
                    line = slice(h * sub, (h + 1) * sub)
                    far = side * rows // 2
                    two.append(
                        given[place, col:col + 128] * shrink[far + h * sub:far + (h + 1) * sub]
                        + mixed[line, c * 128:(c + 1) * 128]
                    )
                out[place, col:col + 128] = jnp.where(
                    lane < width // heads, two[0], two[1]
                ).astype(BF)


def combine_kernel(r0, r1, r2, r3, out):
    width = out.shape[1]
    heads = 8
    line = lax.broadcasted_iota(jnp.int32, (128, 2 * width), 0)
    col = lax.broadcasted_iota(jnp.int32, (128, 2 * width), 1)
    match = (
        (line % heads == (col % width) // (width // heads))
        & ((line // heads) % 2 == col // width)
        & (line < 6 * heads)
    )
    spread = match.astype(F32).astype(BF)
    tops, dens, nums = [], [], []
    for r in (r0, r1, r2, r3):
        wide = jnp.dot(r[:, width:], spread, preferred_element_type=F32)
        tops.append(wide[:, :width])
        dens.append(wide[:, width:])
        nums.append(r[:, :width].astype(F32))
    best = jnp.maximum(jnp.maximum(tops[0], tops[1]), jnp.maximum(tops[2], tops[3]))
    scale = [jnp.exp(v - best) for v in tops]
    numer = sum(a * b for a, b in zip(scale, nums))
    denom = sum(a * b for a, b in zip(scale, dens))
    out[...] = (numer / denom).astype(BF)


def finish_kernel(place, a0, a1, a2, a3, lat, w_out, gain, w_inc, target, predicted, grad, cut):
    me = place[0]
    share, width = a0.shape
    dims = (((0,), (0,)), ((), ()))
    total = jnp.zeros(grad.shape, F32)
    for d, a in enumerate((a0, a1, a2, a3)):
        here = pl.ds(pl.multiple_of((me ^ d) * share, share), share)
        updated = lat[here, :].astype(F32) + jnp.dot(
            a[...], w_out[...], preferred_element_type=F32
        )
        power = jnp.mean(updated * updated, axis=1, keepdims=True)
        normed = (updated * lax.rsqrt(power + 1e-6) * gain[...]).astype(BF)
        answer = jnp.dot(normed, w_inc[...], preferred_element_type=F32)
        predicted[here, :] = answer
        residual = answer - target[here, :].astype(F32)
        high = residual.astype(BF)
        low = (residual - high.astype(F32)).astype(BF)
        for c in range(width // 128):
            cut[d, c] = normed[:, c * 128:(c + 1) * 128]
        mine = cut[d, me]
        total = total + lax.dot_general(mine, high, dims, preferred_element_type=F32)
        total = total + lax.dot_general(mine, low, dims, preferred_element_type=F32)
    grad[...] = total


def body(
    obs_feat,
    row_valid,
    block_owner,
    block_pattern,
    latent,
    w_query,
    w_key,
    w_value,
    self_bias,
    w_out,
    norm_gain,
    w_inc,
    target,
):
    tiles = lax.axis_size("tile")
    groups = lax.axis_size("head")
    me = lax.axis_index("head")
    blocks = block_owner.shape[0]
    block_rows = obs_feat.shape[0] // blocks
    quarter = block_rows // groups
    cols = obs_feat.shape[1]
    lat_rows, width = latent.shape
    subs = block_pattern.shape[1]
    sub = lat_rows // subs
    local_heads = self_bias.shape[0]
    heads = local_heads * groups
    head_size = width // heads
    share = lat_rows // groups

    def swap(v, axis, mask, size):
        return lax.ppermute(v, axis, [(d, d ^ mask) for d in range(size)])

    def pick(v, which):
        return lax.dynamic_index_in_dim(v, which, 0, keepdims=False)

    tile = lax.axis_index("tile")
    whole = lambda *shape: pl.BlockSpec(shape, lambda g, *_: (0,) * len(shape))
    marks, taken = pl.pallas_call(
        marks_kernel,
        grid_spec=pltpu.PrefetchScalarGridSpec(
            num_scalar_prefetch=1,
            grid=(1,),
            in_specs=[whole(blocks, block_rows), whole(subs, blocks)],
            out_specs=[
                whole(tiles, MARK_ROWS, 128),
                pl.BlockSpec(memory_space=pltpu.SMEM),
            ],
            scratch_shapes=[
                pltpu.VMEM((blocks, 128), F32),
                pltpu.SMEM((tiles,), jnp.int32),
            ],
        ),
        out_shape=[
            jax.ShapeDtypeStruct((tiles, MARK_ROWS, 128), F32),
            jax.ShapeDtypeStruct((SLOTS * tiles,), jnp.int32),
        ],
        name="marks",
    )(block_owner[:, 0], row_valid.reshape(blocks, block_rows), block_pattern.T)
    marks = lax.all_to_all(marks, "tile", split_axis=0, concat_axis=0, tiled=True)
    payload = pl.pallas_call(
        pack_kernel,
        grid_spec=pltpu.PrefetchScalarGridSpec(
            num_scalar_prefetch=1,
            grid=(1,),
            in_specs=[whole(blocks, groups, quarter, cols)],
            out_specs=whole(tiles, groups, SLOTS, quarter, cols),
        ),
        out_shape=jax.ShapeDtypeStruct((tiles, groups, SLOTS, quarter, cols), BF),
        compiler_params=pltpu.CompilerParams(vmem_limit_bytes=32 * 1024 * 1024),
        name="pack",
    )(taken, obs_feat.reshape(blocks, groups, quarter, cols))
    arrived = lax.all_to_all(
        payload.reshape(tiles * groups, SLOTS, quarter, cols),
        ("tile", "head"),
        split_axis=0,
        concat_axis=0,
        tiled=True,
    ).reshape(tiles, groups, SLOTS, quarter, cols)

    lists, bias = pl.pallas_call(
        lists_kernel,
        grid=(1,),
        in_specs=[whole(tiles, MARK_ROWS, 128)],
        out_specs=[whole(subs, 256), whole(SLOTS * tiles, 128)],
        out_shape=[
            jax.ShapeDtypeStruct((subs, 256), jnp.int32),
            jax.ShapeDtypeStruct((SLOTS * tiles, 128), F32),
        ],
        name="lists",
    )(marks)

    stacked = jnp.concatenate([w_query, w_key, w_value, w_out.T], axis=1)
    near = jnp.stack(
        [stacked] + [swap(stacked, "head", d, groups) for d in range(1, groups)]
    )
    turn = jnp.arange(groups, dtype=jnp.int32) ^ me
    stacked = jnp.take(near, turn, axis=0)
    wq, wk, wv, wo = [
        stacked[:, :, a * 128:(a + 1) * 128].transpose(1, 0, 2).reshape(width, width)
        for a in range(4)
    ]
    wo = wo.T
    by_distance = jnp.stack(
        [self_bias] + [swap(self_bias, "head", d, groups) for d in range(1, groups)]
    )
    turn = jnp.arange(groups, dtype=jnp.int32) ^ me
    bias_all = jnp.take(by_distance, turn, axis=0).reshape(heads)
    queries = jnp.dot(latent, wq, preferred_element_type=F32).astype(BF)
    own_key = jnp.dot(latent, wk, preferred_element_type=F32).astype(BF)
    q3 = queries.reshape(lat_rows, heads, head_size)
    k3 = wk.reshape(width, heads, head_size)
    scale = 1.0 / math.sqrt(head_size)
    qw = (
        jnp.einsum("lhd,khd->hlk", q3, k3, preferred_element_type=F32) * scale
    ).astype(BF)
    own = (
        jnp.sum(
            q3.astype(F32) * own_key.reshape(lat_rows, heads, head_size).astype(F32), axis=-1
        )
        * scale
        + bias_all[None, :]
    )
    keep = (me == 0).astype(F32)
    states = jnp.pad(
        jnp.concatenate([own, jnp.full((lat_rows, heads), keep)], axis=1),
        ((0, 0), (0, 128 - 2 * heads)),
    )
    numer = jnp.dot(latent, wv, preferred_element_type=F32) * keep

    block = PAIR * sub
    scratch = [
        shape
        for shape in (
            pltpu.VMEM((CHUNK * quarter, width), BF),
            pltpu.VMEM((heads * sub, width), F32),
            pltpu.VMEM((heads * sub, 128), F32),
            pltpu.VMEM((heads * sub, 128), F32),
        )
        for _ in range(PAIR)
    ]
    partial = pl.pallas_call(
        attend_kernel,
        grid_spec=pltpu.PrefetchScalarGridSpec(
            num_scalar_prefetch=1,
            grid=(subs // PAIR,),
            in_specs=[
                whole(*arrived.shape),
                whole(SLOTS * tiles, 128),
                pl.BlockSpec((heads, block, width), lambda g, *_: (0, g, 0)),
                pl.BlockSpec((block, 128), lambda g, *_: (g, 0)),
                pl.BlockSpec((block, width), lambda g, *_: (g, 0)),
                whole(width, width),
            ],
            out_specs=pl.BlockSpec((block, width + 128), lambda g, *_: (g, 0)),
            scratch_shapes=scratch,
        ),
        out_shape=jax.ShapeDtypeStruct((lat_rows, width + 128), BF),
        compiler_params=pltpu.CompilerParams(vmem_limit_bytes=40 * 1024 * 1024),
        name="attend",
    )(lists, arrived, bias, qw, states, numer, wv)

    partial = partial.reshape(groups, share, width + 128)
    received = [pick(partial, me)] + [
        swap(pick(partial, me ^ d), "head", d, groups) for d in range(1, groups)
    ]
    attended = pl.pallas_call(
        combine_kernel,
        grid=(1,),
        in_specs=[whole(share, width + 128)] * groups,
        out_specs=whole(share, width),
        out_shape=jax.ShapeDtypeStruct((share, width), BF),
        name="combine",
    )(*received)
    gathered = [attended] + [swap(attended, "head", d, groups) for d in range(1, groups)]
    predicted, grad = pl.pallas_call(
        finish_kernel,
        grid_spec=pltpu.PrefetchScalarGridSpec(
            num_scalar_prefetch=1,
            grid=(1,),
            in_specs=[whole(share, width)] * groups
            + [
                whole(lat_rows, width),
                whole(width, width),
                whole(1, width),
                whole(width, 128),
                whole(lat_rows, 128),
            ],
            out_specs=[whole(lat_rows, 128), whole(cols, 128)],
            scratch_shapes=[pltpu.VMEM((groups, width // 128, share, 128), BF)],
        ),
        out_shape=[
            jax.ShapeDtypeStruct((lat_rows, 128), F32),
            jax.ShapeDtypeStruct((cols, 128), F32),
        ],
        compiler_params=pltpu.CompilerParams(vmem_limit_bytes=32 * 1024 * 1024),
        name="finish",
    )(
        me[None].astype(jnp.int32),
        *gathered,
        latent,
        wo,
        norm_gain[None, :],
        w_inc,
        target,
    )
    for low, high in ((1, 2), (4, 8), (16, 32)):
        a, b, c = (swap(grad, "tile", m, tiles) for m in (low, high, low + high))
        grad = (grad + a) + (b + c)
    return predicted, grad * (1.0 / math.sqrt(lat_rows * tiles))


def solution(mesh):
    in_specs = (
        P("tile", "head"),
        P("tile"),
        P("tile", None),
        P("tile", None),
        P("tile", None),
        P(None, "head"),
        P(None, "head"),
        P(None, "head"),
        P("head"),
        P("head", None),
        P(),
        P(),
        P("tile", None),
    )
    out_specs = (P("tile", None), P("head", None))
    return jax.shard_map(body, mesh=mesh, in_specs=in_specs, out_specs=out_specs, check_vma=False)
```

```python
import functools
import math

import jax
import jax.numpy as jnp
from jax import lax
from jax.experimental import pallas as pl
from jax.experimental.pallas import tpu as pltpu
from jax.sharding import PartitionSpec as P

BF = jnp.bfloat16
F32 = jnp.float32
NEG = -1e30
SLOTS = 2
CHUNK = 8
PAIR = 8
DEPTH = 6
NEAR = (1, 16, 17, 48, 49, 2, 3, 32)


def route_kernel(spill, owner, alive, obs, row_marks, pattern, sent, info, lanes, extra, near):
    tiles = sent.shape[0]
    blocks, parts, quarter = obs.shape[:3]
    subs = pattern.shape[0]
    me = lax.axis_index("tile")
    lane = lax.broadcasted_iota(jnp.int32, (blocks, 128), 1)
    rows = row_marks[...].astype(F32)
    spot = lax.broadcasted_iota(jnp.int32, (subs, 128), 1)
    line = lax.broadcasted_iota(jnp.int32, (subs, 128), 0)
    shift = (spot == line + quarter).astype(F32).astype(BF)
    groups = lax.dot_general(
        pattern[...].astype(F32).astype(BF),
        shift,
        (((0,), (0,)), ((), ())),
        preferred_element_type=F32,
    )
    for j in range(parts):
        turned = rows if j == 0 else pltpu.roll(rows, 128 - j * quarter, 1)
        info[j, :blocks] = jnp.where(lane < quarter, turned, groups)
        info[j, blocks:] = jnp.zeros((8, 128), F32)
    for m, mask in enumerate(NEAR):
        near[m] = mask

    def clear(t, carry):
        lanes[t] = blocks
        lanes[tiles + t] = 0
        return carry

    lax.fori_loop(0, tiles, clear, 0, unroll=8)
    extra[blocks] = 0

    def place(b, carry):
        t = owner[b]

        @pl.when(alive[b] > 0)
        def _():
            seen = lanes[tiles + t]
            lanes[tiles + t] = 1
            take = (seen == 0) if spill else (seen > 0)

            @pl.when(take)
            def _():
                lanes[t] = b

            @pl.when(jnp.logical_not(take))
            def _():
                n = extra[blocks]
                extra[n] = b
                extra[blocks] = n + 1

        return carry

    lax.fori_loop(0, blocks, place, 0)
    left = jnp.int32(0)
    if spill:

        def move(q, left):
            b = extra[q]
            t = owner[b]
            found = jnp.int32(tiles)
            for a in range(len(NEAR)):
                other = t ^ near[(me + q + a) % len(NEAR)]
                free = (lanes[other] == blocks) & (found == tiles)
                found = jnp.where(free, other, found)

            @pl.when(found < tiles)
            def _():
                lanes[found] = b

            return left + (found == tiles).astype(jnp.int32)

        left = lax.fori_loop(0, extra[blocks], move, left)

    lane1 = lax.broadcasted_iota(jnp.int32, (1, 128), 1)

    def goal(t):
        b = lanes[t]
        return jnp.where(b < blocks, owner[jnp.minimum(b, blocks - 1)] + 1, 0)

    def note(t, table):
        return jnp.where(lane1 == t, goal(t).astype(F32), table)

    table = jnp.where(lane1 == tiles, left.astype(F32), jnp.zeros((1, 128), F32))
    table = lax.fori_loop(0, tiles, note, table)
    line8 = lax.broadcasted_iota(jnp.int32, (8, 128), 0)

    def fill(t, carry):
        b = lanes[t]
        to = jnp.where(lane1 == quarter + subs, goal(t).astype(F32), 0.0)
        for j in range(parts):
            one = info[j, pl.ds(b, 1), :] + to
            tail = jnp.where(line8 == 0, one, jnp.where(line8 == 1, table, 0.0))
            sent[t, j, quarter:, :] = tail.astype(BF)

        @pl.when(b < blocks)
        def _():
            sent[t, :, :quarter, :] = obs[b]

        @pl.when(b >= blocks)
        def _():
            sent[t, :, :quarter, :] = jnp.zeros(obs.shape[1:], BF)

        return carry

    lax.fori_loop(0, tiles, fill, 0)


def before(n):
    return (
        lax.broadcasted_iota(jnp.int32, (n, n), 0) < lax.broadcasted_iota(jnp.int32, (n, n), 1)
    ).astype(F32).astype(BF)


def listing(live):
    rows, n = live.shape
    place = jnp.dot(live.astype(BF), before(n), preferred_element_type=F32)
    turn = lax.broadcasted_iota(jnp.int32, (rows, 128, n), 1).astype(F32)
    name = lax.broadcasted_iota(jnp.int32, (rows, 128, n), 2).astype(F32)
    hit = (place[:, None, :] == turn) & (live[:, None, :] > 0.5)
    order = jnp.sum(jnp.where(hit, name, 0.0), axis=2)
    return order, jnp.sum(live, axis=1, keepdims=True)


def plan_kernel(arrived, plan):
    tiles = arrived.shape[0]
    near = len(NEAR)
    me = lax.axis_index("tile")
    table = arrived[:, 0, 32:40, :].astype(F32)[:, 1, :]
    mine = (lax.broadcasted_iota(jnp.int32, (near, 128), 1) == me).astype(F32).astype(BF)
    goals = lax.dot_general(
        mine, table.astype(BF), (((1,), (1,)), ((), ())), preferred_element_type=F32
    )
    line = lax.broadcasted_iota(jnp.int32, (near, tiles), 0)
    want = jnp.zeros((near, tiles), jnp.int32)
    for m, mask in enumerate(NEAR):
        want = jnp.where(line == m, (me ^ mask) + 1, want)
    order, count = listing((goals == want.astype(F32)).astype(F32))
    place = lax.broadcasted_iota(jnp.int32, (near, 128), 1)
    plan[:near] = jnp.where(place.astype(F32) < count, order, tiles).astype(jnp.int32)
    lane = lax.broadcasted_iota(jnp.int32, (1, 128), 1)
    worst = jnp.zeros((1, 128), F32)
    for mask in NEAR:
        here = (table == ((lane ^ mask) + 1).astype(F32)).astype(F32)
        total = jnp.sum(here, axis=0, keepdims=True)
        worst = jnp.maximum(worst, jnp.where(lane < tiles, total, 0.0))
    left = jnp.sum(jnp.where(lane == tiles, table, 0.0), axis=0, keepdims=True)
    bad = jnp.max(jnp.where(worst > DEPTH, 1.0, left), axis=1, keepdims=True)
    good = jnp.where(bad > 0.0, 0, 1)
    plan[near:] = jnp.broadcast_to(good, (near, 128))


def forward_kernel(plan, arrived, *outs):
    tiles = arrived.shape[0]
    for m, out in enumerate(outs):
        for c in range(DEPTH):
            s = plan[m, c]

            @pl.when(s < tiles)
            def _(s=s, out=out, c=c):
                out[c] = arrived[s]

            @pl.when(s >= tiles)
            def _(out=out, c=c):
                out[c] = jnp.zeros(out.shape[1:], BF)


def lists_kernel(*refs):
    *units, lists, bias, found = refs
    quarter = 32
    subs = lists.shape[0]
    at = 0
    for unit in units:
        n = unit.shape[0]
        found[at:at + n, :] = unit[:, 0, quarter:quarter + 8, :].astype(F32)[:, 0, :]
        at += n
    me = lax.axis_index("tile")
    marks = found[...]
    to = marks[:, quarter + subs:quarter + subs + 1]
    marks = jnp.where(to == (me + 1).astype(F32), marks, 0.0).astype(BF)
    pick_group = (
        lax.broadcasted_iota(jnp.int32, (subs, 128), 1)
        == lax.broadcasted_iota(jnp.int32, (subs, 128), 0) + quarter
    ).astype(F32).astype(BF)
    up = lax.broadcasted_iota(jnp.int32, (128, 128), 0)
    along = lax.broadcasted_iota(jnp.int32, (128, 128), 1)
    widen = ((up < quarter) & (up == along % quarter)).astype(F32).astype(BF)
    live = lax.dot_general(
        pick_group, marks, (((1,), (1,)), ((), ())), preferred_element_type=F32
    )
    order, count = listing(live)
    lists[:, :128] = order.astype(jnp.int32)
    lists[:, 128:] = jnp.broadcast_to(count, (subs, 128)).astype(jnp.int32)
    rows = jnp.dot(marks, widen, preferred_element_type=F32)
    bias[...] = (rows - 1.0) * (-NEG)


def split3(v):
    hi = v.astype(BF).astype(F32)
    mid = (v - hi).astype(BF).astype(F32)
    return hi, mid, v - hi - mid


def attend_kernel(lists, *refs):
    units = refs[:len(NEAR) + 2]
    bias, qw, begun, given, wv, out, x, sems, *scratch = refs[len(NEAR) + 2:]
    step_id = pl.program_id(0)

    @pl.when(step_id == 0)
    def _():
        copies = []
        at = 0
        for u, unit in enumerate(units):
            n = unit.shape[0]
            copies.append(pltpu.make_async_copy(unit, x.at[pl.ds(at, n)], sems.at[u]))
            at += n
        for copy in copies:
            copy.start()
        for copy in copies:
            copy.wait()

    heads, both, width = qw.shape
    sub = both // PAIR
    rows = heads * sub
    quarter = 32
    parts, _, cols = x.shape[1:]
    size = CHUNK * quarter
    per = 128 // quarter
    lane_slot = lax.broadcasted_iota(jnp.int32, (1, 128), 1) // quarter
    lane = lax.broadcasted_iota(jnp.int32, (sub, 128), 1)
    xbufs, accs, tops, dens = (scratch[q * PAIR:(q + 1) * PAIR] for q in range(4))

    def gather(g, n, c, xbuf):
        shades = []
        for part in range(CHUNK // per):
            shade = jnp.full((1, 128), NEG, F32)
            for v in range(per):
                u = part * per + v
                place = c * CHUNK + u
                s = lists[g, jnp.maximum(jnp.minimum(place, n - 1), 0)]
                for i in range(parts):
                    xbuf[u * quarter:(u + 1) * quarter, i * cols:(i + 1) * cols] = x[
                        s, i, :quarter, :
                    ]
                live = (lane_slot == v) & (place < n)
                shade = jnp.where(live, bias[pl.ds(s, 1), :], shade)
            shades.append(shade)
        return xbuf[...], jnp.concatenate(shades, axis=1)

    def chunk(queries, rows_x, shade, old):
        scores = lax.dot_general(
            queries, rows_x, (((1,), (1,)), ((), ())), preferred_element_type=F32
        ) + shade
        new = jnp.maximum(old, jnp.max(scores, axis=1, keepdims=True))
        weights = jnp.exp(scores - jnp.concatenate([new] * (size // 128), axis=1))
        total = jnp.sum(weights, axis=1, keepdims=True)
        more = jnp.dot(weights.astype(BF), rows_x, preferred_element_type=F32)
        return new, jnp.exp(old - new), total, more

    counts, begins = [], []
    for p in range(PAIR):
        g = step_id * PAIR + p
        n = lists[g, 128]
        counts.append(n)
        start = begun[p * sub:(p + 1) * sub, :]
        old = jnp.concatenate(
            [jnp.broadcast_to(start[:, h:h + 1], (sub, 128)) for h in range(heads)], axis=0
        )
        den = jnp.concatenate(
            [
                jnp.broadcast_to(start[:, heads + h:heads + h + 1], (sub, 128))
                for h in range(heads)
            ],
            axis=0,
        )
        begins.append(old)
        rows_x, shade = gather(g, n, 0, xbufs[p])
        queries = qw[:, p * sub:(p + 1) * sub, :].reshape(rows, width)
        new, shrink, total, more = chunk(queries, rows_x, shade, old)
        accs[p][...] = more
        tops[p][...] = new
        dens[p][...] = den * shrink + total

    for p in range(PAIR):
        g = step_id * PAIR + p

        @pl.when(counts[p] > CHUNK)
        def _(p=p, g=g):
            def again(c, carry):
                rows_x, shade = gather(g, counts[p], c, xbufs[p])
                queries = qw[:, p * sub:(p + 1) * sub, :].reshape(rows, width)
                new, shrink, total, more = chunk(queries, rows_x, shade, tops[p][...])
                tops[p][...] = new
                dens[p][...] = dens[p][...] * shrink + total
                wide = jnp.concatenate([shrink] * (width // 128), axis=1)
                accs[p][...] = accs[p][...] * wide + more
                return carry

            lax.fori_loop(1, (counts[p] + CHUNK - 1) // CHUNK, again, 0)

    half = width // 2
    for p in range(PAIR):
        place = slice(p * sub, (p + 1) * sub)
        top = tops[p][...]
        shrink = jnp.exp(begins[p] - top)
        state = jnp.zeros((sub, 128), F32)
        for h in range(heads):
            line = slice(h * sub, (h + 1) * sub)
            state = jnp.where(lane == h, top[line], state)
            state = jnp.where(lane == heads + h, dens[p][line, :], state)
        hi, mid, lo = split3(state)
        packed = hi + pltpu.roll(mid, 2 * heads, 1) + pltpu.roll(lo, 4 * heads, 1)
        out[place, width:] = packed.astype(BF)
        for side in range(2):
            here = slice(side * rows // 2, (side + 1) * rows // 2)
            mixed = jnp.dot(
                accs[p][here, :].astype(BF),
                wv[:, side * half:(side + 1) * half],
                preferred_element_type=F32,
            )
            for c in range(half // 128):
                col = side * half + c * 128
                two = []
                for h in (2 * c, 2 * c + 1):
                    line = slice(h * sub, (h + 1) * sub)
                    far = side * rows // 2
                    two.append(
                        given[place, col:col + 128] * shrink[far + h * sub:far + (h + 1) * sub]
                        + mixed[line, c * 128:(c + 1) * 128]
                    )
                out[place, col:col + 128] = jnp.where(
                    lane < width // heads, two[0], two[1]
                ).astype(BF)


def combine_kernel(r0, r1, r2, r3, out):
    width = out.shape[1]
    heads = 8
    line = lax.broadcasted_iota(jnp.int32, (128, 2 * width), 0)
    col = lax.broadcasted_iota(jnp.int32, (128, 2 * width), 1)
    match = (
        (line % heads == (col % width) // (width // heads))
        & ((line // heads) % 2 == col // width)
        & (line < 6 * heads)
    )
    spread = match.astype(F32).astype(BF)
    tops, dens, nums = [], [], []
    for r in (r0, r1, r2, r3):
        wide = jnp.dot(r[:, width:], spread, preferred_element_type=F32)
        tops.append(wide[:, :width])
        dens.append(wide[:, width:])
        nums.append(r[:, :width].astype(F32))
    best = jnp.maximum(jnp.maximum(tops[0], tops[1]), jnp.maximum(tops[2], tops[3]))
    scale = [jnp.exp(v - best) for v in tops]
    numer = sum(a * b for a, b in zip(scale, nums))
    denom = sum(a * b for a, b in zip(scale, dens))
    out[...] = (numer / denom).astype(BF)


def finish_kernel(place, a0, a1, a2, a3, lat, w_out, gain, w_inc, target, predicted, grad, cut):
    me = place[0]
    share, width = a0.shape
    dims = (((0,), (0,)), ((), ()))
    total = jnp.zeros(grad.shape, F32)
    for d, a in enumerate((a0, a1, a2, a3)):
        here = pl.ds(pl.multiple_of((me ^ d) * share, share), share)
        updated = lat[here, :].astype(F32) + jnp.dot(
            a[...], w_out[...], preferred_element_type=F32
        )
        power = jnp.mean(updated * updated, axis=1, keepdims=True)
        normed = (updated * lax.rsqrt(power + 1e-6) * gain[...]).astype(BF)
        answer = jnp.dot(normed, w_inc[...], preferred_element_type=F32)
        predicted[here, :] = answer
        residual = answer - target[here, :].astype(F32)
        high = residual.astype(BF)
        low = (residual - high.astype(F32)).astype(BF)
        for c in range(width // 128):
            cut[d, c] = normed[:, c * 128:(c + 1) * 128]
        mine = cut[d, me]
        total = total + lax.dot_general(mine, high, dims, preferred_element_type=F32)
        total = total + lax.dot_general(mine, low, dims, preferred_element_type=F32)
    grad[...] = total


def body(
    obs_feat,
    row_valid,
    block_owner,
    block_pattern,
    latent,
    w_query,
    w_key,
    w_value,
    self_bias,
    w_out,
    norm_gain,
    w_inc,
    target,
):
    tiles = lax.axis_size("tile")
    groups = lax.axis_size("head")
    me = lax.axis_index("head")
    blocks = block_owner.shape[0]
    block_rows = obs_feat.shape[0] // blocks
    quarter = block_rows // groups
    cols = obs_feat.shape[1]
    lat_rows, width = latent.shape
    subs = block_pattern.shape[1]
    sub = lat_rows // subs
    local_heads = self_bias.shape[0]
    heads = local_heads * groups
    head_size = width // heads
    share = lat_rows // groups

    def swap(v, axis, mask, size):
        return lax.ppermute(v, axis, [(d, d ^ mask) for d in range(size)])

    def pick(v, which):
        return lax.dynamic_index_in_dim(v, which, 0, keepdims=False)

    tile = lax.axis_index("tile")
    whole = lambda *shape: pl.BlockSpec(shape, lambda g, *_: (0,) * len(shape))
    depth = quarter + 8
    alive = jnp.max(block_pattern.T, axis=0)

    def route(spill):
        sent = pl.pallas_call(
            functools.partial(route_kernel, spill),
            grid_spec=pltpu.PrefetchScalarGridSpec(
                num_scalar_prefetch=2,
                grid=(1,),
                in_specs=[
                    whole(blocks, groups, quarter, cols),
                    whole(blocks, block_rows),
                    whole(subs, blocks),
                ],
                out_specs=whole(tiles, groups, depth, cols),
                scratch_shapes=[
                    pltpu.VMEM((groups, blocks + 8, 128), F32),
                    pltpu.SMEM((2 * tiles,), jnp.int32),
                    pltpu.SMEM((blocks + 1,), jnp.int32),
                    pltpu.SMEM((len(NEAR),), jnp.int32),
                ],
            ),
            out_shape=jax.ShapeDtypeStruct((tiles, groups, depth, cols), BF),
            compiler_params=pltpu.CompilerParams(vmem_limit_bytes=32 * 1024 * 1024),
            name="route",
        )(
            block_owner[:, 0],
            alive,
            obs_feat.reshape(blocks, groups, quarter, cols),
            row_valid.reshape(blocks, block_rows),
            block_pattern.T,
        )
        return lax.all_to_all(
            sent.reshape(tiles * groups, depth, cols),
            ("tile", "head"),
            split_axis=0,
            concat_axis=0,
            tiled=True,
        ).reshape(tiles, groups, depth, cols)

    arrived = route(True)
    near = len(NEAR)
    marks_of = lambda n: pl.BlockSpec((n, 1, depth, cols), lambda g, *_: (0, 0, 0, 0))
    plan = pl.pallas_call(
        plan_kernel,
        grid=(1,),
        in_specs=[marks_of(tiles)],
        out_specs=whole(2 * near, 128),
        out_shape=jax.ShapeDtypeStruct((2 * near, 128), jnp.int32),
        name="plan",
    )(arrived)
    rest = tiles - near * DEPTH

    def forward():
        held = pl.pallas_call(
            forward_kernel,
            grid_spec=pltpu.PrefetchScalarGridSpec(
                num_scalar_prefetch=1,
                grid=(1,),
                in_specs=[whole(tiles, groups, depth, cols)],
                out_specs=[whole(DEPTH, groups, depth, cols)] * near,
            ),
            out_shape=[jax.ShapeDtypeStruct((DEPTH, groups, depth, cols), BF)] * near,
            compiler_params=pltpu.CompilerParams(vmem_limit_bytes=32 * 1024 * 1024),
            name="forward",
        )(plan, arrived)
        moved = [swap(v, "tile", m, tiles) for m, v in zip(NEAR, held)]
        return *moved, jnp.zeros((rest, groups, depth, cols), BF)

    def again():
        second = route(False)
        return *[second[m * DEPTH:(m + 1) * DEPTH] for m in range(near)], second[-rest:]

    units = (arrived, *lax.cond(plan[near, 0] > 0, forward, again))
    lists, bias = pl.pallas_call(
        lists_kernel,
        grid=(1,),
        in_specs=[marks_of(u.shape[0]) for u in units],
        out_specs=[whole(subs, 256), whole(SLOTS * tiles, 128)],
        out_shape=[
            jax.ShapeDtypeStruct((subs, 256), jnp.int32),
            jax.ShapeDtypeStruct((SLOTS * tiles, 128), F32),
        ],
        scratch_shapes=[pltpu.VMEM((SLOTS * tiles, 128), F32)],
        name="lists",
    )(*units)

    stacked = jnp.concatenate([w_query, w_key, w_value, w_out.T], axis=1)
    near = jnp.stack(
        [stacked] + [swap(stacked, "head", d, groups) for d in range(1, groups)]
    )
    turn = jnp.arange(groups, dtype=jnp.int32) ^ me
    stacked = jnp.take(near, turn, axis=0)
    wq, wk, wv, wo = [
        stacked[:, :, a * 128:(a + 1) * 128].transpose(1, 0, 2).reshape(width, width)
        for a in range(4)
    ]
    wo = wo.T
    by_distance = jnp.stack(
        [self_bias] + [swap(self_bias, "head", d, groups) for d in range(1, groups)]
    )
    turn = jnp.arange(groups, dtype=jnp.int32) ^ me
    bias_all = jnp.take(by_distance, turn, axis=0).reshape(heads)
    queries = jnp.dot(latent, wq, preferred_element_type=F32).astype(BF)
    own_key = jnp.dot(latent, wk, preferred_element_type=F32).astype(BF)
    q3 = queries.reshape(lat_rows, heads, head_size)
    k3 = wk.reshape(width, heads, head_size)
    scale = 1.0 / math.sqrt(head_size)
    qw = (
        jnp.einsum("lhd,khd->hlk", q3, k3, preferred_element_type=F32) * scale
    ).astype(BF)
    own = (
        jnp.sum(
            q3.astype(F32) * own_key.reshape(lat_rows, heads, head_size).astype(F32), axis=-1
        )
        * scale
        + bias_all[None, :]
    )
    keep = (me == 0).astype(F32)
    states = jnp.pad(
        jnp.concatenate([own, jnp.full((lat_rows, heads), keep)], axis=1),
        ((0, 0), (0, 128 - 2 * heads)),
    )
    numer = jnp.dot(latent, wv, preferred_element_type=F32) * keep

    block = PAIR * sub
    scratch = [
        pltpu.VMEM((SLOTS * tiles, groups, depth, cols), BF),
        pltpu.SemaphoreType.DMA((len(units),)),
    ] + [
        shape
        for shape in (
            pltpu.VMEM((CHUNK * quarter, width), BF),
            pltpu.VMEM((heads * sub, width), F32),
            pltpu.VMEM((heads * sub, 128), F32),
            pltpu.VMEM((heads * sub, 128), F32),
        )
        for _ in range(PAIR)
    ]
    partial = pl.pallas_call(
        attend_kernel,
        grid_spec=pltpu.PrefetchScalarGridSpec(
            num_scalar_prefetch=1,
            grid=(subs // PAIR,),
            in_specs=[pl.BlockSpec(memory_space=pl.ANY)] * len(units)
            + [
                whole(SLOTS * tiles, 128),
                pl.BlockSpec((heads, block, width), lambda g, *_: (0, g, 0)),
                pl.BlockSpec((block, 128), lambda g, *_: (g, 0)),
                pl.BlockSpec((block, width), lambda g, *_: (g, 0)),
                whole(width, width),
            ],
            out_specs=pl.BlockSpec((block, width + 128), lambda g, *_: (g, 0)),
            scratch_shapes=scratch,
        ),
        out_shape=jax.ShapeDtypeStruct((lat_rows, width + 128), BF),
        compiler_params=pltpu.CompilerParams(vmem_limit_bytes=40 * 1024 * 1024),
        name="attend",
    )(lists, *units, bias, qw, states, numer, wv)

    partial = partial.reshape(groups, share, width + 128)
    received = [pick(partial, me)] + [
        swap(pick(partial, me ^ d), "head", d, groups) for d in range(1, groups)
    ]
    attended = pl.pallas_call(
        combine_kernel,
        grid=(1,),
        in_specs=[whole(share, width + 128)] * groups,
        out_specs=whole(share, width),
        out_shape=jax.ShapeDtypeStruct((share, width), BF),
        name="combine",
    )(*received)
    gathered = [attended] + [swap(attended, "head", d, groups) for d in range(1, groups)]
    predicted, grad = pl.pallas_call(
        finish_kernel,
        grid_spec=pltpu.PrefetchScalarGridSpec(
            num_scalar_prefetch=1,
            grid=(1,),
            in_specs=[whole(share, width)] * groups
            + [
                whole(lat_rows, width),
                whole(width, width),
                whole(1, width),
                whole(width, 128),
                whole(lat_rows, 128),
            ],
            out_specs=[whole(lat_rows, 128), whole(cols, 128)],
            scratch_shapes=[pltpu.VMEM((groups, width // 128, share, 128), BF)],
        ),
        out_shape=[
            jax.ShapeDtypeStruct((lat_rows, 128), F32),
            jax.ShapeDtypeStruct((cols, 128), F32),
        ],
        compiler_params=pltpu.CompilerParams(vmem_limit_bytes=32 * 1024 * 1024),
        name="finish",
    )(
        me[None].astype(jnp.int32),
        *gathered,
        latent,
        wo,
        norm_gain[None, :],
        w_inc,
        target,
    )
    for low, high in ((1, 2), (4, 8), (16, 32)):
        a, b, c = (swap(grad, "tile", m, tiles) for m in (low, high, low + high))
        grad = (grad + a) + (b + c)
    return predicted, grad * (1.0 / math.sqrt(lat_rows * tiles))


def solution(mesh):
    in_specs = (
        P("tile", "head"),
        P("tile"),
        P("tile", None),
        P("tile", None),
        P("tile", None),
        P(None, "head"),
        P(None, "head"),
        P(None, "head"),
        P("head"),
        P("head", None),
        P(),
        P(),
        P("tile", None),
    )
    out_specs = (P("tile", None), P("head", None))
    return jax.shard_map(body, mesh=mesh, in_specs=in_specs, out_specs=out_specs, check_vma=False)
```

```python
import functools
import math

import jax
import jax.numpy as jnp
from jax import lax
from jax.experimental import pallas as pl
from jax.experimental.pallas import tpu as pltpu
from jax.sharding import PartitionSpec as P

BF = jnp.bfloat16
F32 = jnp.float32
NEG = -1e30
SLOTS = 2
CHUNK = 8
PAIR = 8
NEAR = (1, 16, 17, 48, 49, 2, 3, 32)
DEPTHS = (6, 6, 6, 6, 6, 6, 6, 2)


def route_kernel(spill, owner, alive, obs, row_marks, pattern, sent, info, lanes, extra, near):
    tiles = sent.shape[0]
    blocks, parts, quarter = obs.shape[:3]
    subs = pattern.shape[0]
    me = lax.axis_index("tile")
    lane = lax.broadcasted_iota(jnp.int32, (blocks, 128), 1)
    rows = row_marks[...].astype(F32)
    spot = lax.broadcasted_iota(jnp.int32, (subs, 128), 1)
    line = lax.broadcasted_iota(jnp.int32, (subs, 128), 0)
    shift = (spot == line + quarter).astype(F32).astype(BF)
    groups = lax.dot_general(
        pattern[...].astype(F32).astype(BF),
        shift,
        (((0,), (0,)), ((), ())),
        preferred_element_type=F32,
    )
    for j in range(parts):
        turned = rows if j == 0 else pltpu.roll(rows, 128 - j * quarter, 1)
        info[j, :blocks] = jnp.where(lane < quarter, turned, groups)
        info[j, blocks:] = jnp.zeros((8, 128), F32)
    for m, mask in enumerate(NEAR):
        near[m] = mask

    def clear(t, carry):
        lanes[t] = blocks
        lanes[tiles + t] = 0
        return carry

    lax.fori_loop(0, tiles, clear, 0, unroll=8)

    def place(b, n):
        t = owner[b]
        live = alive[b]
        seen = lanes[tiles + t]
        take = (live > 0) & ((seen == 0) if spill else (seen > 0))
        lanes[t] = jnp.where(take, b, lanes[t])
        lanes[tiles + t] = seen | live
        extra[n] = b
        return n + (live & seen)

    more = lax.fori_loop(0, blocks, place, jnp.int32(0), unroll=4)
    left = jnp.int32(0)
    if spill:

        def move(q, left):
            b = extra[q]
            t = owner[b]
            found = jnp.int32(tiles)
            last = len(NEAR) - 1
            for a in range(len(NEAR)):
                other = t ^ (NEAR[last] if a == last else near[(me + q + a) % last])
                free = (lanes[other] == blocks) & (found == tiles)
                found = jnp.where(free, other, found)

            @pl.when(found < tiles)
            def _():
                lanes[found] = b

            return left + (found == tiles).astype(jnp.int32)

        left = lax.fori_loop(0, more, move, left)

    lane1 = lax.broadcasted_iota(jnp.int32, (1, 128), 1)

    def goal(t):
        b = lanes[t]
        return jnp.where(b < blocks, owner[jnp.minimum(b, blocks - 1)] + 1, 0)

    def note(t, table):
        return jnp.where(lane1 == t, goal(t).astype(F32), table)

    table = jnp.where(lane1 == tiles, left.astype(F32), jnp.zeros((1, 128), F32))
    table = lax.fori_loop(0, tiles, note, table, unroll=8)
    line8 = lax.broadcasted_iota(jnp.int32, (8, 128), 0)

    def fill(t, carry):
        b = lanes[t]
        to = jnp.where(lane1 == quarter + subs, goal(t).astype(F32), 0.0)
        for j in range(parts):
            one = info[j, pl.ds(b, 1), :] + to
            tail = jnp.where(line8 == 0, one, jnp.where(line8 == 1, table, 0.0))
            sent[t, j, quarter:, :] = tail.astype(BF)

        @pl.when(b < blocks)
        def _():
            sent[t, :, :quarter, :] = obs[b]

        @pl.when(b >= blocks)
        def _():
            sent[t, :, :quarter, :] = jnp.zeros(obs.shape[1:], BF)

        return carry

    lax.fori_loop(0, tiles, fill, 0, unroll=2)


def before(n):
    return (
        lax.broadcasted_iota(jnp.int32, (n, n), 0) < lax.broadcasted_iota(jnp.int32, (n, n), 1)
    ).astype(F32).astype(BF)


def listing(live):
    rows, n = live.shape
    place = jnp.dot(live.astype(BF), before(n), preferred_element_type=F32)
    turn = lax.broadcasted_iota(jnp.int32, (rows, 128, n), 1).astype(F32)
    name = lax.broadcasted_iota(jnp.int32, (rows, 128, n), 2).astype(F32)
    hit = (place[:, None, :] == turn) & (live[:, None, :] > 0.5)
    order = jnp.sum(jnp.where(hit, name, 0.0), axis=2)
    return order, jnp.sum(live, axis=1, keepdims=True)


def plan_kernel(arrived, plan):
    tiles = arrived.shape[0]
    near = len(NEAR)
    me = lax.axis_index("tile")
    table = arrived[:, 0, 32:40, :].astype(F32)[:, 1, :]
    mine = (lax.broadcasted_iota(jnp.int32, (near, 128), 1) == me).astype(F32).astype(BF)
    goals = lax.dot_general(
        mine, table.astype(BF), (((1,), (1,)), ((), ())), preferred_element_type=F32
    )
    line = lax.broadcasted_iota(jnp.int32, (near, tiles), 0)
    want = jnp.zeros((near, tiles), jnp.int32)
    for m, mask in enumerate(NEAR):
        want = jnp.where(line == m, (me ^ mask) + 1, want)
    order, count = listing((goals == want.astype(F32)).astype(F32))
    place = lax.broadcasted_iota(jnp.int32, (near, 128), 1)
    plan[:near] = jnp.where(place.astype(F32) < count, order, tiles).astype(jnp.int32)
    lane = lax.broadcasted_iota(jnp.int32, (1, 128), 1)
    worst = jnp.zeros((1, 128), F32)
    for mask, depth in zip(NEAR, DEPTHS):
        here = (table == ((lane ^ mask) + 1).astype(F32)).astype(F32)
        total = jnp.sum(here, axis=0, keepdims=True)
        worst = jnp.maximum(worst, jnp.where(lane < tiles, total - depth, 0.0))
    left = jnp.sum(jnp.where(lane == tiles, table, 0.0), axis=0, keepdims=True)
    bad = jnp.max(jnp.where(worst > 0.0, 1.0, left), axis=1, keepdims=True)
    good = jnp.where(bad > 0.0, 0, 1)
    plan[near:] = jnp.broadcast_to(good, (near, 128))


def forward_kernel(plan, arrived, *outs):
    tiles = arrived.shape[0]
    for m, out in enumerate(outs):
        for c in range(DEPTHS[m]):
            s = plan[m, c]

            @pl.when(s < tiles)
            def _(s=s, out=out, c=c):
                out[c] = arrived[s]

            @pl.when(s >= tiles)
            def _(out=out, c=c):
                out[c] = jnp.zeros(out.shape[1:], BF)


def lists_of(marks, quarter, subs):
    me = lax.axis_index("tile")
    to = marks[:, quarter + subs:quarter + subs + 1]
    marks = jnp.where(to == (me + 1).astype(F32), marks, 0.0).astype(BF)
    pick_group = (
        lax.broadcasted_iota(jnp.int32, (subs, 128), 1)
        == lax.broadcasted_iota(jnp.int32, (subs, 128), 0) + quarter
    ).astype(F32).astype(BF)
    up = lax.broadcasted_iota(jnp.int32, (128, 128), 0)
    along = lax.broadcasted_iota(jnp.int32, (128, 128), 1)
    widen = ((up < quarter) & (up == along % quarter)).astype(F32).astype(BF)
    live = lax.dot_general(
        pick_group, marks, (((1,), (1,)), ((), ())), preferred_element_type=F32
    )
    order, count = listing(live)
    rows = jnp.dot(marks, widen, preferred_element_type=F32)
    return order, count, (rows - 1.0) * (-NEG)


def split3(v):
    hi = v.astype(BF).astype(F32)
    mid = (v - hi).astype(BF).astype(F32)
    return hi, mid, v - hi - mid


def attend_kernel(*refs):
    units = refs[:len(NEAR) + 2]
    qw, begun, given, wv, out, x, sems, made, lists, bias, *scratch = refs[len(NEAR) + 2:]
    step_id = pl.program_id(0)
    quarter = 32

    @pl.when(step_id == 0)
    def _():
        copies = []
        at = 0
        for u, unit in enumerate(units):
            n = unit.shape[0]
            copies.append(pltpu.make_async_copy(unit, x.at[pl.ds(at, n)], sems.at[u]))
            at += n
        for copy in copies:
            copy.start()
        for copy in copies:
            copy.wait()
        marks = x[:, 0, quarter:quarter + 8, :].astype(F32)[:, 0, :]
        order, count, shade = lists_of(marks, quarter, made.shape[0])
        bias[...] = shade
        made[:, :128] = order.astype(jnp.int32)
        made[:, 128:] = jnp.broadcast_to(count, order.shape).astype(jnp.int32)
        copy = pltpu.make_async_copy(made, lists, sems.at[len(units)])
        copy.start()
        copy.wait()

    heads, both, width = qw.shape
    sub = both // PAIR
    rows = heads * sub
    parts, _, cols = x.shape[1:]
    size = CHUNK * quarter
    per = 128 // quarter
    lane_slot = lax.broadcasted_iota(jnp.int32, (1, 128), 1) // quarter
    lane = lax.broadcasted_iota(jnp.int32, (sub, 128), 1)
    xbufs, accs, tops, dens = (scratch[q * PAIR:(q + 1) * PAIR] for q in range(4))

    def gather(g, n, c, xbuf):
        shades = []
        for part in range(CHUNK // per):
            shade = jnp.full((1, 128), NEG, F32)
            for v in range(per):
                u = part * per + v
                place = c * CHUNK + u
                s = lists[g, jnp.maximum(jnp.minimum(place, n - 1), 0)]
                for i in range(parts):
                    xbuf[u * quarter:(u + 1) * quarter, i * cols:(i + 1) * cols] = x[
                        s, i, :quarter, :
                    ]
                live = (lane_slot == v) & (place < n)
                shade = jnp.where(live, bias[pl.ds(s, 1), :], shade)
            shades.append(shade)
        return xbuf[...], jnp.concatenate(shades, axis=1)

    def chunk(queries, rows_x, shade, old):
        scores = lax.dot_general(
            queries, rows_x, (((1,), (1,)), ((), ())), preferred_element_type=F32
        ) + shade
        new = jnp.maximum(old, jnp.max(scores, axis=1, keepdims=True))
        weights = jnp.exp(scores - jnp.concatenate([new] * (size // 128), axis=1))
        total = jnp.sum(weights, axis=1, keepdims=True)
        more = jnp.dot(weights.astype(BF), rows_x, preferred_element_type=F32)
        return new, jnp.exp(old - new), total, more

    counts, begins = [], []
    for p in range(PAIR):
        g = step_id * PAIR + p
        n = lists[g, 128]
        counts.append(n)
        start = begun[p * sub:(p + 1) * sub, :]
        old = jnp.concatenate(
            [jnp.broadcast_to(start[:, h:h + 1], (sub, 128)) for h in range(heads)], axis=0
        )
        den = jnp.concatenate(
            [
                jnp.broadcast_to(start[:, heads + h:heads + h + 1], (sub, 128))
                for h in range(heads)
            ],
            axis=0,
        )
        begins.append(old)
        rows_x, shade = gather(g, n, 0, xbufs[p])
        queries = qw[:, p * sub:(p + 1) * sub, :].reshape(rows, width)
        new, shrink, total, more = chunk(queries, rows_x, shade, old)
        accs[p][...] = more
        tops[p][...] = new
        dens[p][...] = den * shrink + total

    for p in range(PAIR):
        g = step_id * PAIR + p

        @pl.when(counts[p] > CHUNK)
        def _(p=p, g=g):
            def again(c, carry):
                rows_x, shade = gather(g, counts[p], c, xbufs[p])
                queries = qw[:, p * sub:(p + 1) * sub, :].reshape(rows, width)
                new, shrink, total, more = chunk(queries, rows_x, shade, tops[p][...])
                tops[p][...] = new
                dens[p][...] = dens[p][...] * shrink + total
                wide = jnp.concatenate([shrink] * (width // 128), axis=1)
                accs[p][...] = accs[p][...] * wide + more
                return carry

            lax.fori_loop(1, (counts[p] + CHUNK - 1) // CHUNK, again, 0)

    half = width // 2
    for p in range(PAIR):
        place = slice(p * sub, (p + 1) * sub)
        top = tops[p][...]
        shrink = jnp.exp(begins[p] - top)
        state = jnp.zeros((sub, 128), F32)
        for h in range(heads):
            line = slice(h * sub, (h + 1) * sub)
            state = jnp.where(lane == h, top[line], state)
            state = jnp.where(lane == heads + h, dens[p][line, :], state)
        hi, mid, lo = split3(state)
        packed = hi + pltpu.roll(mid, 2 * heads, 1) + pltpu.roll(lo, 4 * heads, 1)
        out[place, width:] = packed.astype(BF)
        for side in range(2):
            here = slice(side * rows // 2, (side + 1) * rows // 2)
            mixed = jnp.dot(
                accs[p][here, :].astype(BF),
                wv[:, side * half:(side + 1) * half],
                preferred_element_type=F32,
            )
            for c in range(half // 128):
                col = side * half + c * 128
                two = []
                for h in (2 * c, 2 * c + 1):
                    line = slice(h * sub, (h + 1) * sub)
                    far = side * rows // 2
                    two.append(
                        given[place, col:col + 128] * shrink[far + h * sub:far + (h + 1) * sub]
                        + mixed[line, c * 128:(c + 1) * 128]
                    )
                out[place, col:col + 128] = jnp.where(
                    lane < width // heads, two[0], two[1]
                ).astype(BF)


def finish_kernel(place, r0, r1, r2, r3, lat, w_out, gain, w_inc, target, predicted, grad):
    width = lat.shape[1]
    heads = 8
    line = lax.broadcasted_iota(jnp.int32, (128, 2 * width), 0)
    col = lax.broadcasted_iota(jnp.int32, (128, 2 * width), 1)
    match = (
        (line % heads == (col % width) // (width // heads))
        & ((line // heads) % 2 == col // width)
        & (line < 6 * heads)
    )
    spread = match.astype(F32).astype(BF)
    tops, dens, nums = [], [], []
    for r in (r0, r1, r2, r3):
        wide = jnp.dot(r[:, width:], spread, preferred_element_type=F32)
        tops.append(wide[:, :width])
        dens.append(wide[:, width:])
        nums.append(r[:, :width].astype(F32))
    best = jnp.maximum(jnp.maximum(tops[0], tops[1]), jnp.maximum(tops[2], tops[3]))
    scale = [jnp.exp(v - best) for v in tops]
    numer = sum(a * b for a, b in zip(scale, nums))
    denom = sum(a * b for a, b in zip(scale, dens))
    attended = (numer / denom).astype(BF)
    updated = lat[...].astype(F32) + jnp.dot(attended, w_out[...], preferred_element_type=F32)
    power = jnp.mean(updated * updated, axis=1, keepdims=True)
    normed = (updated * lax.rsqrt(power + 1e-6) * gain[...]).astype(BF)
    answer = jnp.dot(normed, w_inc[...], preferred_element_type=F32)
    predicted[...] = answer
    residual = answer - target[...].astype(F32)
    high = residual.astype(BF)
    low = (residual - high.astype(F32)).astype(BF)
    dims = (((0,), (0,)), ((), ()))
    total = lax.dot_general(normed, high, dims, preferred_element_type=F32)
    total = total + lax.dot_general(normed, low, dims, preferred_element_type=F32)
    size = width // grad.shape[0]
    for d in range(grad.shape[0]):
        grad[d] = total[d * size:(d + 1) * size]


def body(
    obs_feat,
    row_valid,
    block_owner,
    block_pattern,
    latent,
    w_query,
    w_key,
    w_value,
    self_bias,
    w_out,
    norm_gain,
    w_inc,
    target,
):
    tiles = lax.axis_size("tile")
    groups = lax.axis_size("head")
    me = lax.axis_index("head")
    blocks = block_owner.shape[0]
    block_rows = obs_feat.shape[0] // blocks
    quarter = block_rows // groups
    cols = obs_feat.shape[1]
    lat_rows, width = latent.shape
    subs = block_pattern.shape[1]
    sub = lat_rows // subs
    local_heads = self_bias.shape[0]
    heads = local_heads * groups
    head_size = width // heads
    share = lat_rows // groups

    def swap(v, axis, mask, size):
        return lax.ppermute(v, axis, [(d, d ^ mask) for d in range(size)])

    def pick(v, which):
        return lax.dynamic_index_in_dim(v, which, 0, keepdims=False)

    tile = lax.axis_index("tile")
    whole = lambda *shape: pl.BlockSpec(shape, lambda g, *_: (0,) * len(shape))
    depth = quarter + 8
    alive = jnp.max(block_pattern.T, axis=0)

    def route(spill):
        sent = pl.pallas_call(
            functools.partial(route_kernel, spill),
            grid_spec=pltpu.PrefetchScalarGridSpec(
                num_scalar_prefetch=2,
                grid=(1,),
                in_specs=[
                    whole(blocks, groups, quarter, cols),
                    whole(blocks, block_rows),
                    whole(subs, blocks),
                ],
                out_specs=whole(tiles, groups, depth, cols),
                scratch_shapes=[
                    pltpu.VMEM((groups, blocks + 8, 128), F32),
                    pltpu.SMEM((2 * tiles,), jnp.int32),
                    pltpu.SMEM((blocks + 8,), jnp.int32),
                    pltpu.SMEM((len(NEAR),), jnp.int32),
                ],
            ),
            out_shape=jax.ShapeDtypeStruct((tiles, groups, depth, cols), BF),
            compiler_params=pltpu.CompilerParams(vmem_limit_bytes=32 * 1024 * 1024),
            name="route",
        )(
            block_owner[:, 0],
            alive,
            obs_feat.reshape(blocks, groups, quarter, cols),
            row_valid.reshape(blocks, block_rows),
            block_pattern.T,
        )
        return lax.all_to_all(
            sent.reshape(tiles * groups, depth, cols),
            ("tile", "head"),
            split_axis=0,
            concat_axis=0,
            tiled=True,
        ).reshape(tiles, groups, depth, cols)

    arrived = route(True)
    near = len(NEAR)
    marks_of = lambda n: pl.BlockSpec((n, 1, depth, cols), lambda g, *_: (0, 0, 0, 0))
    plan = pl.pallas_call(
        plan_kernel,
        grid=(1,),
        in_specs=[marks_of(tiles)],
        out_specs=whole(2 * near, 128),
        out_shape=jax.ShapeDtypeStruct((2 * near, 128), jnp.int32),
        name="plan",
    )(arrived)
    rest = tiles - sum(DEPTHS)
    starts = [sum(DEPTHS[:m]) for m in range(near)]

    def forward():
        held = pl.pallas_call(
            forward_kernel,
            grid_spec=pltpu.PrefetchScalarGridSpec(
                num_scalar_prefetch=1,
                grid=(1,),
                in_specs=[whole(tiles, groups, depth, cols)],
                out_specs=[whole(n, groups, depth, cols) for n in DEPTHS],
            ),
            out_shape=[jax.ShapeDtypeStruct((n, groups, depth, cols), BF) for n in DEPTHS],
            compiler_params=pltpu.CompilerParams(vmem_limit_bytes=32 * 1024 * 1024),
            name="forward",
        )(plan, arrived)
        moved = [swap(v, "tile", m, tiles) for m, v in zip(NEAR, held)]
        return *moved, jnp.zeros((rest, groups, depth, cols), BF)

    def again():
        second = route(False)
        return *[second[a:a + n] for a, n in zip(starts, DEPTHS)], second[-rest:]

    units = (arrived, *lax.cond(plan[near, 0] > 0, forward, again))
    stacked = jnp.concatenate([w_query, w_key, w_value, w_out.T], axis=1)
    near = jnp.stack(
        [stacked] + [swap(stacked, "head", d, groups) for d in range(1, groups)]
    )
    turn = jnp.arange(groups, dtype=jnp.int32) ^ me
    stacked = jnp.take(near, turn, axis=0)
    wq, wk, wv, wo = [
        stacked[:, :, a * 128:(a + 1) * 128].transpose(1, 0, 2).reshape(width, width)
        for a in range(4)
    ]
    wo = wo.T
    by_distance = jnp.stack(
        [self_bias] + [swap(self_bias, "head", d, groups) for d in range(1, groups)]
    )
    turn = jnp.arange(groups, dtype=jnp.int32) ^ me
    bias_all = jnp.take(by_distance, turn, axis=0).reshape(heads)
    queries = jnp.dot(latent, wq, preferred_element_type=F32).astype(BF)
    own_key = jnp.dot(latent, wk, preferred_element_type=F32).astype(BF)
    q3 = queries.reshape(lat_rows, heads, head_size)
    k3 = wk.reshape(width, heads, head_size)
    scale = 1.0 / math.sqrt(head_size)
    qw = (
        jnp.einsum("lhd,khd->hlk", q3, k3, preferred_element_type=F32) * scale
    ).astype(BF)
    own = (
        jnp.sum(
            q3.astype(F32) * own_key.reshape(lat_rows, heads, head_size).astype(F32), axis=-1
        )
        * scale
        + bias_all[None, :]
    )
    keep = (me == 0).astype(F32)
    states = jnp.pad(
        jnp.concatenate([own, jnp.full((lat_rows, heads), keep)], axis=1),
        ((0, 0), (0, 128 - 2 * heads)),
    )
    numer = jnp.dot(latent, wv, preferred_element_type=F32) * keep

    block = PAIR * sub
    scratch = [
        pltpu.VMEM((SLOTS * tiles, groups, depth, cols), BF),
        pltpu.SemaphoreType.DMA((len(units) + 1,)),
        pltpu.VMEM((subs, 256), jnp.int32),
        pltpu.SMEM((subs, 256), jnp.int32),
        pltpu.VMEM((SLOTS * tiles, 128), F32),
    ] + [
        shape
        for shape in (
            pltpu.VMEM((CHUNK * quarter, width), BF),
            pltpu.VMEM((heads * sub, width), F32),
            pltpu.VMEM((heads * sub, 128), F32),
            pltpu.VMEM((heads * sub, 128), F32),
        )
        for _ in range(PAIR)
    ]
    partial = pl.pallas_call(
        attend_kernel,
        grid=(subs // PAIR,),
        in_specs=[pl.BlockSpec(memory_space=pl.ANY)] * len(units)
        + [
            pl.BlockSpec((heads, block, width), lambda g: (0, g, 0)),
            pl.BlockSpec((block, 128), lambda g: (g, 0)),
            pl.BlockSpec((block, width), lambda g: (g, 0)),
            whole(width, width),
        ],
        out_specs=pl.BlockSpec((block, width + 128), lambda g: (g, 0)),
        scratch_shapes=scratch,
        out_shape=jax.ShapeDtypeStruct((lat_rows, width + 128), BF),
        compiler_params=pltpu.CompilerParams(vmem_limit_bytes=48 * 1024 * 1024),
        name="attend",
    )(*units, qw, states, numer, wv)

    partial = partial.reshape(groups, share, width + 128)
    received = [pick(partial, me)] + [
        swap(pick(partial, me ^ d), "head", d, groups) for d in range(1, groups)
    ]
    row = lambda *shape: pl.BlockSpec(shape, lambda i, m: (m[0], 0))
    mine, grads = pl.pallas_call(
        finish_kernel,
        grid_spec=pltpu.PrefetchScalarGridSpec(
            num_scalar_prefetch=1,
            grid=(1,),
            in_specs=[whole(share, width + 128)] * groups
            + [
                row(share, width),
                whole(width, width),
                whole(1, width),
                whole(width, 128),
                row(share, 128),
            ],
            out_specs=[whole(share, 128), whole(groups, cols, 128)],
        ),
        out_shape=[
            jax.ShapeDtypeStruct((share, 128), F32),
            jax.ShapeDtypeStruct((groups, cols, 128), F32),
        ],
        compiler_params=pltpu.CompilerParams(vmem_limit_bytes=32 * 1024 * 1024),
        name="finish",
    )(
        me[None].astype(jnp.int32),
        *received,
        latent,
        wo,
        norm_gain[None, :],
        w_inc,
        target,
    )
    grads = [pick(grads, me)] + [
        swap(pick(grads, me ^ d), "head", d, groups) for d in range(1, groups)
    ]
    grad = (grads[0] + grads[1]) + (grads[2] + grads[3])
    for low, high in ((1, 2), (4, 8), (16, 32)):
        a, b, c = (swap(grad, "tile", m, tiles) for m in (low, high, low + high))
        grad = (grad + a) + (b + c)
    preds = jnp.stack([mine] + [swap(mine, "head", d, groups) for d in range(1, groups)])
    predicted = jnp.take(preds, turn, axis=0).reshape(lat_rows, 128)
    return predicted, grad * (1.0 / math.sqrt(lat_rows * tiles))


def solution(mesh):
    in_specs = (
        P("tile", "head"),
        P("tile"),
        P("tile", None),
        P("tile", None),
        P("tile", None),
        P(None, "head"),
        P(None, "head"),
        P(None, "head"),
        P("head"),
        P("head", None),
        P(),
        P(),
        P("tile", None),
    )
    out_specs = (P("tile", None), P("head", None))
    return jax.shard_map(body, mesh=mesh, in_specs=in_specs, out_specs=out_specs, check_vma=False)
```

```python
import functools
import math

import jax
import jax.numpy as jnp
from jax import lax
from jax.experimental import pallas as pl
from jax.experimental.pallas import tpu as pltpu
from jax.sharding import PartitionSpec as P

BF = jnp.bfloat16
F32 = jnp.float32
NEG = -1e30
SLOTS = 2
CHUNK = 8
PAIR = 8
NEAR = (1, 16, 17, 48, 49, 2, 3, 32)
DEPTHS = (6, 6, 6, 6, 6, 6, 6, 2)


def route_kernel(spill, owner, alive, obs, row_marks, pattern, sent, info, lanes, extra, near):
    tiles = sent.shape[0]
    blocks, parts, quarter = obs.shape[:3]
    subs = pattern.shape[0]
    me = lax.axis_index("tile")
    lane = lax.broadcasted_iota(jnp.int32, (blocks, 128), 1)
    rows = row_marks[...].astype(F32)
    spot = lax.broadcasted_iota(jnp.int32, (subs, 128), 1)
    line = lax.broadcasted_iota(jnp.int32, (subs, 128), 0)
    shift = (spot == line + quarter).astype(F32).astype(BF)
    groups = lax.dot_general(
        pattern[...].astype(F32).astype(BF),
        shift,
        (((0,), (0,)), ((), ())),
        preferred_element_type=F32,
    )
    for j in range(parts):
        turned = rows if j == 0 else pltpu.roll(rows, 128 - j * quarter, 1)
        info[j, :blocks] = jnp.where(lane < quarter, turned, groups)
        info[j, blocks:] = jnp.zeros((8, 128), F32)
    for m, mask in enumerate(NEAR):
        near[m] = mask

    def clear(t, carry):
        lanes[t] = blocks
        lanes[tiles + t] = 0
        return carry

    lax.fori_loop(0, tiles, clear, 0, unroll=8)

    def place(b, n):
        t = owner[b]
        live = alive[b]
        seen = lanes[tiles + t]
        take = (live > 0) & ((seen == 0) if spill else (seen > 0))
        lanes[t] = jnp.where(take, b, lanes[t])
        lanes[tiles + t] = seen | live
        extra[n] = b
        return n + (live & seen)

    more = lax.fori_loop(0, blocks, place, jnp.int32(0), unroll=4)
    left = jnp.int32(0)
    if spill:

        def move(q, left):
            b = extra[q]
            t = owner[b]
            found = jnp.int32(tiles)
            last = len(NEAR) - 1
            for a in range(len(NEAR)):
                other = t ^ (NEAR[last] if a == last else near[(me + q + a) % last])
                free = (lanes[other] == blocks) & (found == tiles)
                found = jnp.where(free, other, found)

            @pl.when(found < tiles)
            def _():
                lanes[found] = b

            return left + (found == tiles).astype(jnp.int32)

        left = lax.fori_loop(0, more, move, left)

    lane1 = lax.broadcasted_iota(jnp.int32, (1, 128), 1)

    def goal(t):
        b = lanes[t]
        return jnp.where(b < blocks, owner[jnp.minimum(b, blocks - 1)] + 1, 0)

    def note(t, table):
        return jnp.where(lane1 == t, goal(t).astype(F32), table)

    table = jnp.where(lane1 == tiles, left.astype(F32), jnp.zeros((1, 128), F32))
    table = lax.fori_loop(0, tiles, note, table, unroll=8)
    line8 = lax.broadcasted_iota(jnp.int32, (8, 128), 0)

    def fill(t, carry):
        b = lanes[t]
        to = jnp.where(lane1 == quarter + subs, goal(t).astype(F32), 0.0)
        for j in range(parts):
            one = info[j, pl.ds(b, 1), :] + to
            tail = jnp.where(line8 == 0, one, jnp.where(line8 == 1, table, 0.0))
            sent[t, j, quarter:, :] = tail.astype(BF)

        @pl.when(b < blocks)
        def _():
            sent[t, :, :quarter, :] = obs[b]

        @pl.when(b >= blocks)
        def _():
            sent[t, :, :quarter, :] = jnp.zeros(obs.shape[1:], BF)

        return carry

    lax.fori_loop(0, tiles, fill, 0, unroll=2)


def before(n):
    return (
        lax.broadcasted_iota(jnp.int32, (n, n), 0) < lax.broadcasted_iota(jnp.int32, (n, n), 1)
    ).astype(F32).astype(BF)


def listing(live):
    rows, n = live.shape
    place = jnp.dot(live.astype(BF), before(n), preferred_element_type=F32)
    turn = lax.broadcasted_iota(jnp.int32, (rows, 128, n), 1).astype(F32)
    name = lax.broadcasted_iota(jnp.int32, (rows, 128, n), 2).astype(F32)
    hit = (place[:, None, :] == turn) & (live[:, None, :] > 0.5)
    order = jnp.sum(jnp.where(hit, name, 0.0), axis=2)
    return order, jnp.sum(live, axis=1, keepdims=True)


def plan_kernel(arrived, plan, *rest):
    *outs, lists, sem = rest
    tiles = arrived.shape[0]
    near = len(NEAR)
    me = lax.axis_index("tile")
    table = arrived[:, 0, 32:40, :].astype(F32)[:, 1, :]
    mine = (lax.broadcasted_iota(jnp.int32, (near, 128), 1) == me).astype(F32).astype(BF)
    goals = lax.dot_general(
        mine, table.astype(BF), (((1,), (1,)), ((), ())), preferred_element_type=F32
    )
    line = lax.broadcasted_iota(jnp.int32, (near, tiles), 0)
    want = jnp.zeros((near, tiles), jnp.int32)
    for m, mask in enumerate(NEAR):
        want = jnp.where(line == m, (me ^ mask) + 1, want)
    order, count = listing((goals == want.astype(F32)).astype(F32))
    place = lax.broadcasted_iota(jnp.int32, (near, 128), 1)
    plan[:near] = jnp.where(place.astype(F32) < count, order, tiles).astype(jnp.int32)
    lane = lax.broadcasted_iota(jnp.int32, (1, 128), 1)
    worst = jnp.zeros((1, 128), F32)
    for mask, depth in zip(NEAR, DEPTHS):
        here = (table == ((lane ^ mask) + 1).astype(F32)).astype(F32)
        total = jnp.sum(here, axis=0, keepdims=True)
        worst = jnp.maximum(worst, jnp.where(lane < tiles, total - depth, 0.0))
    left = jnp.sum(jnp.where(lane == tiles, table, 0.0), axis=0, keepdims=True)
    bad = jnp.max(jnp.where(worst > 0.0, 1.0, left), axis=1, keepdims=True)
    good = jnp.where(bad > 0.0, 0, 1)
    plan[near:] = jnp.broadcast_to(good, (near, 128))
    copy = pltpu.make_async_copy(plan, lists, sem)
    copy.start()
    copy.wait()
    for m, out in enumerate(outs):
        for c in range(DEPTHS[m]):
            s = lists[m, c]

            @pl.when(s < tiles)
            def _(s=s, out=out, c=c):
                out[c] = arrived[s]

            @pl.when(s >= tiles)
            def _(out=out, c=c):
                out[c] = jnp.zeros(out.shape[1:], BF)


def lists_of(marks, quarter, subs):
    me = lax.axis_index("tile")
    to = marks[:, quarter + subs:quarter + subs + 1]
    marks = jnp.where(to == (me + 1).astype(F32), marks, 0.0).astype(BF)
    pick_group = (
        lax.broadcasted_iota(jnp.int32, (subs, 128), 1)
        == lax.broadcasted_iota(jnp.int32, (subs, 128), 0) + quarter
    ).astype(F32).astype(BF)
    up = lax.broadcasted_iota(jnp.int32, (128, 128), 0)
    along = lax.broadcasted_iota(jnp.int32, (128, 128), 1)
    widen = ((up < quarter) & (up == along % quarter)).astype(F32).astype(BF)
    live = lax.dot_general(
        pick_group, marks, (((1,), (1,)), ((), ())), preferred_element_type=F32
    )
    order, count = listing(live)
    rows = jnp.dot(marks, widen, preferred_element_type=F32)
    return order, count, (rows - 1.0) * (-NEG)


def split3(v):
    hi = v.astype(BF).astype(F32)
    mid = (v - hi).astype(BF).astype(F32)
    return hi, mid, v - hi - mid


def attend_kernel(*refs):
    units = refs[:len(NEAR) + 2]
    qw, begun, given, wv, *refs = refs[len(NEAR) + 2:]
    outs, (x, sems, made, lists, bias, result, *scratch) = refs[:4], refs[4:]
    me = lax.axis_index("head")
    step_id = pl.program_id(0)
    quarter = 32

    @pl.when(step_id == 0)
    def _():
        copies = []
        at = 0
        for u, unit in enumerate(units):
            n = unit.shape[0]
            copies.append(pltpu.make_async_copy(unit, x.at[pl.ds(at, n)], sems.at[u]))
            at += n
        for copy in copies:
            copy.start()
        for copy in copies:
            copy.wait()
        marks = x[:, 0, quarter:quarter + 8, :].astype(F32)[:, 0, :]
        order, count, shade = lists_of(marks, quarter, made.shape[0])
        bias[...] = shade
        made[:, :128] = order.astype(jnp.int32)
        made[:, 128:] = jnp.broadcast_to(count, order.shape).astype(jnp.int32)
        copy = pltpu.make_async_copy(made, lists, sems.at[len(units)])
        copy.start()
        copy.wait()

    heads, both, width = qw.shape
    sub = both // PAIR
    rows = heads * sub
    parts, _, cols = x.shape[1:]
    size = CHUNK * quarter
    per = 128 // quarter
    lane_slot = lax.broadcasted_iota(jnp.int32, (1, 128), 1) // quarter
    lane = lax.broadcasted_iota(jnp.int32, (sub, 128), 1)
    xbufs, accs, tops, dens = (scratch[q * PAIR:(q + 1) * PAIR] for q in range(4))

    def gather(g, n, c, xbuf):
        shades = []
        for part in range(CHUNK // per):
            shade = jnp.full((1, 128), NEG, F32)
            for v in range(per):
                u = part * per + v
                place = c * CHUNK + u
                s = lists[g, jnp.maximum(jnp.minimum(place, n - 1), 0)]
                for i in range(parts):
                    xbuf[u * quarter:(u + 1) * quarter, i * cols:(i + 1) * cols] = x[
                        s, i, :quarter, :
                    ]
                live = (lane_slot == v) & (place < n)
                shade = jnp.where(live, bias[pl.ds(s, 1), :], shade)
            shades.append(shade)
        return xbuf[...], jnp.concatenate(shades, axis=1)

    def chunk(queries, rows_x, shade, old):
        scores = lax.dot_general(
            queries, rows_x, (((1,), (1,)), ((), ())), preferred_element_type=F32
        ) + shade
        new = jnp.maximum(old, jnp.max(scores, axis=1, keepdims=True))
        weights = jnp.exp(scores - jnp.concatenate([new] * (size // 128), axis=1))
        total = jnp.sum(weights, axis=1, keepdims=True)
        more = jnp.dot(weights.astype(BF), rows_x, preferred_element_type=F32)
        return new, jnp.exp(old - new), total, more

    counts, begins = [], []
    for p in range(PAIR):
        g = step_id * PAIR + p
        n = lists[g, 128]
        counts.append(n)
        start = begun[p * sub:(p + 1) * sub, :]
        old = jnp.concatenate(
            [jnp.broadcast_to(start[:, h:h + 1], (sub, 128)) for h in range(heads)], axis=0
        )
        den = jnp.concatenate(
            [
                jnp.broadcast_to(start[:, heads + h:heads + h + 1], (sub, 128))
                for h in range(heads)
            ],
            axis=0,
        )
        begins.append(old)
        rows_x, shade = gather(g, n, 0, xbufs[p])
        queries = qw[:, p * sub:(p + 1) * sub, :].reshape(rows, width)
        new, shrink, total, more = chunk(queries, rows_x, shade, old)
        accs[p][...] = more
        tops[p][...] = new
        dens[p][...] = den * shrink + total

    for p in range(PAIR):
        g = step_id * PAIR + p

        @pl.when(counts[p] > CHUNK)
        def _(p=p, g=g):
            def again(c, carry):
                rows_x, shade = gather(g, counts[p], c, xbufs[p])
                queries = qw[:, p * sub:(p + 1) * sub, :].reshape(rows, width)
                new, shrink, total, more = chunk(queries, rows_x, shade, tops[p][...])
                tops[p][...] = new
                dens[p][...] = dens[p][...] * shrink + total
                wide = jnp.concatenate([shrink] * (width // 128), axis=1)
                accs[p][...] = accs[p][...] * wide + more
                return carry

            lax.fori_loop(1, (counts[p] + CHUNK - 1) // CHUNK, again, 0)

    half = width // 2
    for p in range(PAIR):
        place = slice(p * sub, (p + 1) * sub)
        share = outs[0].shape[0]
        quarter_id = (step_id * (PAIR * sub // share) + p * sub // share) ^ me
        line0 = (p * sub) % share
        spot = slice(line0, line0 + sub)
        top = tops[p][...]
        shrink = jnp.exp(begins[p] - top)
        state = jnp.zeros((sub, 128), F32)
        for h in range(heads):
            line = slice(h * sub, (h + 1) * sub)
            state = jnp.where(lane == h, top[line], state)
            state = jnp.where(lane == heads + h, dens[p][line, :], state)
        hi, mid, lo = split3(state)
        packed = hi + pltpu.roll(mid, 2 * heads, 1) + pltpu.roll(lo, 4 * heads, 1)
        result[quarter_id, spot, width:] = packed.astype(BF)
        for side in range(2):
            here = slice(side * rows // 2, (side + 1) * rows // 2)
            mixed = jnp.dot(
                accs[p][here, :].astype(BF),
                wv[:, side * half:(side + 1) * half],
                preferred_element_type=F32,
            )
            for c in range(half // 128):
                col = side * half + c * 128
                two = []
                for h in (2 * c, 2 * c + 1):
                    line = slice(h * sub, (h + 1) * sub)
                    far = side * rows // 2
                    two.append(
                        given[place, col:col + 128] * shrink[far + h * sub:far + (h + 1) * sub]
                        + mixed[line, c * 128:(c + 1) * 128]
                    )
                result[quarter_id, spot, col:col + 128] = jnp.where(
                    lane < width // heads, two[0], two[1]
                ).astype(BF)

    @pl.when(step_id == pl.num_programs(0) - 1)
    def _():
        for d, out in enumerate(outs):
            out[...] = result[d]


def finish_kernel(place, r0, r1, r2, r3, lat, w_out, gain, w_inc, target, predicted, *grads):
    width = lat.shape[1]
    heads = 8
    line = lax.broadcasted_iota(jnp.int32, (128, 2 * width), 0)
    col = lax.broadcasted_iota(jnp.int32, (128, 2 * width), 1)
    match = (
        (line % heads == (col % width) // (width // heads))
        & ((line // heads) % 2 == col // width)
        & (line < 6 * heads)
    )
    spread = match.astype(F32).astype(BF)
    tops, dens, nums = [], [], []
    for r in (r0, r1, r2, r3):
        wide = jnp.dot(r[:, width:], spread, preferred_element_type=F32)
        tops.append(wide[:, :width])
        dens.append(wide[:, width:])
        nums.append(r[:, :width].astype(F32))
    best = jnp.maximum(jnp.maximum(tops[0], tops[1]), jnp.maximum(tops[2], tops[3]))
    scale = [jnp.exp(v - best) for v in tops]
    numer = sum(a * b for a, b in zip(scale, nums))
    denom = sum(a * b for a, b in zip(scale, dens))
    attended = (numer / denom).astype(BF)
    updated = lat[...].astype(F32) + jnp.dot(attended, w_out[...], preferred_element_type=F32)
    power = jnp.mean(updated * updated, axis=1, keepdims=True)
    normed = (updated * lax.rsqrt(power + 1e-6) * gain[...]).astype(BF)
    answer = jnp.dot(normed, w_inc[...], preferred_element_type=F32)
    predicted[...] = answer
    residual = answer - target[...].astype(F32)
    high = residual.astype(BF)
    low = (residual - high.astype(F32)).astype(BF)
    dims = (((0,), (0,)), ((), ()))
    total = lax.dot_general(normed, high, dims, preferred_element_type=F32)
    total = total + lax.dot_general(normed, low, dims, preferred_element_type=F32)
    *grads, cut = grads
    size = grads[0].shape[0]
    for c in range(width // size):
        cut[c] = total[c * size:(c + 1) * size]
    for d, grad in enumerate(grads):
        grad[...] = cut[place[0] ^ d]


def body(
    obs_feat,
    row_valid,
    block_owner,
    block_pattern,
    latent,
    w_query,
    w_key,
    w_value,
    self_bias,
    w_out,
    norm_gain,
    w_inc,
    target,
):
    tiles = lax.axis_size("tile")
    groups = lax.axis_size("head")
    me = lax.axis_index("head")
    blocks = block_owner.shape[0]
    block_rows = obs_feat.shape[0] // blocks
    quarter = block_rows // groups
    cols = obs_feat.shape[1]
    lat_rows, width = latent.shape
    subs = block_pattern.shape[1]
    sub = lat_rows // subs
    local_heads = self_bias.shape[0]
    heads = local_heads * groups
    head_size = width // heads
    share = lat_rows // groups

    def swap(v, axis, mask, size):
        return lax.ppermute(v, axis, [(d, d ^ mask) for d in range(size)])

    whole = lambda *shape: pl.BlockSpec(shape, lambda g, *_: (0,) * len(shape))
    depth = quarter + 8
    alive = jnp.max(block_pattern.T, axis=0)

    def route(spill):
        sent = pl.pallas_call(
            functools.partial(route_kernel, spill),
            grid_spec=pltpu.PrefetchScalarGridSpec(
                num_scalar_prefetch=2,
                grid=(1,),
                in_specs=[
                    whole(blocks, groups, quarter, cols),
                    whole(blocks, block_rows),
                    whole(subs, blocks),
                ],
                out_specs=whole(tiles, groups, depth, cols),
                scratch_shapes=[
                    pltpu.VMEM((groups, blocks + 8, 128), F32),
                    pltpu.SMEM((2 * tiles,), jnp.int32),
                    pltpu.SMEM((blocks + 8,), jnp.int32),
                    pltpu.SMEM((len(NEAR),), jnp.int32),
                ],
            ),
            out_shape=jax.ShapeDtypeStruct((tiles, groups, depth, cols), BF),
            compiler_params=pltpu.CompilerParams(vmem_limit_bytes=32 * 1024 * 1024),
            name="route",
        )(
            block_owner[:, 0],
            alive,
            obs_feat.reshape(blocks, groups, quarter, cols),
            row_valid.reshape(blocks, block_rows),
            block_pattern.T,
        )
        return lax.all_to_all(
            sent.reshape(tiles * groups, depth, cols),
            ("tile", "head"),
            split_axis=0,
            concat_axis=0,
            tiled=True,
        ).reshape(tiles, groups, depth, cols)

    arrived = route(True)
    near = len(NEAR)
    stacked = jnp.concatenate([w_query, w_key, w_value, w_out.T], axis=1)
    nearby = [stacked] + [swap(stacked, "head", d, groups) for d in range(1, groups)]
    turn = jnp.arange(groups, dtype=jnp.int32) ^ me
    biases = [self_bias] + [swap(self_bias, "head", d, groups) for d in range(1, groups)]

    def prepare():
        stacked = jnp.take(jnp.stack(nearby), turn, axis=0)
        wq, wk, wv, wo = [
            stacked[:, :, a * 128:(a + 1) * 128].transpose(1, 0, 2).reshape(width, width)
            for a in range(4)
        ]
        wo = wo.T
        bias_all = jnp.take(jnp.stack(biases), turn, axis=0).reshape(heads)
        queries = jnp.dot(latent, wq, preferred_element_type=F32).astype(BF)
        own_key = jnp.dot(latent, wk, preferred_element_type=F32).astype(BF)
        q3 = queries.reshape(lat_rows, heads, head_size)
        k3 = wk.reshape(width, heads, head_size)
        scale = 1.0 / math.sqrt(head_size)
        qw = (
            jnp.einsum("lhd,khd->hlk", q3, k3, preferred_element_type=F32) * scale
        ).astype(BF)
        own = (
            jnp.sum(
                q3.astype(F32) * own_key.reshape(lat_rows, heads, head_size).astype(F32), axis=-1
            )
            * scale
            + bias_all[None, :]
        )
        keep = (me == 0).astype(F32)
        states = jnp.pad(
            jnp.concatenate([own, jnp.full((lat_rows, heads), keep)], axis=1),
            ((0, 0), (0, 128 - 2 * heads)),
        )
        numer = jnp.dot(latent, wv, preferred_element_type=F32) * keep
        return qw, states, numer, wv, wo

    plan, *held = pl.pallas_call(
        plan_kernel,
        grid=(1,),
        in_specs=[whole(tiles, groups, depth, cols)],
        out_specs=[whole(2 * near, 128)]
        + [whole(n, groups, depth, cols) for n in DEPTHS],
        out_shape=[jax.ShapeDtypeStruct((2 * near, 128), jnp.int32)]
        + [jax.ShapeDtypeStruct((n, groups, depth, cols), BF) for n in DEPTHS],
        scratch_shapes=[
            pltpu.SMEM((2 * near, 128), jnp.int32),
            pltpu.SemaphoreType.DMA,
        ],
        compiler_params=pltpu.CompilerParams(vmem_limit_bytes=32 * 1024 * 1024),
        name="plan",
    )(arrived)
    rest = tiles - sum(DEPTHS)
    starts = [sum(DEPTHS[:m]) for m in range(near)]

    def forward():
        moved = [swap(v, "tile", m, tiles) for m, v in zip(NEAR, held)]
        return (*moved, jnp.zeros((rest, groups, depth, cols), BF)), prepare()

    def again():
        second = route(False)
        parts = [second[a:a + n] for a, n in zip(starts, DEPTHS)]
        return (*parts, second[-rest:]), prepare()

    units, (qw, states, numer, wv, wo) = lax.cond(plan[near, 0] > 0, forward, again)
    units = (arrived, *units)
    block = PAIR * sub
    scratch = [
        pltpu.VMEM((SLOTS * tiles, groups, depth, cols), BF),
        pltpu.SemaphoreType.DMA((len(units) + 1,)),
        pltpu.VMEM((subs, 256), jnp.int32),
        pltpu.SMEM((subs, 256), jnp.int32),
        pltpu.VMEM((SLOTS * tiles, 128), F32),
        pltpu.VMEM((groups, share, width + 128), BF),
    ] + [
        shape
        for shape in (
            pltpu.VMEM((CHUNK * quarter, width), BF),
            pltpu.VMEM((heads * sub, width), F32),
            pltpu.VMEM((heads * sub, 128), F32),
            pltpu.VMEM((heads * sub, 128), F32),
        )
        for _ in range(PAIR)
    ]
    partials = pl.pallas_call(
        attend_kernel,
        grid=(subs // PAIR,),
        in_specs=[pl.BlockSpec(memory_space=pl.ANY)] * len(units)
        + [
            pl.BlockSpec((heads, block, width), lambda g: (0, g, 0)),
            pl.BlockSpec((block, 128), lambda g: (g, 0)),
            pl.BlockSpec((block, width), lambda g: (g, 0)),
            whole(width, width),
        ],
        out_specs=[whole(share, width + 128)] * groups,
        scratch_shapes=scratch,
        out_shape=[jax.ShapeDtypeStruct((share, width + 128), BF)] * groups,
        compiler_params=pltpu.CompilerParams(vmem_limit_bytes=48 * 1024 * 1024),
        name="attend",
    )(*units, qw, states, numer, wv)

    received = [partials[0]] + [
        swap(partials[d], "head", d, groups) for d in range(1, groups)
    ]
    row = lambda *shape: pl.BlockSpec(shape, lambda i, m: (m[0], 0))
    mine, *grads = pl.pallas_call(
        finish_kernel,
        grid_spec=pltpu.PrefetchScalarGridSpec(
            num_scalar_prefetch=1,
            grid=(1,),
            in_specs=[whole(share, width + 128)] * groups
            + [
                row(share, width),
                whole(width, width),
                whole(1, width),
                whole(width, 128),
                row(share, 128),
            ],
            out_specs=[whole(share, 128)] + [whole(cols, 128)] * groups,
            scratch_shapes=[pltpu.VMEM((groups, cols, 128), F32)],
        ),
        out_shape=[jax.ShapeDtypeStruct((share, 128), F32)]
        + [jax.ShapeDtypeStruct((cols, 128), F32)] * groups,
        compiler_params=pltpu.CompilerParams(vmem_limit_bytes=32 * 1024 * 1024),
        name="finish",
    )(
        me[None].astype(jnp.int32),
        *received,
        latent,
        wo,
        norm_gain[None, :],
        w_inc,
        target,
    )
    grads = [grads[0]] + [swap(grads[d], "head", d, groups) for d in range(1, groups)]
    grad = (grads[0] + grads[1]) + (grads[2] + grads[3])
    for low, high in ((1, 2), (4, 8), (16, 32)):
        a, b, c = (swap(grad, "tile", m, tiles) for m in (low, high, low + high))
        grad = (grad + a) + (b + c)
    preds = jnp.stack([mine] + [swap(mine, "head", d, groups) for d in range(1, groups)])
    predicted = jnp.take(preds, turn, axis=0).reshape(lat_rows, 128)
    return predicted, grad * (1.0 / math.sqrt(lat_rows * tiles))


def solution(mesh):
    in_specs = (
        P("tile", "head"),
        P("tile"),
        P("tile", None),
        P("tile", None),
        P("tile", None),
        P(None, "head"),
        P(None, "head"),
        P(None, "head"),
        P("head"),
        P("head", None),
        P(),
        P(),
        P("tile", None),
    )
    out_specs = (P("tile", None), P("head", None))
    return jax.shard_map(body, mesh=mesh, in_specs=in_specs, out_specs=out_specs, check_vma=False)
```

```python
import functools
import math

import jax
import jax.numpy as jnp
from jax import lax
from jax.experimental import pallas as pl
from jax.experimental.pallas import tpu as pltpu
from jax.sharding import PartitionSpec as P

BF = jnp.bfloat16
F32 = jnp.float32
NEG = -1e30
SLOTS = 2
CHUNK = 8
PAIR = 8
NEAR = (1, 16, 17, 48, 49, 2, 3, 32)
DEPTHS = (6, 6, 6, 6, 6, 6, 6, 2)


def route_kernel(spill, owner, alive, obs, row_marks, pattern, sent, info, lanes, extra, near):
    tiles = sent.shape[0]
    blocks, parts, quarter = obs.shape[:3]
    subs = pattern.shape[0]
    me = lax.axis_index("tile")
    lane = lax.broadcasted_iota(jnp.int32, (blocks, 128), 1)
    rows = row_marks[...].astype(F32)
    spot = lax.broadcasted_iota(jnp.int32, (subs, 128), 1)
    line = lax.broadcasted_iota(jnp.int32, (subs, 128), 0)
    shift = (spot == line + quarter).astype(F32).astype(BF)
    groups = lax.dot_general(
        pattern[...].astype(F32).astype(BF),
        shift,
        (((0,), (0,)), ((), ())),
        preferred_element_type=F32,
    )
    for j in range(parts):
        turned = rows if j == 0 else pltpu.roll(rows, 128 - j * quarter, 1)
        info[j, :blocks] = jnp.where(lane < quarter, turned, groups)
        info[j, blocks:] = jnp.zeros((8, 128), F32)
    for m, mask in enumerate(NEAR):
        near[m] = mask

    def clear(t, carry):
        lanes[t] = blocks
        lanes[tiles + t] = 0
        return carry

    lax.fori_loop(0, tiles, clear, 0, unroll=8)

    def place(b, n):
        t = owner[b]
        live = alive[b]
        seen = lanes[tiles + t]
        take = (live > 0) & ((seen == 0) if spill else (seen > 0))
        lanes[t] = jnp.where(take, b, lanes[t])
        lanes[tiles + t] = seen | live
        extra[n] = b
        return n + (live & seen)

    more = lax.fori_loop(0, blocks, place, jnp.int32(0), unroll=4)
    left = jnp.int32(0)
    if spill:

        def move(q, left):
            b = extra[q]
            t = owner[b]
            found = jnp.int32(tiles)
            last = len(NEAR) - 1
            for a in range(len(NEAR)):
                other = t ^ (NEAR[last] if a == last else near[(me + q + a) % last])
                free = (lanes[other] == blocks) & (found == tiles)
                found = jnp.where(free, other, found)

            @pl.when(found < tiles)
            def _():
                lanes[found] = b

            return left + (found == tiles).astype(jnp.int32)

        left = lax.fori_loop(0, more, move, left)

    lane1 = lax.broadcasted_iota(jnp.int32, (1, 128), 1)

    def goal(t):
        b = lanes[t]
        return jnp.where(b < blocks, owner[jnp.minimum(b, blocks - 1)] + 1, 0)

    def note(t, table):
        return jnp.where(lane1 == t, goal(t).astype(F32), table)

    table = jnp.where(lane1 == tiles, left.astype(F32), jnp.zeros((1, 128), F32))
    table = lax.fori_loop(0, tiles, note, table, unroll=8)
    line8 = lax.broadcasted_iota(jnp.int32, (8, 128), 0)

    def fill(t, carry):
        b = lanes[t]
        to = jnp.where(lane1 == quarter + subs, goal(t).astype(F32), 0.0)
        for j in range(parts):
            one = info[j, pl.ds(b, 1), :] + to
            tail = jnp.where(line8 == 0, one, jnp.where(line8 == 1, table, 0.0))
            sent[t, j, quarter:, :] = tail.astype(BF)

        @pl.when(b < blocks)
        def _():
            sent[t, :, :quarter, :] = obs[b]

        @pl.when(b >= blocks)
        def _():
            sent[t, :, :quarter, :] = jnp.zeros(obs.shape[1:], BF)

        return carry

    lax.fori_loop(0, tiles, fill, 0, unroll=2)


def prepare_kernel(*refs):
    biases, weights, (lat, qw, states, numer, wv, wo) = refs[:4], refs[4:8], refs[8:]
    me = lax.axis_index("head")
    heads, lat_rows, width = qw.shape
    each = heads // len(weights)
    size = width // heads
    scale = 1.0 / math.sqrt(size)
    latent = lat[...]
    lane = lax.broadcasted_iota(jnp.int32, (lat_rows, 128), 1)
    keep = jnp.where(me == 0, 1.0, 0.0)
    total = jnp.where((lane >= heads) & (lane < 2 * heads), keep, 0.0)
    for d, (bias, w) in enumerate(zip(biases, weights)):
        block = me ^ d
        far = pl.ds(pl.multiple_of(block * 128, 128), 128)
        q = jnp.dot(latent, w[:, :128], preferred_element_type=F32).astype(BF).astype(F32)
        k = jnp.dot(latent, w[:, 128:256], preferred_element_type=F32).astype(BF).astype(F32)
        v = jnp.dot(latent, w[:, 256:384], preferred_element_type=F32)
        numer[:, far] = v * keep
        wv[:, far] = w[:, 256:384]
        wo[:, far] = w[:, 384:]
        for e in range(each):
            mine = lane // size == e
            own = jnp.sum(jnp.where(mine, q * k, 0.0), axis=1, keepdims=True)
            own = own * scale + bias[e]
            total = jnp.where(lane == block * each + e, own, total)
            carried = lax.dot_general(
                jnp.where(mine, q, 0.0).astype(BF),
                w[:, 128:256],
                (((1,), (1,)), ((), ())),
                preferred_element_type=F32,
            )
            qw[block * each + e] = (carried * scale).astype(BF)
    states[...] = total


def before(n):
    return (
        lax.broadcasted_iota(jnp.int32, (n, n), 0) < lax.broadcasted_iota(jnp.int32, (n, n), 1)
    ).astype(F32).astype(BF)


def listing(live):
    rows, n = live.shape
    place = jnp.dot(live.astype(BF), before(n), preferred_element_type=F32)
    turn = lax.broadcasted_iota(jnp.int32, (rows, 128, n), 1).astype(F32)
    name = lax.broadcasted_iota(jnp.int32, (rows, 128, n), 2).astype(F32)
    hit = (place[:, None, :] == turn) & (live[:, None, :] > 0.5)
    order = jnp.sum(jnp.where(hit, name, 0.0), axis=2)
    return order, jnp.sum(live, axis=1, keepdims=True)


def plan_kernel(arrived, plan, *rest):
    *outs, lists, sem = rest
    tiles = arrived.shape[0]
    near = len(NEAR)
    me = lax.axis_index("tile")
    table = arrived[:, 0, 32:40, :].astype(F32)[:, 1, :]
    mine = (lax.broadcasted_iota(jnp.int32, (near, 128), 1) == me).astype(F32).astype(BF)
    goals = lax.dot_general(
        mine, table.astype(BF), (((1,), (1,)), ((), ())), preferred_element_type=F32
    )
    line = lax.broadcasted_iota(jnp.int32, (near, tiles), 0)
    want = jnp.zeros((near, tiles), jnp.int32)
    for m, mask in enumerate(NEAR):
        want = jnp.where(line == m, (me ^ mask) + 1, want)
    order, count = listing((goals == want.astype(F32)).astype(F32))
    place = lax.broadcasted_iota(jnp.int32, (near, 128), 1)
    plan[:near] = jnp.where(place.astype(F32) < count, order, tiles).astype(jnp.int32)
    lane = lax.broadcasted_iota(jnp.int32, (1, 128), 1)
    worst = jnp.zeros((1, 128), F32)
    for mask, depth in zip(NEAR, DEPTHS):
        here = (table == ((lane ^ mask) + 1).astype(F32)).astype(F32)
        total = jnp.sum(here, axis=0, keepdims=True)
        worst = jnp.maximum(worst, jnp.where(lane < tiles, total - depth, 0.0))
    left = jnp.sum(jnp.where(lane == tiles, table, 0.0), axis=0, keepdims=True)
    bad = jnp.max(jnp.where(worst > 0.0, 1.0, left), axis=1, keepdims=True)
    good = jnp.where(bad > 0.0, 0, 1)
    plan[near:] = jnp.broadcast_to(good, (near, 128))
    copy = pltpu.make_async_copy(plan, lists, sem)
    copy.start()
    copy.wait()
    for m, out in enumerate(outs):
        for c in range(DEPTHS[m]):
            s = lists[m, c]

            @pl.when(s < tiles)
            def _(s=s, out=out, c=c):
                out[c] = arrived[s]

            @pl.when(s >= tiles)
            def _(out=out, c=c):
                out[c] = jnp.zeros(out.shape[1:], BF)


def lists_of(marks, quarter, subs):
    me = lax.axis_index("tile")
    to = marks[:, quarter + subs:quarter + subs + 1]
    marks = jnp.where(to == (me + 1).astype(F32), marks, 0.0).astype(BF)
    pick_group = (
        lax.broadcasted_iota(jnp.int32, (subs, 128), 1)
        == lax.broadcasted_iota(jnp.int32, (subs, 128), 0) + quarter
    ).astype(F32).astype(BF)
    up = lax.broadcasted_iota(jnp.int32, (128, 128), 0)
    along = lax.broadcasted_iota(jnp.int32, (128, 128), 1)
    widen = ((up < quarter) & (up == along % quarter)).astype(F32).astype(BF)
    live = lax.dot_general(
        pick_group, marks, (((1,), (1,)), ((), ())), preferred_element_type=F32
    )
    order, count = listing(live)
    rows = jnp.dot(marks, widen, preferred_element_type=F32)
    return order, count, (rows - 1.0) * (-NEG)


def split3(v):
    hi = v.astype(BF).astype(F32)
    mid = (v - hi).astype(BF).astype(F32)
    return hi, mid, v - hi - mid


def attend_kernel(*refs):
    units = refs[:len(NEAR) + 2]
    qw, begun, given, wv, *refs = refs[len(NEAR) + 2:]
    outs, (x, sems, made, lists, bias, result, *scratch) = refs[:4], refs[4:]
    me = lax.axis_index("head")
    step_id = pl.program_id(0)
    quarter = 32

    @pl.when(step_id == 0)
    def _():
        copies = []
        at = 0
        for u, unit in enumerate(units):
            n = unit.shape[0]
            copies.append(pltpu.make_async_copy(unit, x.at[pl.ds(at, n)], sems.at[u]))
            at += n
        for copy in copies:
            copy.start()
        for copy in copies:
            copy.wait()
        marks = x[:, 0, quarter:quarter + 8, :].astype(F32)[:, 0, :]
        order, count, shade = lists_of(marks, quarter, made.shape[0])
        bias[...] = shade
        made[:, :128] = order.astype(jnp.int32)
        made[:, 128:] = jnp.broadcast_to(count, order.shape).astype(jnp.int32)
        copy = pltpu.make_async_copy(made, lists, sems.at[len(units)])
        copy.start()
        copy.wait()

    heads, both, width = qw.shape
    sub = both // PAIR
    rows = heads * sub
    parts, _, cols = x.shape[1:]
    size = CHUNK * quarter
    per = 128 // quarter
    lane_slot = lax.broadcasted_iota(jnp.int32, (1, 128), 1) // quarter
    lane = lax.broadcasted_iota(jnp.int32, (sub, 128), 1)
    xbufs, accs, tops, dens = (scratch[q * PAIR:(q + 1) * PAIR] for q in range(4))

    def gather(g, n, c, xbuf):
        shades = []
        for part in range(CHUNK // per):
            shade = jnp.full((1, 128), NEG, F32)
            for v in range(per):
                u = part * per + v
                place = c * CHUNK + u
                s = lists[g, jnp.maximum(jnp.minimum(place, n - 1), 0)]
                for i in range(parts):
                    xbuf[u * quarter:(u + 1) * quarter, i * cols:(i + 1) * cols] = x[
                        s, i, :quarter, :
                    ]
                live = (lane_slot == v) & (place < n)
                shade = jnp.where(live, bias[pl.ds(s, 1), :], shade)
            shades.append(shade)
        return xbuf[...], jnp.concatenate(shades, axis=1)

    def chunk(queries, rows_x, shade, old):
        scores = lax.dot_general(
            queries, rows_x, (((1,), (1,)), ((), ())), preferred_element_type=F32
        ) + shade
        new = jnp.maximum(old, jnp.max(scores, axis=1, keepdims=True))
        weights = jnp.exp(scores - jnp.concatenate([new] * (size // 128), axis=1))
        total = jnp.sum(weights, axis=1, keepdims=True)
        more = jnp.dot(weights.astype(BF), rows_x, preferred_element_type=F32)
        return new, jnp.exp(old - new), total, more

    counts, begins = [], []
    for p in range(PAIR):
        g = step_id * PAIR + p
        n = lists[g, 128]
        counts.append(n)
        start = begun[p * sub:(p + 1) * sub, :]
        old = jnp.concatenate(
            [jnp.broadcast_to(start[:, h:h + 1], (sub, 128)) for h in range(heads)], axis=0
        )
        den = jnp.concatenate(
            [
                jnp.broadcast_to(start[:, heads + h:heads + h + 1], (sub, 128))
                for h in range(heads)
            ],
            axis=0,
        )
        begins.append(old)
        rows_x, shade = gather(g, n, 0, xbufs[p])
        queries = qw[:, p * sub:(p + 1) * sub, :].reshape(rows, width)
        new, shrink, total, more = chunk(queries, rows_x, shade, old)
        accs[p][...] = more
        tops[p][...] = new
        dens[p][...] = den * shrink + total

    for p in range(PAIR):
        g = step_id * PAIR + p

        @pl.when(counts[p] > CHUNK)
        def _(p=p, g=g):
            def again(c, carry):
                rows_x, shade = gather(g, counts[p], c, xbufs[p])
                queries = qw[:, p * sub:(p + 1) * sub, :].reshape(rows, width)
                new, shrink, total, more = chunk(queries, rows_x, shade, tops[p][...])
                tops[p][...] = new
                dens[p][...] = dens[p][...] * shrink + total
                wide = jnp.concatenate([shrink] * (width // 128), axis=1)
                accs[p][...] = accs[p][...] * wide + more
                return carry

            lax.fori_loop(1, (counts[p] + CHUNK - 1) // CHUNK, again, 0)

    half = width // 2
    for p in range(PAIR):
        place = slice(p * sub, (p + 1) * sub)
        share = outs[0].shape[0]
        quarter_id = (step_id * (PAIR * sub // share) + p * sub // share) ^ me
        line0 = (p * sub) % share
        spot = slice(line0, line0 + sub)
        top = tops[p][...]
        shrink = jnp.exp(begins[p] - top)
        state = jnp.zeros((sub, 128), F32)
        for h in range(heads):
            line = slice(h * sub, (h + 1) * sub)
            state = jnp.where(lane == h, top[line], state)
            state = jnp.where(lane == heads + h, dens[p][line, :], state)
        hi, mid, lo = split3(state)
        packed = hi + pltpu.roll(mid, 2 * heads, 1) + pltpu.roll(lo, 4 * heads, 1)
        result[quarter_id, spot, width:] = packed.astype(BF)
        for side in range(2):
            here = slice(side * rows // 2, (side + 1) * rows // 2)
            mixed = jnp.dot(
                accs[p][here, :].astype(BF),
                wv[:, side * half:(side + 1) * half],
                preferred_element_type=F32,
            )
            for c in range(half // 128):
                col = side * half + c * 128
                two = []
                for h in (2 * c, 2 * c + 1):
                    line = slice(h * sub, (h + 1) * sub)
                    far = side * rows // 2
                    two.append(
                        given[place, col:col + 128] * shrink[far + h * sub:far + (h + 1) * sub]
                        + mixed[line, c * 128:(c + 1) * 128]
                    )
                result[quarter_id, spot, col:col + 128] = jnp.where(
                    lane < width // heads, two[0], two[1]
                ).astype(BF)

    @pl.when(step_id == pl.num_programs(0) - 1)
    def _():
        for d, out in enumerate(outs):
            out[...] = result[d]


def finish_kernel(place, r0, r1, r2, r3, lat, w_out, gain, w_inc, target, predicted, *grads):
    width = lat.shape[1]
    heads = 8
    line = lax.broadcasted_iota(jnp.int32, (128, 2 * width), 0)
    col = lax.broadcasted_iota(jnp.int32, (128, 2 * width), 1)
    match = (
        (line % heads == (col % width) // (width // heads))
        & ((line // heads) % 2 == col // width)
        & (line < 6 * heads)
    )
    spread = match.astype(F32).astype(BF)
    tops, dens, nums = [], [], []
    for r in (r0, r1, r2, r3):
        wide = jnp.dot(r[:, width:], spread, preferred_element_type=F32)
        tops.append(wide[:, :width])
        dens.append(wide[:, width:])
        nums.append(r[:, :width].astype(F32))
    best = jnp.maximum(jnp.maximum(tops[0], tops[1]), jnp.maximum(tops[2], tops[3]))
    scale = [jnp.exp(v - best) for v in tops]
    numer = sum(a * b for a, b in zip(scale, nums))
    denom = sum(a * b for a, b in zip(scale, dens))
    attended = (numer / denom).astype(BF)
    updated = lat[...].astype(F32) + lax.dot_general(
        attended, w_out[...], (((1,), (1,)), ((), ())), preferred_element_type=F32
    )
    power = jnp.mean(updated * updated, axis=1, keepdims=True)
    normed = (updated * lax.rsqrt(power + 1e-6) * gain[...]).astype(BF)
    answer = jnp.dot(normed, w_inc[...], preferred_element_type=F32)
    predicted[...] = answer
    residual = answer - target[...].astype(F32)
    high = residual.astype(BF)
    low = (residual - high.astype(F32)).astype(BF)
    dims = (((0,), (0,)), ((), ()))
    total = lax.dot_general(normed, high, dims, preferred_element_type=F32)
    total = total + lax.dot_general(normed, low, dims, preferred_element_type=F32)
    *grads, cut = grads
    size = grads[0].shape[0]
    for c in range(width // size):
        cut[c] = total[c * size:(c + 1) * size]
    for d, grad in enumerate(grads):
        grad[...] = cut[place[0] ^ d]


def body(
    obs_feat,
    row_valid,
    block_owner,
    block_pattern,
    latent,
    w_query,
    w_key,
    w_value,
    self_bias,
    w_out,
    norm_gain,
    w_inc,
    target,
):
    tiles = lax.axis_size("tile")
    groups = lax.axis_size("head")
    me = lax.axis_index("head")
    blocks = block_owner.shape[0]
    block_rows = obs_feat.shape[0] // blocks
    quarter = block_rows // groups
    cols = obs_feat.shape[1]
    lat_rows, width = latent.shape
    subs = block_pattern.shape[1]
    sub = lat_rows // subs
    local_heads = self_bias.shape[0]
    heads = local_heads * groups
    head_size = width // heads
    share = lat_rows // groups

    def swap(v, axis, mask, size):
        return lax.ppermute(v, axis, [(d, d ^ mask) for d in range(size)])

    whole = lambda *shape: pl.BlockSpec(shape, lambda g, *_: (0,) * len(shape))
    depth = quarter + 8
    alive = jnp.max(block_pattern.T, axis=0)

    def route(spill):
        sent = pl.pallas_call(
            functools.partial(route_kernel, spill),
            grid_spec=pltpu.PrefetchScalarGridSpec(
                num_scalar_prefetch=2,
                grid=(1,),
                in_specs=[
                    whole(blocks, groups, quarter, cols),
                    whole(blocks, block_rows),
                    whole(subs, blocks),
                ],
                out_specs=whole(tiles, groups, depth, cols),
                scratch_shapes=[
                    pltpu.VMEM((groups, blocks + 8, 128), F32),
                    pltpu.SMEM((2 * tiles,), jnp.int32),
                    pltpu.SMEM((blocks + 8,), jnp.int32),
                    pltpu.SMEM((len(NEAR),), jnp.int32),
                ],
            ),
            out_shape=jax.ShapeDtypeStruct((tiles, groups, depth, cols), BF),
            compiler_params=pltpu.CompilerParams(vmem_limit_bytes=32 * 1024 * 1024),
            name="route",
        )(
            block_owner[:, 0],
            alive,
            obs_feat.reshape(blocks, groups, quarter, cols),
            row_valid.reshape(blocks, block_rows),
            block_pattern.T,
        )
        return lax.all_to_all(
            sent.reshape(tiles * groups, depth, cols),
            ("tile", "head"),
            split_axis=0,
            concat_axis=0,
            tiled=True,
        ).reshape(tiles, groups, depth, cols)

    arrived = route(True)
    near = len(NEAR)
    stacked = jnp.concatenate([w_query, w_key, w_value, w_out.T], axis=1)
    nearby = [stacked] + [swap(stacked, "head", d, groups) for d in range(1, groups)]
    turn = jnp.arange(groups, dtype=jnp.int32) ^ me
    biases = [self_bias] + [swap(self_bias, "head", d, groups) for d in range(1, groups)]

    qw, states, numer, wv, wo = pl.pallas_call(
        prepare_kernel,
        grid=(1,),
        in_specs=[pl.BlockSpec(memory_space=pltpu.SMEM)] * groups
        + [whole(width, width)] * groups
        + [whole(lat_rows, width)],
        out_specs=[
            whole(heads, lat_rows, width),
            whole(lat_rows, 128),
            whole(lat_rows, width),
            whole(width, width),
            whole(width, width),
        ],
        out_shape=[
            jax.ShapeDtypeStruct((heads, lat_rows, width), BF),
            jax.ShapeDtypeStruct((lat_rows, 128), F32),
            jax.ShapeDtypeStruct((lat_rows, width), F32),
            jax.ShapeDtypeStruct((width, width), BF),
            jax.ShapeDtypeStruct((width, width), BF),
        ],
        compiler_params=pltpu.CompilerParams(vmem_limit_bytes=32 * 1024 * 1024),
        name="prepare",
    )(*biases, *nearby, latent)

    plan, *held = pl.pallas_call(
        plan_kernel,
        grid=(1,),
        in_specs=[whole(tiles, groups, depth, cols)],
        out_specs=[whole(2 * near, 128)]
        + [whole(n, groups, depth, cols) for n in DEPTHS],
        out_shape=[jax.ShapeDtypeStruct((2 * near, 128), jnp.int32)]
        + [jax.ShapeDtypeStruct((n, groups, depth, cols), BF) for n in DEPTHS],
        scratch_shapes=[
            pltpu.SMEM((2 * near, 128), jnp.int32),
            pltpu.SemaphoreType.DMA,
        ],
        compiler_params=pltpu.CompilerParams(vmem_limit_bytes=32 * 1024 * 1024),
        name="plan",
    )(arrived)
    rest = tiles - sum(DEPTHS)
    starts = [sum(DEPTHS[:m]) for m in range(near)]

    def forward():
        moved = [swap(v, "tile", m, tiles) for m, v in zip(NEAR, held)]
        return *moved, jnp.zeros((rest, groups, depth, cols), BF)

    def again():
        second = route(False)
        parts = [second[a:a + n] for a, n in zip(starts, DEPTHS)]
        return *parts, second[-rest:]

    units = (arrived, *lax.cond(plan[near, 0] > 0, forward, again))
    block = PAIR * sub
    scratch = [
        pltpu.VMEM((SLOTS * tiles, groups, depth, cols), BF),
        pltpu.SemaphoreType.DMA((len(units) + 1,)),
        pltpu.VMEM((subs, 256), jnp.int32),
        pltpu.SMEM((subs, 256), jnp.int32),
        pltpu.VMEM((SLOTS * tiles, 128), F32),
        pltpu.VMEM((groups, share, width + 128), BF),
    ] + [
        shape
        for shape in (
            pltpu.VMEM((CHUNK * quarter, width), BF),
            pltpu.VMEM((heads * sub, width), F32),
            pltpu.VMEM((heads * sub, 128), F32),
            pltpu.VMEM((heads * sub, 128), F32),
        )
        for _ in range(PAIR)
    ]
    partials = pl.pallas_call(
        attend_kernel,
        grid=(subs // PAIR,),
        in_specs=[pl.BlockSpec(memory_space=pl.ANY)] * len(units)
        + [
            pl.BlockSpec((heads, block, width), lambda g: (0, g, 0)),
            pl.BlockSpec((block, 128), lambda g: (g, 0)),
            pl.BlockSpec((block, width), lambda g: (g, 0)),
            whole(width, width),
        ],
        out_specs=[whole(share, width + 128)] * groups,
        scratch_shapes=scratch,
        out_shape=[jax.ShapeDtypeStruct((share, width + 128), BF)] * groups,
        compiler_params=pltpu.CompilerParams(vmem_limit_bytes=48 * 1024 * 1024),
        name="attend",
    )(*units, qw, states, numer, wv)

    received = [partials[0]] + [
        swap(partials[d], "head", d, groups) for d in range(1, groups)
    ]
    row = lambda *shape: pl.BlockSpec(shape, lambda i, m: (m[0], 0))
    mine, *grads = pl.pallas_call(
        finish_kernel,
        grid_spec=pltpu.PrefetchScalarGridSpec(
            num_scalar_prefetch=1,
            grid=(1,),
            in_specs=[whole(share, width + 128)] * groups
            + [
                row(share, width),
                whole(width, width),
                whole(1, width),
                whole(width, 128),
                row(share, 128),
            ],
            out_specs=[whole(share, 128)] + [whole(cols, 128)] * groups,
            scratch_shapes=[pltpu.VMEM((groups, cols, 128), F32)],
        ),
        out_shape=[jax.ShapeDtypeStruct((share, 128), F32)]
        + [jax.ShapeDtypeStruct((cols, 128), F32)] * groups,
        compiler_params=pltpu.CompilerParams(vmem_limit_bytes=32 * 1024 * 1024),
        name="finish",
    )(
        me[None].astype(jnp.int32),
        *received,
        latent,
        wo,
        norm_gain[None, :],
        w_inc,
        target,
    )
    grads = [grads[0]] + [swap(grads[d], "head", d, groups) for d in range(1, groups)]
    grad = (grads[0] + grads[1]) + (grads[2] + grads[3])
    for low, high in ((1, 2), (4, 8), (16, 32)):
        a, b, c = (swap(grad, "tile", m, tiles) for m in (low, high, low + high))
        grad = (grad + a) + (b + c)
    preds = jnp.stack([mine] + [swap(mine, "head", d, groups) for d in range(1, groups)])
    predicted = jnp.take(preds, turn, axis=0).reshape(lat_rows, 128)
    return predicted, grad * (1.0 / math.sqrt(lat_rows * tiles))


def solution(mesh):
    in_specs = (
        P("tile", "head"),
        P("tile"),
        P("tile", None),
        P("tile", None),
        P("tile", None),
        P(None, "head"),
        P(None, "head"),
        P(None, "head"),
        P("head"),
        P("head", None),
        P(),
        P(),
        P("tile", None),
    )
    out_specs = (P("tile", None), P("head", None))
    return jax.shard_map(body, mesh=mesh, in_specs=in_specs, out_specs=out_specs, check_vma=False)
```

```python
import functools
import math

import jax
import jax.numpy as jnp
from jax import lax
from jax.experimental import pallas as pl
from jax.experimental.pallas import tpu as pltpu
from jax.sharding import PartitionSpec as P

BF = jnp.bfloat16
F32 = jnp.float32
NEG = -1e30
SLOTS = 2
CHUNK = 8
PAIR = 8
NEAR = (1, 16, 17, 48, 49, 2, 3, 32)
DEPTHS = (6, 6, 6, 6, 6, 6, 6, 2)


def route_kernel(spill, owner, alive, obs, row_marks, pattern, sent, info, lanes, extra, near):
    tiles = sent.shape[0]
    blocks, parts, quarter = obs.shape[:3]
    subs = pattern.shape[0]
    me = lax.axis_index("tile")
    lane = lax.broadcasted_iota(jnp.int32, (blocks, 128), 1)
    rows = row_marks[...].astype(F32)
    spot = lax.broadcasted_iota(jnp.int32, (subs, 128), 1)
    line = lax.broadcasted_iota(jnp.int32, (subs, 128), 0)
    shift = (spot == line + quarter).astype(F32).astype(BF)
    groups = lax.dot_general(
        pattern[...].astype(F32).astype(BF),
        shift,
        (((0,), (0,)), ((), ())),
        preferred_element_type=F32,
    )
    for j in range(parts):
        turned = rows if j == 0 else pltpu.roll(rows, 128 - j * quarter, 1)
        info[j, :blocks] = jnp.where(lane < quarter, turned, groups)
        info[j, blocks:] = jnp.zeros((8, 128), F32)
    for m, mask in enumerate(NEAR):
        near[m] = mask

    def clear(t, carry):
        lanes[t] = blocks
        lanes[tiles + t] = 0
        return carry

    lax.fori_loop(0, tiles, clear, 0, unroll=8)

    def place(b, n):
        t = owner[b]
        live = alive[b]
        seen = lanes[tiles + t]
        take = (live > 0) & ((seen == 0) if spill else (seen > 0))
        lanes[t] = jnp.where(take, b, lanes[t])
        lanes[tiles + t] = seen | live
        extra[n] = b
        return n + (live & seen)

    more = lax.fori_loop(0, blocks, place, jnp.int32(0), unroll=4)
    left = jnp.int32(0)
    if spill:

        def move(q, left):
            b = extra[q]
            t = owner[b]
            found = jnp.int32(tiles)
            last = len(NEAR) - 1
            for a in range(len(NEAR)):
                other = t ^ (NEAR[last] if a == last else near[(me + q + a) % last])
                free = (lanes[other] == blocks) & (found == tiles)
                found = jnp.where(free, other, found)

            @pl.when(found < tiles)
            def _():
                lanes[found] = b

            return left + (found == tiles).astype(jnp.int32)

        left = lax.fori_loop(0, more, move, left)

    lane1 = lax.broadcasted_iota(jnp.int32, (1, 128), 1)

    def goal(t):
        b = lanes[t]
        return jnp.where(b < blocks, owner[jnp.minimum(b, blocks - 1)] + 1, 0)

    def note(t, table):
        return jnp.where(lane1 == t, goal(t).astype(F32), table)

    table = jnp.where(lane1 == tiles, left.astype(F32), jnp.zeros((1, 128), F32))
    table = lax.fori_loop(0, tiles, note, table, unroll=8)
    line8 = lax.broadcasted_iota(jnp.int32, (8, 128), 0)

    def fill(t, carry):
        b = lanes[t]
        to = jnp.where(lane1 == quarter + subs, goal(t).astype(F32), 0.0)
        for j in range(parts):
            one = info[j, pl.ds(b, 1), :] + to
            tail = jnp.where(line8 == 0, one, jnp.where(line8 == 1, table, 0.0))
            sent[t, j, quarter:, :] = tail.astype(BF)

        @pl.when(b < blocks)
        def _():
            sent[t, :, :quarter, :] = obs[b]

        @pl.when(b >= blocks)
        def _():
            sent[t, :, :quarter, :] = jnp.zeros(obs.shape[1:], BF)

        return carry

    lax.fori_loop(0, tiles, fill, 0, unroll=2)


def prepare_kernel(*refs):
    biases, weights, (lat, qw, states, numer, wv, wo) = refs[:4], refs[4:8], refs[8:]
    me = lax.axis_index("head")
    heads, lat_rows, width = qw.shape
    each = heads // len(weights)
    size = width // heads
    scale = 1.0 / math.sqrt(size)
    latent = lat[...]
    lane = lax.broadcasted_iota(jnp.int32, (lat_rows, 128), 1)
    keep = jnp.where(me == 0, 1.0, 0.0)
    total = jnp.where((lane >= heads) & (lane < 2 * heads), keep, 0.0)
    for d, (bias, w) in enumerate(zip(biases, weights)):
        block = me ^ d
        far = pl.ds(pl.multiple_of(block * 128, 128), 128)
        q = jnp.dot(latent, w[:, :128], preferred_element_type=F32).astype(BF).astype(F32)
        k = jnp.dot(latent, w[:, 128:256], preferred_element_type=F32).astype(BF).astype(F32)
        v = jnp.dot(latent, w[:, 256:384], preferred_element_type=F32)
        numer[:, far] = v * keep
        wv[:, far] = w[:, 256:384]
        wo[:, far] = w[:, 384:]
        for e in range(each):
            mine = lane // size == e
            own = jnp.sum(jnp.where(mine, q * k, 0.0), axis=1, keepdims=True)
            own = own * scale + bias[e]
            total = jnp.where(lane == block * each + e, own, total)
            carried = lax.dot_general(
                jnp.where(mine, q, 0.0).astype(BF),
                w[:, 128:256],
                (((1,), (1,)), ((), ())),
                preferred_element_type=F32,
            )
            qw[block * each + e] = (carried * scale).astype(BF)
    states[...] = total


def before(n):
    return (
        lax.broadcasted_iota(jnp.int32, (n, n), 0) < lax.broadcasted_iota(jnp.int32, (n, n), 1)
    ).astype(F32).astype(BF)


def listing(live):
    rows, n = live.shape
    place = jnp.dot(live.astype(BF), before(n), preferred_element_type=F32)
    turn = lax.broadcasted_iota(jnp.int32, (rows, 128, n), 1).astype(F32)
    name = lax.broadcasted_iota(jnp.int32, (rows, 128, n), 2).astype(F32)
    hit = (place[:, None, :] == turn) & (live[:, None, :] > 0.5)
    order = jnp.sum(jnp.where(hit, name, 0.0), axis=2)
    return order, jnp.sum(live, axis=1, keepdims=True)


def plan_kernel(arrived, plan, *rest):
    *outs, lists, sem = rest
    tiles = arrived.shape[0]
    near = len(NEAR)
    me = lax.axis_index("tile")
    table = arrived[:, 0, 32:40, :].astype(F32)[:, 1, :]
    mine = (lax.broadcasted_iota(jnp.int32, (near, 128), 1) == me).astype(F32).astype(BF)
    goals = lax.dot_general(
        mine, table.astype(BF), (((1,), (1,)), ((), ())), preferred_element_type=F32
    )
    line = lax.broadcasted_iota(jnp.int32, (near, tiles), 0)
    want = jnp.zeros((near, tiles), jnp.int32)
    for m, mask in enumerate(NEAR):
        want = jnp.where(line == m, (me ^ mask) + 1, want)
    order, count = listing((goals == want.astype(F32)).astype(F32))
    place = lax.broadcasted_iota(jnp.int32, (near, 128), 1)
    plan[:near] = jnp.where(place.astype(F32) < count, order, tiles).astype(jnp.int32)
    lane = lax.broadcasted_iota(jnp.int32, (1, 128), 1)
    worst = jnp.zeros((1, 128), F32)
    for mask, depth in zip(NEAR, DEPTHS):
        here = (table == ((lane ^ mask) + 1).astype(F32)).astype(F32)
        total = jnp.sum(here, axis=0, keepdims=True)
        worst = jnp.maximum(worst, jnp.where(lane < tiles, total - depth, 0.0))
    left = jnp.sum(jnp.where(lane == tiles, table, 0.0), axis=0, keepdims=True)
    bad = jnp.max(jnp.where(worst > 0.0, 1.0, left), axis=1, keepdims=True)
    good = jnp.where(bad > 0.0, 0, 1)
    plan[near:] = jnp.broadcast_to(good, (near, 128))
    copy = pltpu.make_async_copy(plan, lists, sem)
    copy.start()
    copy.wait()
    for m, out in enumerate(outs):
        for c in range(DEPTHS[m]):
            s = lists[m, c]

            @pl.when(s < tiles)
            def _(s=s, out=out, c=c):
                out[c] = arrived[s]

            @pl.when(s >= tiles)
            def _(out=out, c=c):
                out[c] = jnp.zeros(out.shape[1:], BF)


def lists_of(marks, quarter, subs):
    me = lax.axis_index("tile")
    to = marks[:, quarter + subs:quarter + subs + 1]
    marks = jnp.where(to == (me + 1).astype(F32), marks, 0.0).astype(BF)
    pick_group = (
        lax.broadcasted_iota(jnp.int32, (subs, 128), 1)
        == lax.broadcasted_iota(jnp.int32, (subs, 128), 0) + quarter
    ).astype(F32).astype(BF)
    up = lax.broadcasted_iota(jnp.int32, (128, 128), 0)
    along = lax.broadcasted_iota(jnp.int32, (128, 128), 1)
    widen = ((up < quarter) & (up == along % quarter)).astype(F32).astype(BF)
    live = lax.dot_general(
        pick_group, marks, (((1,), (1,)), ((), ())), preferred_element_type=F32
    )
    order, count = listing(live)
    rows = jnp.dot(marks, widen, preferred_element_type=F32)
    return order, count, (rows - 1.0) * (-NEG)


def split3(v):
    hi = v.astype(BF).astype(F32)
    mid = (v - hi).astype(BF).astype(F32)
    return hi, mid, v - hi - mid


def attend_kernel(*refs):
    units = refs[:len(NEAR) + 2]
    qw, begun, given, wv, *refs = refs[len(NEAR) + 2:]
    outs, (x, sems, made, lists, bias, result, *scratch) = refs[:4], refs[4:]
    me = lax.axis_index("head")
    step_id = pl.program_id(0)
    quarter = 32

    @pl.when(step_id == 0)
    def _():
        copies = []
        at = 0
        for u, unit in enumerate(units):
            n = unit.shape[0]
            copies.append(pltpu.make_async_copy(unit, x.at[pl.ds(at, n)], sems.at[u]))
            at += n
        for copy in copies:
            copy.start()
        for copy in copies:
            copy.wait()
        marks = x[:, 0, quarter:quarter + 8, :].astype(F32)[:, 0, :]
        order, count, shade = lists_of(marks, quarter, made.shape[0])
        bias[...] = shade
        made[:, :128] = order.astype(jnp.int32)
        made[:, 128:] = jnp.broadcast_to(count, order.shape).astype(jnp.int32)
        copy = pltpu.make_async_copy(made, lists, sems.at[len(units)])
        copy.start()
        copy.wait()

    heads, both, width = qw.shape
    sub = both // PAIR
    rows = heads * sub
    parts, _, cols = x.shape[1:]
    size = CHUNK * quarter
    per = 128 // quarter
    lane_slot = lax.broadcasted_iota(jnp.int32, (1, 128), 1) // quarter
    lane = lax.broadcasted_iota(jnp.int32, (sub, 128), 1)
    xbufs, accs, tops, dens = (scratch[q * PAIR:(q + 1) * PAIR] for q in range(4))

    def gather(g, n, c, xbuf):
        shades = []
        for part in range(CHUNK // per):
            shade = jnp.full((1, 128), NEG, F32)
            for v in range(per):
                u = part * per + v
                place = c * CHUNK + u
                s = lists[g, jnp.maximum(jnp.minimum(place, n - 1), 0)]
                for i in range(parts):
                    xbuf[u * quarter:(u + 1) * quarter, i * cols:(i + 1) * cols] = x[
                        s, i, :quarter, :
                    ]
                live = (lane_slot == v) & (place < n)
                shade = jnp.where(live, bias[pl.ds(s, 1), :], shade)
            shades.append(shade)
        return xbuf[...], jnp.concatenate(shades, axis=1)

    def chunk(queries, rows_x, shade, old):
        scores = lax.dot_general(
            queries, rows_x, (((1,), (1,)), ((), ())), preferred_element_type=F32
        ) + shade
        new = jnp.maximum(old, jnp.max(scores, axis=1, keepdims=True))
        weights = jnp.exp(scores - jnp.concatenate([new] * (size // 128), axis=1))
        total = jnp.sum(weights, axis=1, keepdims=True)
        more = jnp.dot(weights.astype(BF), rows_x, preferred_element_type=F32)
        return new, jnp.exp(old - new), total, more

    counts, begins = [], []
    for p in range(PAIR):
        g = step_id * PAIR + p
        n = lists[g, 128]
        counts.append(n)
        start = begun[p * sub:(p + 1) * sub, :]
        old = jnp.concatenate(
            [jnp.broadcast_to(start[:, h:h + 1], (sub, 128)) for h in range(heads)], axis=0
        )
        den = jnp.concatenate(
            [
                jnp.broadcast_to(start[:, heads + h:heads + h + 1], (sub, 128))
                for h in range(heads)
            ],
            axis=0,
        )
        begins.append(old)
        rows_x, shade = gather(g, n, 0, xbufs[p])
        queries = qw[:, p * sub:(p + 1) * sub, :].reshape(rows, width)
        new, shrink, total, more = chunk(queries, rows_x, shade, old)
        accs[p][...] = more
        tops[p][...] = new
        dens[p][...] = den * shrink + total

    for p in range(PAIR):
        g = step_id * PAIR + p

        @pl.when(counts[p] > CHUNK)
        def _(p=p, g=g):
            def again(c, carry):
                rows_x, shade = gather(g, counts[p], c, xbufs[p])
                queries = qw[:, p * sub:(p + 1) * sub, :].reshape(rows, width)
                new, shrink, total, more = chunk(queries, rows_x, shade, tops[p][...])
                tops[p][...] = new
                dens[p][...] = dens[p][...] * shrink + total
                wide = jnp.concatenate([shrink] * (width // 128), axis=1)
                accs[p][...] = accs[p][...] * wide + more
                return carry

            lax.fori_loop(1, (counts[p] + CHUNK - 1) // CHUNK, again, 0)

    half = width // 2
    for p in range(PAIR):
        place = slice(p * sub, (p + 1) * sub)
        share = outs[0].shape[0]
        quarter_id = (step_id * (PAIR * sub // share) + p * sub // share) ^ me
        line0 = (p * sub) % share
        spot = slice(line0, line0 + sub)
        top = tops[p][...]
        shrink = jnp.exp(begins[p] - top)
        state = jnp.zeros((sub, 128), F32)
        for h in range(heads):
            line = slice(h * sub, (h + 1) * sub)
            state = jnp.where(lane == h, top[line], state)
            state = jnp.where(lane == heads + h, dens[p][line, :], state)
        hi, mid, lo = split3(state)
        packed = hi + pltpu.roll(mid, 2 * heads, 1) + pltpu.roll(lo, 4 * heads, 1)
        result[quarter_id, spot, width:] = packed.astype(BF)
        for side in range(2):
            here = slice(side * rows // 2, (side + 1) * rows // 2)
            mixed = jnp.dot(
                accs[p][here, :].astype(BF),
                wv[:, side * half:(side + 1) * half],
                preferred_element_type=F32,
            )
            for c in range(half // 128):
                col = side * half + c * 128
                two = []
                for h in (2 * c, 2 * c + 1):
                    line = slice(h * sub, (h + 1) * sub)
                    far = side * rows // 2
                    two.append(
                        given[place, col:col + 128] * shrink[far + h * sub:far + (h + 1) * sub]
                        + mixed[line, c * 128:(c + 1) * 128]
                    )
                result[quarter_id, spot, col:col + 128] = jnp.where(
                    lane < width // heads, two[0], two[1]
                ).astype(BF)

    @pl.when(step_id == pl.num_programs(0) - 1)
    def _():
        for d, out in enumerate(outs):
            out[...] = result[d]


def finish_kernel(place, r0, r1, r2, r3, lat, w_out, gain, w_inc, target, *grads):
    width = lat.shape[1]
    heads = 8
    line = lax.broadcasted_iota(jnp.int32, (128, 2 * width), 0)
    col = lax.broadcasted_iota(jnp.int32, (128, 2 * width), 1)
    match = (
        (line % heads == (col % width) // (width // heads))
        & ((line // heads) % 2 == col // width)
        & (line < 6 * heads)
    )
    spread = match.astype(F32).astype(BF)
    tops, dens, nums = [], [], []
    for r in (r0, r1, r2, r3):
        wide = jnp.dot(r[:, width:], spread, preferred_element_type=F32)
        tops.append(wide[:, :width])
        dens.append(wide[:, width:])
        nums.append(r[:, :width].astype(F32))
    best = jnp.maximum(jnp.maximum(tops[0], tops[1]), jnp.maximum(tops[2], tops[3]))
    scale = [jnp.exp(v - best) for v in tops]
    numer = sum(a * b for a, b in zip(scale, nums))
    denom = sum(a * b for a, b in zip(scale, dens))
    attended = (numer / denom).astype(BF)
    updated = lat[...].astype(F32) + lax.dot_general(
        attended, w_out[...], (((1,), (1,)), ((), ())), preferred_element_type=F32
    )
    power = jnp.mean(updated * updated, axis=1, keepdims=True)
    normed = (updated * lax.rsqrt(power + 1e-6) * gain[...]).astype(BF)
    answer = jnp.dot(normed, w_inc[...], preferred_element_type=F32)
    residual = answer - target[...].astype(F32)
    high = residual.astype(BF)
    low = (residual - high.astype(F32)).astype(BF)
    dims = (((0,), (0,)), ((), ()))
    total = lax.dot_general(normed, high, dims, preferred_element_type=F32)
    total = total + lax.dot_general(normed, low, dims, preferred_element_type=F32)
    *grads, cut = grads
    size = cut.shape[1]
    for c in range(width // size):
        cut[c] = total[c * size:(c + 1) * size]
    for d, grad in enumerate(grads):
        grad[:size, :] = cut[place[0] ^ d]
        grad[size:, :] = answer


def body(
    obs_feat,
    row_valid,
    block_owner,
    block_pattern,
    latent,
    w_query,
    w_key,
    w_value,
    self_bias,
    w_out,
    norm_gain,
    w_inc,
    target,
):
    tiles = lax.axis_size("tile")
    groups = lax.axis_size("head")
    me = lax.axis_index("head")
    blocks = block_owner.shape[0]
    block_rows = obs_feat.shape[0] // blocks
    quarter = block_rows // groups
    cols = obs_feat.shape[1]
    lat_rows, width = latent.shape
    subs = block_pattern.shape[1]
    sub = lat_rows // subs
    local_heads = self_bias.shape[0]
    heads = local_heads * groups
    head_size = width // heads
    share = lat_rows // groups

    def swap(v, axis, mask, size):
        return lax.ppermute(v, axis, [(d, d ^ mask) for d in range(size)])

    whole = lambda *shape: pl.BlockSpec(shape, lambda g, *_: (0,) * len(shape))
    depth = quarter + 8
    alive = jnp.max(block_pattern.T, axis=0)

    def route(spill):
        sent = pl.pallas_call(
            functools.partial(route_kernel, spill),
            grid_spec=pltpu.PrefetchScalarGridSpec(
                num_scalar_prefetch=2,
                grid=(1,),
                in_specs=[
                    whole(blocks, groups, quarter, cols),
                    whole(blocks, block_rows),
                    whole(subs, blocks),
                ],
                out_specs=whole(tiles, groups, depth, cols),
                scratch_shapes=[
                    pltpu.VMEM((groups, blocks + 8, 128), F32),
                    pltpu.SMEM((2 * tiles,), jnp.int32),
                    pltpu.SMEM((blocks + 8,), jnp.int32),
                    pltpu.SMEM((len(NEAR),), jnp.int32),
                ],
            ),
            out_shape=jax.ShapeDtypeStruct((tiles, groups, depth, cols), BF),
            compiler_params=pltpu.CompilerParams(vmem_limit_bytes=32 * 1024 * 1024),
            name="route",
        )(
            block_owner[:, 0],
            alive,
            obs_feat.reshape(blocks, groups, quarter, cols),
            row_valid.reshape(blocks, block_rows),
            block_pattern.T,
        )
        return lax.all_to_all(
            sent.reshape(tiles * groups, depth, cols),
            ("tile", "head"),
            split_axis=0,
            concat_axis=0,
            tiled=True,
        ).reshape(tiles, groups, depth, cols)

    arrived = route(True)
    near = len(NEAR)
    stacked = jnp.concatenate([w_query, w_key, w_value, w_out.T], axis=1)
    nearby = [stacked] + [swap(stacked, "head", d, groups) for d in range(1, groups)]
    turn = jnp.arange(groups, dtype=jnp.int32) ^ me
    biases = [self_bias] + [swap(self_bias, "head", d, groups) for d in range(1, groups)]

    qw, states, numer, wv, wo = pl.pallas_call(
        prepare_kernel,
        grid=(1,),
        in_specs=[pl.BlockSpec(memory_space=pltpu.SMEM)] * groups
        + [whole(width, width)] * groups
        + [whole(lat_rows, width)],
        out_specs=[
            whole(heads, lat_rows, width),
            whole(lat_rows, 128),
            whole(lat_rows, width),
            whole(width, width),
            whole(width, width),
        ],
        out_shape=[
            jax.ShapeDtypeStruct((heads, lat_rows, width), BF),
            jax.ShapeDtypeStruct((lat_rows, 128), F32),
            jax.ShapeDtypeStruct((lat_rows, width), F32),
            jax.ShapeDtypeStruct((width, width), BF),
            jax.ShapeDtypeStruct((width, width), BF),
        ],
        compiler_params=pltpu.CompilerParams(vmem_limit_bytes=32 * 1024 * 1024),
        name="prepare",
    )(*biases, *nearby, latent)

    plan, *held = pl.pallas_call(
        plan_kernel,
        grid=(1,),
        in_specs=[whole(tiles, groups, depth, cols)],
        out_specs=[whole(2 * near, 128)]
        + [whole(n, groups, depth, cols) for n in DEPTHS],
        out_shape=[jax.ShapeDtypeStruct((2 * near, 128), jnp.int32)]
        + [jax.ShapeDtypeStruct((n, groups, depth, cols), BF) for n in DEPTHS],
        scratch_shapes=[
            pltpu.SMEM((2 * near, 128), jnp.int32),
            pltpu.SemaphoreType.DMA,
        ],
        compiler_params=pltpu.CompilerParams(vmem_limit_bytes=32 * 1024 * 1024),
        name="plan",
    )(arrived)
    rest = tiles - sum(DEPTHS)
    starts = [sum(DEPTHS[:m]) for m in range(near)]

    def forward():
        moved = [swap(v, "tile", m, tiles) for m, v in zip(NEAR[:-1], held[:-1])]
        final, moved[0] = lax.optimization_barrier((held[-1], moved[0]))
        moved.append(swap(final, "tile", NEAR[-1], tiles))
        return *moved, jnp.zeros((rest, groups, depth, cols), BF)

    def again():
        second = route(False)
        parts = [second[a:a + n] for a, n in zip(starts, DEPTHS)]
        return *parts, second[-rest:]

    units = (arrived, *lax.cond(plan[near, 0] > 0, forward, again))
    block = PAIR * sub
    scratch = [
        pltpu.VMEM((SLOTS * tiles, groups, depth, cols), BF),
        pltpu.SemaphoreType.DMA((len(units) + 1,)),
        pltpu.VMEM((subs, 256), jnp.int32),
        pltpu.SMEM((subs, 256), jnp.int32),
        pltpu.VMEM((SLOTS * tiles, 128), F32),
        pltpu.VMEM((groups, share, width + 128), BF),
    ] + [
        shape
        for shape in (
            pltpu.VMEM((CHUNK * quarter, width), BF),
            pltpu.VMEM((heads * sub, width), F32),
            pltpu.VMEM((heads * sub, 128), F32),
            pltpu.VMEM((heads * sub, 128), F32),
        )
        for _ in range(PAIR)
    ]
    partials = pl.pallas_call(
        attend_kernel,
        grid=(subs // PAIR,),
        in_specs=[pl.BlockSpec(memory_space=pl.ANY)] * len(units)
        + [
            pl.BlockSpec((heads, block, width), lambda g: (0, g, 0)),
            pl.BlockSpec((block, 128), lambda g: (g, 0)),
            pl.BlockSpec((block, width), lambda g: (g, 0)),
            whole(width, width),
        ],
        out_specs=[whole(share, width + 128)] * groups,
        scratch_shapes=scratch,
        out_shape=[jax.ShapeDtypeStruct((share, width + 128), BF)] * groups,
        compiler_params=pltpu.CompilerParams(vmem_limit_bytes=48 * 1024 * 1024),
        name="attend",
    )(*units, qw, states, numer, wv)

    received = [partials[0]] + [
        swap(partials[d], "head", d, groups) for d in range(1, groups)
    ]
    row = lambda *shape: pl.BlockSpec(shape, lambda i, m: (m[0], 0))
    terms = pl.pallas_call(
        finish_kernel,
        grid_spec=pltpu.PrefetchScalarGridSpec(
            num_scalar_prefetch=1,
            grid=(1,),
            in_specs=[whole(share, width + 128)] * groups
            + [
                row(share, width),
                whole(width, width),
                whole(1, width),
                whole(width, 128),
                row(share, 128),
            ],
            out_specs=[whole(cols + share, 128)] * groups,
            scratch_shapes=[pltpu.VMEM((groups, cols, 128), F32)],
        ),
        out_shape=[jax.ShapeDtypeStruct((cols + share, 128), F32)] * groups,
        compiler_params=pltpu.CompilerParams(vmem_limit_bytes=32 * 1024 * 1024),
        name="finish",
    )(
        me[None].astype(jnp.int32),
        *received,
        latent,
        wo,
        norm_gain[None, :],
        w_inc,
        target,
    )
    terms = [terms[0]] + [swap(terms[d], "head", d, groups) for d in range(1, groups)]
    grads = [term[:cols] for term in terms]
    grad = (grads[0] + grads[1]) + (grads[2] + grads[3])
    for low, high in ((1, 2), (4, 8), (16, 32)):
        a, b, c = (swap(grad, "tile", m, tiles) for m in (low, high, low + high))
        grad = (grad + a) + (b + c)
    predicted = jnp.take(jnp.stack([term[cols:] for term in terms]), turn, axis=0).reshape(lat_rows, 128)
    return predicted, grad * (1.0 / math.sqrt(lat_rows * tiles))


def solution(mesh):
    in_specs = (
        P("tile", "head"),
        P("tile"),
        P("tile", None),
        P("tile", None),
        P("tile", None),
        P(None, "head"),
        P(None, "head"),
        P(None, "head"),
        P("head"),
        P("head", None),
        P(),
        P(),
        P("tile", None),
    )
    out_specs = (P("tile", None), P("head", None))
    return jax.shard_map(body, mesh=mesh, in_specs=in_specs, out_specs=out_specs, check_vma=False)
```

```python
import functools
import math

import jax
import jax.numpy as jnp
from jax import lax
from jax.experimental import pallas as pl
from jax.experimental.pallas import tpu as pltpu
from jax.sharding import PartitionSpec as P

BF = jnp.bfloat16
F32 = jnp.float32
NEG = -1e30
SLOTS = 2
CHUNK = 8
PAIR = 8
NEAR = (1, 16, 17, 48, 49, 2, 3, 32)
DEPTHS = (6, 6, 6, 6, 6, 6, 6, 2)


def route_kernel(spill, owner, alive, obs, row_marks, pattern, sent, info, lanes, extra, near):
    tiles = sent.shape[0]
    blocks, parts, quarter = obs.shape[:3]
    subs = pattern.shape[0]
    me = lax.axis_index("tile")
    lane = lax.broadcasted_iota(jnp.int32, (blocks, 128), 1)
    rows = row_marks[...].astype(F32)
    spot = lax.broadcasted_iota(jnp.int32, (subs, 128), 1)
    line = lax.broadcasted_iota(jnp.int32, (subs, 128), 0)
    shift = (spot == line + quarter).astype(F32).astype(BF)
    groups = lax.dot_general(
        pattern[...].astype(F32).astype(BF),
        shift,
        (((0,), (0,)), ((), ())),
        preferred_element_type=F32,
    )
    for j in range(parts):
        turned = rows if j == 0 else pltpu.roll(rows, 128 - j * quarter, 1)
        info[j, :blocks] = jnp.where(lane < quarter, turned, groups)
        info[j, blocks:] = jnp.zeros((8, 128), F32)
    for m, mask in enumerate(NEAR):
        near[m] = mask

    def clear(t, carry):
        lanes[t] = blocks
        lanes[tiles + t] = 0
        return carry

    lax.fori_loop(0, tiles, clear, 0, unroll=8)

    def place(b, n):
        t = owner[b]
        live = alive[b]
        seen = lanes[tiles + t]
        take = (live > 0) & ((seen == 0) if spill else (seen > 0))
        lanes[t] = jnp.where(take, b, lanes[t])
        lanes[tiles + t] = seen | live
        extra[n] = b
        return n + (live & seen)

    more = lax.fori_loop(0, blocks, place, jnp.int32(0), unroll=4)
    left = jnp.int32(0)
    if spill:

        def move(q, left):
            b = extra[q]
            t = owner[b]
            found = jnp.int32(tiles)
            last = len(NEAR) - 1
            for a in range(len(NEAR)):
                other = t ^ (NEAR[last] if a == last else near[(me + q + a) % last])
                free = (lanes[other] == blocks) & (found == tiles)
                found = jnp.where(free, other, found)

            @pl.when(found < tiles)
            def _():
                lanes[found] = b

            return left + (found == tiles).astype(jnp.int32)

        left = lax.fori_loop(0, more, move, left)

    lane1 = lax.broadcasted_iota(jnp.int32, (1, 128), 1)

    def goal(t):
        b = lanes[t]
        return jnp.where(b < blocks, owner[jnp.minimum(b, blocks - 1)] + 1, 0)

    def note(t, table):
        return jnp.where(lane1 == t, goal(t).astype(F32), table)

    table = jnp.where(lane1 == tiles, left.astype(F32), jnp.zeros((1, 128), F32))
    table = lax.fori_loop(0, tiles, note, table, unroll=8)
    line8 = lax.broadcasted_iota(jnp.int32, (8, 128), 0)

    def fill(t, carry):
        b = lanes[t]
        to = jnp.where(lane1 == quarter + subs, goal(t).astype(F32), 0.0)
        for j in range(parts):
            one = info[j, pl.ds(b, 1), :] + to
            tail = jnp.where(line8 == 0, one, jnp.where(line8 == 1, table, 0.0))
            sent[t, j, quarter:, :] = tail.astype(BF)

        @pl.when(b < blocks)
        def _():
            sent[t, :, :quarter, :] = obs[b]

        @pl.when(b >= blocks)
        def _():
            sent[t, :, :quarter, :] = jnp.zeros(obs.shape[1:], BF)

        return carry

    lax.fori_loop(0, tiles, fill, 0, unroll=2)


def prepare_kernel(*refs):
    biases, weights, (lat, qw, states, numer, wv, wo) = refs[:4], refs[4:8], refs[8:]
    me = lax.axis_index("head")
    heads, lat_rows, width = qw.shape
    each = heads // len(weights)
    size = width // heads
    scale = 1.0 / math.sqrt(size)
    latent = lat[...]
    lane = lax.broadcasted_iota(jnp.int32, (lat_rows, 128), 1)
    keep = jnp.where(me == 0, 1.0, 0.0)
    total = jnp.where((lane >= heads) & (lane < 2 * heads), keep, 0.0)
    for d, (bias, w) in enumerate(zip(biases, weights)):
        block = me ^ d
        far = pl.ds(pl.multiple_of(block * 128, 128), 128)
        q = jnp.dot(latent, w[:, :128], preferred_element_type=F32).astype(BF).astype(F32)
        k = jnp.dot(latent, w[:, 128:256], preferred_element_type=F32).astype(BF).astype(F32)
        v = jnp.dot(latent, w[:, 256:384], preferred_element_type=F32)
        numer[:, far] = v * keep
        wv[:, far] = w[:, 256:384]
        wo[:, far] = w[:, 384:]
        for e in range(each):
            mine = lane // size == e
            own = jnp.sum(jnp.where(mine, q * k, 0.0), axis=1, keepdims=True)
            own = own * scale + bias[e]
            total = jnp.where(lane == block * each + e, own, total)
            carried = lax.dot_general(
                jnp.where(mine, q, 0.0).astype(BF),
                w[:, 128:256],
                (((1,), (1,)), ((), ())),
                preferred_element_type=F32,
            )
            qw[block * each + e] = (carried * scale).astype(BF)
    states[...] = total


def before(n):
    return (
        lax.broadcasted_iota(jnp.int32, (n, n), 0) < lax.broadcasted_iota(jnp.int32, (n, n), 1)
    ).astype(F32).astype(BF)


def listing(live):
    rows, n = live.shape
    place = jnp.dot(live.astype(BF), before(n), preferred_element_type=F32)
    turn = lax.broadcasted_iota(jnp.int32, (rows, 128, n), 1).astype(F32)
    name = lax.broadcasted_iota(jnp.int32, (rows, 128, n), 2).astype(F32)
    hit = (place[:, None, :] == turn) & (live[:, None, :] > 0.5)
    order = jnp.sum(jnp.where(hit, name, 0.0), axis=2)
    return order, jnp.sum(live, axis=1, keepdims=True)


def plan_kernel(arrived, plan, *rest):
    *outs, lists, sem = rest
    tiles = arrived.shape[0]
    near = len(NEAR)
    me = lax.axis_index("tile")
    table = arrived[:, 0, 32:40, :].astype(F32)[:, 1, :]
    mine = (lax.broadcasted_iota(jnp.int32, (near, 128), 1) == me).astype(F32).astype(BF)
    goals = lax.dot_general(
        mine, table.astype(BF), (((1,), (1,)), ((), ())), preferred_element_type=F32
    )
    line = lax.broadcasted_iota(jnp.int32, (near, tiles), 0)
    want = jnp.zeros((near, tiles), jnp.int32)
    for m, mask in enumerate(NEAR):
        want = jnp.where(line == m, (me ^ mask) + 1, want)
    order, count = listing((goals == want.astype(F32)).astype(F32))
    place = lax.broadcasted_iota(jnp.int32, (near, 128), 1)
    plan[:near] = jnp.where(place.astype(F32) < count, order, tiles).astype(jnp.int32)
    lane = lax.broadcasted_iota(jnp.int32, (1, 128), 1)
    worst = jnp.zeros((1, 128), F32)
    for mask, depth in zip(NEAR, DEPTHS):
        here = (table == ((lane ^ mask) + 1).astype(F32)).astype(F32)
        total = jnp.sum(here, axis=0, keepdims=True)
        worst = jnp.maximum(worst, jnp.where(lane < tiles, total - depth, 0.0))
    left = jnp.sum(jnp.where(lane == tiles, table, 0.0), axis=0, keepdims=True)
    bad = jnp.max(jnp.where(worst > 0.0, 1.0, left), axis=1, keepdims=True)
    good = jnp.where(bad > 0.0, 0, 1)
    plan[near:] = jnp.broadcast_to(good, (near, 128))
    copy = pltpu.make_async_copy(plan, lists, sem)
    copy.start()
    copy.wait()
    for m, out in enumerate(outs):
        for c in range(DEPTHS[m]):
            s = lists[m, c]

            @pl.when(s < tiles)
            def _(s=s, out=out, c=c):
                out[c] = arrived[s]

            @pl.when(s >= tiles)
            def _(out=out, c=c):
                out[c] = jnp.zeros(out.shape[1:], BF)


def lists_of(marks, quarter, subs):
    me = lax.axis_index("tile")
    to = marks[:, quarter + subs:quarter + subs + 1]
    marks = jnp.where(to == (me + 1).astype(F32), marks, 0.0).astype(BF)
    pick_group = (
        lax.broadcasted_iota(jnp.int32, (subs, 128), 1)
        == lax.broadcasted_iota(jnp.int32, (subs, 128), 0) + quarter
    ).astype(F32).astype(BF)
    up = lax.broadcasted_iota(jnp.int32, (128, 128), 0)
    along = lax.broadcasted_iota(jnp.int32, (128, 128), 1)
    widen = ((up < quarter) & (up == along % quarter)).astype(F32).astype(BF)
    live = lax.dot_general(
        pick_group, marks, (((1,), (1,)), ((), ())), preferred_element_type=F32
    )
    order, count = listing(live)
    rows = jnp.dot(marks, widen, preferred_element_type=F32)
    return order, count, (rows - 1.0) * (-NEG)


def split3(v):
    hi = v.astype(BF).astype(F32)
    mid = (v - hi).astype(BF).astype(F32)
    return hi, mid, v - hi - mid


def attend_kernel(*refs):
    units = refs[:len(NEAR) + 2]
    qw, begun, given, wv, *refs = refs[len(NEAR) + 2:]
    outs, (x, sems, made, lists, bias, result, *scratch) = refs[:4], refs[4:]
    me = lax.axis_index("head")
    step_id = pl.program_id(0)
    quarter = 32

    @pl.when(step_id == 0)
    def _():
        copies = []
        at = 0
        for u, unit in enumerate(units):
            n = unit.shape[0]
            copies.append(pltpu.make_async_copy(unit, x.at[pl.ds(at, n)], sems.at[u]))
            at += n
        for copy in copies:
            copy.start()
        for copy in copies:
            copy.wait()
        marks = x[:, 0, quarter:quarter + 8, :].astype(F32)[:, 0, :]
        order, count, shade = lists_of(marks, quarter, made.shape[0])
        bias[...] = shade
        made[:, :128] = order.astype(jnp.int32)
        made[:, 128:] = jnp.broadcast_to(count, order.shape).astype(jnp.int32)
        copy = pltpu.make_async_copy(made, lists, sems.at[len(units)])
        copy.start()
        copy.wait()

    heads, both, width = qw.shape
    sub = both // PAIR
    rows = heads * sub
    parts, _, cols = x.shape[1:]
    size = CHUNK * quarter
    per = 128 // quarter
    lane_slot = lax.broadcasted_iota(jnp.int32, (1, 128), 1) // quarter
    lane = lax.broadcasted_iota(jnp.int32, (sub, 128), 1)
    xbufs, accs, tops, dens = (scratch[q * PAIR:(q + 1) * PAIR] for q in range(4))

    def gather(g, n, c, xbuf):
        shades = []
        for part in range(CHUNK // per):
            shade = jnp.full((1, 128), NEG, F32)
            for v in range(per):
                u = part * per + v
                place = c * CHUNK + u
                s = lists[g, jnp.maximum(jnp.minimum(place, n - 1), 0)]
                for i in range(parts):
                    xbuf[u * quarter:(u + 1) * quarter, i * cols:(i + 1) * cols] = x[
                        s, i, :quarter, :
                    ]
                live = (lane_slot == v) & (place < n)
                shade = jnp.where(live, bias[pl.ds(s, 1), :], shade)
            shades.append(shade)
        return xbuf[...], jnp.concatenate(shades, axis=1)

    def chunk(queries, rows_x, shade, old):
        scores = lax.dot_general(
            queries, rows_x, (((1,), (1,)), ((), ())), preferred_element_type=F32
        ) + shade
        new = jnp.maximum(old, jnp.max(scores, axis=1, keepdims=True))
        weights = jnp.exp(scores - jnp.concatenate([new] * (size // 128), axis=1))
        total = jnp.sum(weights, axis=1, keepdims=True)
        more = jnp.dot(weights.astype(BF), rows_x, preferred_element_type=F32)
        return new, jnp.exp(old - new), total, more

    counts, begins = [], []
    for p in range(PAIR):
        g = step_id * PAIR + p
        n = lists[g, 128]
        counts.append(n)
        start = begun[p * sub:(p + 1) * sub, :]
        old = jnp.concatenate(
            [jnp.broadcast_to(start[:, h:h + 1], (sub, 128)) for h in range(heads)], axis=0
        )
        den = jnp.concatenate(
            [
                jnp.broadcast_to(start[:, heads + h:heads + h + 1], (sub, 128))
                for h in range(heads)
            ],
            axis=0,
        )
        begins.append(old)
        rows_x, shade = gather(g, n, 0, xbufs[p])
        queries = qw[:, p * sub:(p + 1) * sub, :].reshape(rows, width)
        new, shrink, total, more = chunk(queries, rows_x, shade, old)
        accs[p][...] = more
        tops[p][...] = new
        dens[p][...] = den * shrink + total

    for p in range(PAIR):
        g = step_id * PAIR + p

        @pl.when(counts[p] > CHUNK)
        def _(p=p, g=g):
            def again(c, carry):
                rows_x, shade = gather(g, counts[p], c, xbufs[p])
                queries = qw[:, p * sub:(p + 1) * sub, :].reshape(rows, width)
                new, shrink, total, more = chunk(queries, rows_x, shade, tops[p][...])
                tops[p][...] = new
                dens[p][...] = dens[p][...] * shrink + total
                wide = jnp.concatenate([shrink] * (width // 128), axis=1)
                accs[p][...] = accs[p][...] * wide + more
                return carry

            lax.fori_loop(1, (counts[p] + CHUNK - 1) // CHUNK, again, 0)

    half = width // 2
    for p in range(PAIR):
        place = slice(p * sub, (p + 1) * sub)
        share = outs[0].shape[0]
        quarter_id = (step_id * (PAIR * sub // share) + p * sub // share) ^ me
        line0 = (p * sub) % share
        spot = slice(line0, line0 + sub)
        top = tops[p][...]
        shrink = jnp.exp(begins[p] - top)
        state = jnp.zeros((sub, 128), F32)
        for h in range(heads):
            line = slice(h * sub, (h + 1) * sub)
            state = jnp.where(lane == h, top[line], state)
            state = jnp.where(lane == heads + h, dens[p][line, :], state)
        hi, mid, lo = split3(state)
        packed = hi + pltpu.roll(mid, 2 * heads, 1) + pltpu.roll(lo, 4 * heads, 1)
        result[quarter_id, spot, width:] = packed.astype(BF)
        for side in range(2):
            here = slice(side * rows // 2, (side + 1) * rows // 2)
            mixed = jnp.dot(
                accs[p][here, :].astype(BF),
                wv[:, side * half:(side + 1) * half],
                preferred_element_type=F32,
            )
            for c in range(half // 128):
                col = side * half + c * 128
                two = []
                for h in (2 * c, 2 * c + 1):
                    line = slice(h * sub, (h + 1) * sub)
                    far = side * rows // 2
                    two.append(
                        given[place, col:col + 128] * shrink[far + h * sub:far + (h + 1) * sub]
                        + mixed[line, c * 128:(c + 1) * 128]
                    )
                result[quarter_id, spot, col:col + 128] = jnp.where(
                    lane < width // heads, two[0], two[1]
                ).astype(BF)

    @pl.when(step_id == pl.num_programs(0) - 1)
    def _():
        for d, out in enumerate(outs):
            out[...] = result[d]


def finish_kernel(place, r0, r1, r2, r3, lat, w_out, gain, w_inc, target, *grads):
    width = lat.shape[1]
    heads = 8
    line = lax.broadcasted_iota(jnp.int32, (128, 2 * width), 0)
    col = lax.broadcasted_iota(jnp.int32, (128, 2 * width), 1)
    match = (
        (line % heads == (col % width) // (width // heads))
        & ((line // heads) % 2 == col // width)
        & (line < 6 * heads)
    )
    spread = match.astype(F32).astype(BF)
    tops, dens, nums = [], [], []
    for r in (r0, r1, r2, r3):
        wide = jnp.dot(r[:, width:], spread, preferred_element_type=F32)
        tops.append(wide[:, :width])
        dens.append(wide[:, width:])
        nums.append(r[:, :width].astype(F32))
    best = jnp.maximum(jnp.maximum(tops[0], tops[1]), jnp.maximum(tops[2], tops[3]))
    scale = [jnp.exp(v - best) for v in tops]
    numer = sum(a * b for a, b in zip(scale, nums))
    denom = sum(a * b for a, b in zip(scale, dens))
    attended = (numer / denom).astype(BF)
    updated = lat[...].astype(F32) + lax.dot_general(
        attended, w_out[...], (((1,), (1,)), ((), ())), preferred_element_type=F32
    )
    power = jnp.mean(updated * updated, axis=1, keepdims=True)
    normed = (updated * lax.rsqrt(power + 1e-6) * gain[...]).astype(BF)
    answer = jnp.dot(normed, w_inc[...], preferred_element_type=F32)
    residual = answer - target[...].astype(F32)
    high = residual.astype(BF)
    low = (residual - high.astype(F32)).astype(BF)
    dims = (((0,), (0,)), ((), ()))
    total = lax.dot_general(normed, high, dims, preferred_element_type=F32)
    total = total + lax.dot_general(normed, low, dims, preferred_element_type=F32)
    *grads, cut = grads
    size = cut.shape[1]
    for c in range(width // size):
        cut[c] = total[c * size:(c + 1) * size]
    for d, grad in enumerate(grads):
        grad[:size, :] = cut[place[0] ^ d]
        grad[size:, :] = answer


def body(
    obs_feat,
    row_valid,
    block_owner,
    block_pattern,
    latent,
    w_query,
    w_key,
    w_value,
    self_bias,
    w_out,
    norm_gain,
    w_inc,
    target,
):
    tiles = lax.axis_size("tile")
    groups = lax.axis_size("head")
    me = lax.axis_index("head")
    blocks = block_owner.shape[0]
    block_rows = obs_feat.shape[0] // blocks
    quarter = block_rows // groups
    cols = obs_feat.shape[1]
    lat_rows, width = latent.shape
    subs = block_pattern.shape[1]
    sub = lat_rows // subs
    local_heads = self_bias.shape[0]
    heads = local_heads * groups
    head_size = width // heads
    share = lat_rows // groups

    def swap(v, axis, mask, size):
        return lax.ppermute(v, axis, [(d, d ^ mask) for d in range(size)])

    whole = lambda *shape: pl.BlockSpec(shape, lambda g, *_: (0,) * len(shape))
    depth = quarter + 8
    alive = jnp.max(block_pattern.T, axis=0)

    def route(spill):
        sent = pl.pallas_call(
            functools.partial(route_kernel, spill),
            grid_spec=pltpu.PrefetchScalarGridSpec(
                num_scalar_prefetch=2,
                grid=(1,),
                in_specs=[
                    whole(blocks, groups, quarter, cols),
                    whole(blocks, block_rows),
                    whole(subs, blocks),
                ],
                out_specs=whole(tiles, groups, depth, cols),
                scratch_shapes=[
                    pltpu.VMEM((groups, blocks + 8, 128), F32),
                    pltpu.SMEM((2 * tiles,), jnp.int32),
                    pltpu.SMEM((blocks + 8,), jnp.int32),
                    pltpu.SMEM((len(NEAR),), jnp.int32),
                ],
            ),
            out_shape=jax.ShapeDtypeStruct((tiles, groups, depth, cols), BF),
            compiler_params=pltpu.CompilerParams(vmem_limit_bytes=20 * 1024 * 1024),
            name="route",
        )(
            block_owner[:, 0],
            alive,
            obs_feat.reshape(blocks, groups, quarter, cols),
            row_valid.reshape(blocks, block_rows),
            block_pattern.T,
        )
        return lax.all_to_all(
            sent.reshape(tiles * groups, depth, cols),
            ("tile", "head"),
            split_axis=0,
            concat_axis=0,
            tiled=True,
        ).reshape(tiles, groups, depth, cols)

    arrived = route(True)
    near = len(NEAR)
    stacked = jnp.concatenate([w_query, w_key, w_value, w_out.T], axis=1)
    nearby = [stacked] + [swap(stacked, "head", d, groups) for d in range(1, groups)]
    turn = jnp.arange(groups, dtype=jnp.int32) ^ me
    biases = [self_bias] + [swap(self_bias, "head", d, groups) for d in range(1, groups)]

    qw, states, numer, wv, wo = pl.pallas_call(
        prepare_kernel,
        grid=(1,),
        in_specs=[pl.BlockSpec(memory_space=pltpu.SMEM)] * groups
        + [whole(width, width)] * groups
        + [whole(lat_rows, width)],
        out_specs=[
            whole(heads, lat_rows, width),
            whole(lat_rows, 128),
            whole(lat_rows, width),
            whole(width, width),
            whole(width, width),
        ],
        out_shape=[
            jax.ShapeDtypeStruct((heads, lat_rows, width), BF),
            jax.ShapeDtypeStruct((lat_rows, 128), F32),
            jax.ShapeDtypeStruct((lat_rows, width), F32),
            jax.ShapeDtypeStruct((width, width), BF),
            jax.ShapeDtypeStruct((width, width), BF),
        ],
        compiler_params=pltpu.CompilerParams(vmem_limit_bytes=28 * 1024 * 1024),
        name="prepare",
    )(*biases, *nearby, latent)

    plan, *held = pl.pallas_call(
        plan_kernel,
        grid=(1,),
        in_specs=[whole(tiles, groups, depth, cols)],
        out_specs=[whole(2 * near, 128)]
        + [whole(n, groups, depth, cols) for n in DEPTHS],
        out_shape=[jax.ShapeDtypeStruct((2 * near, 128), jnp.int32)]
        + [jax.ShapeDtypeStruct((n, groups, depth, cols), BF) for n in DEPTHS],
        scratch_shapes=[
            pltpu.SMEM((2 * near, 128), jnp.int32),
            pltpu.SemaphoreType.DMA,
        ],
        compiler_params=pltpu.CompilerParams(vmem_limit_bytes=20 * 1024 * 1024),
        name="plan",
    )(arrived)
    rest = tiles - sum(DEPTHS)
    starts = [sum(DEPTHS[:m]) for m in range(near)]

    def forward():
        moved = [swap(v, "tile", m, tiles) for m, v in zip(NEAR[:-1], held[:-1])]
        final, moved[0] = lax.optimization_barrier((held[-1], moved[0]))
        moved.append(swap(final, "tile", NEAR[-1], tiles))
        return *moved, jnp.zeros((rest, groups, depth, cols), BF)

    def again():
        second = route(False)
        parts = [second[a:a + n] for a, n in zip(starts, DEPTHS)]
        return *parts, second[-rest:]

    units = (arrived, *lax.cond(plan[near, 0] > 0, forward, again))
    block = PAIR * sub
    scratch = [
        pltpu.VMEM((SLOTS * tiles, groups, depth, cols), BF),
        pltpu.SemaphoreType.DMA((len(units) + 1,)),
        pltpu.VMEM((subs, 256), jnp.int32),
        pltpu.SMEM((subs, 256), jnp.int32),
        pltpu.VMEM((SLOTS * tiles, 128), F32),
        pltpu.VMEM((groups, share, width + 128), BF),
    ] + [
        shape
        for shape in (
            pltpu.VMEM((CHUNK * quarter, width), BF),
            pltpu.VMEM((heads * sub, width), F32),
            pltpu.VMEM((heads * sub, 128), F32),
            pltpu.VMEM((heads * sub, 128), F32),
        )
        for _ in range(PAIR)
    ]
    partials = pl.pallas_call(
        attend_kernel,
        grid=(subs // PAIR,),
        in_specs=[pl.BlockSpec(memory_space=pl.ANY)] * len(units)
        + [
            pl.BlockSpec((heads, block, width), lambda g: (0, g, 0)),
            pl.BlockSpec((block, 128), lambda g: (g, 0)),
            pl.BlockSpec((block, width), lambda g: (g, 0)),
            whole(width, width),
        ],
        out_specs=[whole(share, width + 128)] * groups,
        scratch_shapes=scratch,
        out_shape=[jax.ShapeDtypeStruct((share, width + 128), BF)] * groups,
        compiler_params=pltpu.CompilerParams(vmem_limit_bytes=30 * 1024 * 1024),
        name="attend",
    )(*units, qw, states, numer, wv)

    received = [partials[0]] + [
        swap(partials[d], "head", d, groups) for d in range(1, groups)
    ]
    row = lambda *shape: pl.BlockSpec(shape, lambda i, m: (m[0], 0))
    terms = pl.pallas_call(
        finish_kernel,
        grid_spec=pltpu.PrefetchScalarGridSpec(
            num_scalar_prefetch=1,
            grid=(1,),
            in_specs=[whole(share, width + 128)] * groups
            + [
                row(share, width),
                whole(width, width),
                whole(1, width),
                whole(width, 128),
                row(share, 128),
            ],
            out_specs=[whole(cols + share, 128)] * groups,
            scratch_shapes=[pltpu.VMEM((groups, cols, 128), F32)],
        ),
        out_shape=[jax.ShapeDtypeStruct((cols + share, 128), F32)] * groups,
        compiler_params=pltpu.CompilerParams(vmem_limit_bytes=16 * 1024 * 1024),
        name="finish",
    )(
        me[None].astype(jnp.int32),
        *received,
        latent,
        wo,
        norm_gain[None, :],
        w_inc,
        target,
    )
    terms = [terms[0]] + [swap(terms[d], "head", d, groups) for d in range(1, groups)]
    grads = [term[:cols] for term in terms]
    grad = (grads[0] + grads[1]) + (grads[2] + grads[3])
    for low, high in ((1, 2), (4, 8), (16, 32)):
        a, b, c = (swap(grad, "tile", m, tiles) for m in (low, high, low + high))
        grad = (grad + a) + (b + c)
    predicted = jnp.take(jnp.stack([term[cols:] for term in terms]), turn, axis=0).reshape(lat_rows, 128)
    return predicted, grad * (1.0 / math.sqrt(lat_rows * tiles))


def solution(mesh):
    in_specs = (
        P("tile", "head"),
        P("tile"),
        P("tile", None),
        P("tile", None),
        P("tile", None),
        P(None, "head"),
        P(None, "head"),
        P(None, "head"),
        P("head"),
        P("head", None),
        P(),
        P(),
        P("tile", None),
    )
    out_specs = (P("tile", None), P("head", None))
    return jax.shard_map(body, mesh=mesh, in_specs=in_specs, out_specs=out_specs, check_vma=False)
```
